128 devices in a mesh: seq: 128 (over z, x, y, core).
Axes of the slice: x: 4, y: 4, z: 4, core: 2. Of those that a mesh axis runs over, the one named last changes fastest.
Arguments:
- point_feats: bfloat16 [131072, 256], P('seq'), may hold values from -6 to 6
- scene_id: int32 [131072], P('seq'), may hold values from 0 to 127, never falling along the last dimension, each value on 1 to 2048 neighbouring positions
- hilbert_rank: int32 [131072], P('seq'), may hold values from 0 to 131071, as said below
- norm_gains: float32 [2, 2, 256], replicated, may hold values from 0.1 to 1.9
- w_qkv: bfloat16 [2, 256, 768], replicated
- w_proj: bfloat16 [2, 256, 256], replicated, may hold values from -0.375 to 0.375
- w_up: bfloat16 [2, 256, 1024], replicated, may hold values from -0.375 to 0.375
- w_down: bfloat16 [2, 1024, 256], replicated, may hold values from -0.1875 to 0.1875
Outputs:
- block_out: bfloat16 [131072, 256], P('seq')
The draws below stay inside these ranges and needn't reach their ends.
Inputs may be any that keep to these rules, and one draw needn't show every extreme that they name: `hilbert_rank`: A permutation. Positions move in aligned tiles of 32 that keep their order: a tile either stays or goes to the same place on another device. One device sends at most 96 points to each of the two devices beside it (indices one up and one down, cyclically) and at most 32 points to any other device; both bounds are reached.
All inputs are finite; a program needn't handle non-finite values.
Results may differ from the reference program's by a relative error of at most 0.039.
The reference program's roundings to bfloat16 on the way count: a program that leaves them out, or rounds other values in their place, can miss the bound.
Values may be sent and summed in bfloat16 or wider, within the bound.
No kernel may reach another device: no remote copies, remote signals or barrier semaphores. Data moves between devices by JAX's collectives and lax.ppermute only.
A program may use at most 128 MiB of HBM per device.

```python
import math
import jax
import jax.numpy as jnp
import numpy as np
from jax import lax

C = 256
HEADS = 16
PATCH = 1024
FFN = 1024
ROWS_DEV = 1024
TILES = 32
MOST_TILES = 3
FAR_TILES = 26
TILE = 32
TOKENS = 131072
N_SEQ = 128


def draw_hilbert_rank(key, part):
    key = jax.random.fold_in(key, 7)
    key_first, key_second, key_far, key_pick = jax.random.split(key, 4)
    pair_count = N_SEQ // 2
    first_counts = jax.random.randint(key_first, (pair_count,), 1, MOST_TILES + 1)
    chosen = jax.random.randint(key_pick, (), 0, pair_count)
    first_counts = jnp.where(jnp.arange(pair_count) == chosen, MOST_TILES, first_counts)
    second_counts = jax.random.randint(key_second, (pair_count,), 1, MOST_TILES + 1)
    far_steps = 2 * jax.random.permutation(key_far, jnp.arange(1, pair_count, dtype=jnp.int32))[:FAR_TILES]
    device = jnp.arange(N_SEQ, dtype=jnp.int32)
    count_one = first_counts[device // 2]
    partner_one = device ^ 1
    second_index = jnp.where(device % 2 == 1, (device - 1) // 2, (device - 2) % N_SEQ // 2)
    count_two = second_counts[second_index]
    partner_two = jnp.where(device % 2 == 1, (device + 1) % N_SEQ, (device - 1) % N_SEQ)
    tile_index = jnp.arange(TILES, dtype=jnp.int32)[None, :]
    owner = jnp.where(tile_index < count_one[:, None], partner_one[:, None], device[:, None])
    in_second = (tile_index >= MOST_TILES) & (tile_index < MOST_TILES + count_two[:, None])
    owner = jnp.where(in_second, partner_two[:, None], owner)
    far_start = TILES - FAR_TILES
    step_table = jnp.concatenate([jnp.zeros((far_start,), jnp.int32), far_steps.astype(jnp.int32)])
    is_far = tile_index >= far_start
    owner = jnp.where(is_far, device[:, None] ^ step_table[None, :], owner)
    ranks = owner[:, :, None] * ROWS_DEV + tile_index[:, :, None] * TILE + jnp.arange(TILE, dtype=jnp.int32)[None, None, :]
    return ranks.reshape(-1).astype(jnp.int32)


def draw_w_qkv(key, part):
    key = jax.random.fold_in(key, 11)
    key_base = jax.random.fold_in(key, 0)
    weights = jax.random.normal(key_base, (2, C, 3 * C), jnp.float32) * C ** (-0.5)
    return weights.astype(jnp.bfloat16)


def shard_levels(stream_key, dims, cuts, low, largest):
    factor_of, own = 1.0, jax.random.fold_in(stream_key, 6)
    for position, shards_of in cuts:
        heights = jnp.exp(jax.random.uniform(jax.random.fold_in(own, position), (shards_of,), jnp.float32, low / len(cuts), largest / len(cuts)))
        factor_of = factor_of * jnp.repeat(heights, dims[position] // shards_of).reshape([-1 if axis == position else 1 for axis in range(len(dims))])
    return factor_of


def profile(number_of, total, limit, skew):
    loads = [(1 << 20) // math.isqrt(standing ** skew) + 1 for standing in range(2, number_of + 1)]
    rest, counts = total - limit - (number_of - 1), [1] * (number_of - 1)
    while rest > 0:
        free = [i for i in range(number_of - 1) if counts[i] < limit]
        pool, left = sum([loads[i] for i in free]), rest
        for i in free:
            extra = min(limit - counts[i], max(1, left * loads[i] // pool), rest)
            counts[i] = counts[i] + extra
            rest = rest - extra
    return np.array([limit] + counts)


def ragged(rng, number_of, total, limit, slope):
    if number_of == 2:
        one = jax.random.randint(rng, (), max(1, total - limit), min(limit, total - 1) + 1)
        return jnp.stack([one, total - one])
    lengths = jnp.asarray(profile(number_of, total, limit, slope), jnp.int32)
    twos = (number_of - 1) // 2
    giver, taker = lengths[1:1 + 2 * twos:2], lengths[2:2 + 2 * twos:2]
    margin = jnp.minimum(giver - 1, limit - taker)
    passed = jax.random.randint(jax.random.fold_in(rng, 1), (twos,), 0, 1 << 20) % (margin + 1)
    lengths = lengths.at[1:1 + 2 * twos:2].set(giver - passed).at[2:2 + 2 * twos:2].set(taker + passed)
    return lengths[jax.random.permutation(jax.random.fold_in(rng, 2), number_of)]


def scatter_about(own_key, shape, scale, reach, pieces=(), kind=jnp.bfloat16):
    loudness = shard_levels(own_key, shape, pieces, -0.22, 0.18) if pieces else 1.0
    values = jax.random.normal(own_key, shape, jnp.float32) * scale * loudness
    return jnp.minimum(jnp.maximum(values, -reach), reach).astype(kind)


def setup_inputs(seed: int = 0) -> dict:
    arg_keys = jax.random.split(jax.random.key(seed), 9)
    return {
        "point_feats": scatter_about(arg_keys[0], (TOKENS, C), 1.0, 6.0, ((0, 128),)),
        "scene_id": jnp.searchsorted(jnp.cumsum(ragged(arg_keys[1], TOKENS // PATCH, TOKENS, 2 * PATCH, 1)), jnp.arange(TOKENS), side="right").astype(jnp.int32),
        "hilbert_rank": draw_hilbert_rank(jax.random.fold_in(arg_keys[8], 71), 0),
        "norm_gains": jnp.clip(1.0 + 0.18 * jax.random.normal(arg_keys[3], (2, 2, C), jnp.float32), 0.1, 1.9),
        "w_qkv": draw_w_qkv(jax.random.fold_in(arg_keys[8], 71), 0),
        "w_proj": scatter_about(arg_keys[5], (2, C, C), C ** -0.5, 0.375),
        "w_up": scatter_about(arg_keys[6], (2, C, FFN), C ** -0.5, 0.375),
        "w_down": scatter_about(arg_keys[7], (2, FFN, C), FFN ** -0.5, 0.1875),
    }


EPSILON = 1e-05

def layer_norm(values):
    values = values.astype(jnp.float32)
    center = values - lax.optimization_barrier(jnp.mean(values, axis=-1, keepdims=True))
    spread = lax.optimization_barrier(jnp.mean(center * center, axis=-1, keepdims=True))
    return center * lax.rsqrt(spread + EPSILON)

def patch_attention(qkv_rows, scene_rows, heads):
    width = qkv_rows.shape[1] // 3
    head_size = width // heads
    group = min(4, heads)
    groups = heads // group
    patches = qkv_rows.shape[0] // PATCH
    stacked = qkv_rows.reshape(patches, PATCH, 3, groups, group, head_size)
    stacked = jnp.transpose(stacked, (0, 3, 2, 1, 4, 5))
    stacked = stacked.reshape(patches * groups, 3, PATCH, group, head_size)
    scenes = jnp.repeat(scene_rows.reshape(patches, 1, PATCH), groups, axis=1).reshape(patches * groups, PATCH)

    def one_group(operands):
        parts, labels = operands
        same_scene = labels[:, None] == labels[None, :]
        scores = jnp.einsum('qhd,khd->hqk', parts[0].astype(jnp.float32), parts[1].astype(jnp.float32)) * head_size ** (-0.5)
        scores = jnp.where(same_scene[None], scores, jnp.float32(-1e+30))
        highest = lax.optimization_barrier(jnp.max(scores, axis=-1, keepdims=True))
        expo = jnp.exp(scores - highest)
        weights = (expo / lax.optimization_barrier(jnp.sum(expo, axis=-1, keepdims=True))).astype(jnp.bfloat16)
        return jnp.einsum('hqk,khd->qhd', weights.astype(jnp.float32), parts[2].astype(jnp.float32))
    outputs = lax.map(one_group, (stacked, scenes))
    outputs = outputs.reshape(patches, groups, PATCH, group, head_size)
    return jnp.transpose(outputs, (0, 2, 1, 3, 4)).reshape(patches * PATCH, width)

def attention_block(inputs, labels, gain_pair, w_qkv, w_proj, w_up, w_down):
    normed = (layer_norm(inputs) * gain_pair[0]).astype(jnp.bfloat16)
    qkv_rows = jnp.dot(normed, w_qkv, preferred_element_type=jnp.float32).astype(jnp.bfloat16)
    attended = patch_attention(qkv_rows, labels, HEADS).astype(jnp.bfloat16)
    middle = (inputs.astype(jnp.float32) + jnp.dot(attended, w_proj, preferred_element_type=jnp.float32)).astype(jnp.bfloat16)
    normed_two = (layer_norm(middle) * gain_pair[1]).astype(jnp.bfloat16)
    hidden_act = jax.nn.gelu(jnp.dot(normed_two, w_up, preferred_element_type=jnp.float32), approximate=False).astype(jnp.bfloat16)
    return (middle.astype(jnp.float32) + jnp.dot(hidden_act, w_down, preferred_element_type=jnp.float32)).astype(jnp.bfloat16)

def reference(point_feats, scene_id, hilbert_rank, norm_gains, w_qkv, w_proj, w_up, w_down):
    after_one = attention_block(point_feats, scene_id, norm_gains[0], w_qkv[0], w_proj[0], w_up[0], w_down[0])
    reordered = jnp.zeros_like(after_one).at[hilbert_rank].set(after_one)
    scene_moved = jnp.zeros_like(scene_id).at[hilbert_rank].set(scene_id)
    return attention_block(reordered, scene_moved, norm_gains[1], w_qkv[1], w_proj[1], w_up[1], w_down[1])
```

```python
import functools

import jax
import jax.numpy as jnp
from jax import lax
from jax.experimental import pallas as pl
from jax.experimental.pallas import tpu as pltpu
from jax.sharding import PartitionSpec as P

C = 256
HEADS = 16
HEAD = 16
ROWS = 1024
FFN = 1024
TILES = 32
TILE = 32
MOST_TILES = 3
EPSILON = 1e-05
QUERY_BLOCK = 256
WINDOW = 512
ROW_BLOCK = 256
SPLIT_SCALE = 8.0
SCORE_LIMIT = 40.0
VALUE_LIMIT = 40.0
BF16 = jnp.bfloat16
F32 = jnp.float32
F8 = jnp.float8_e4m3fn
VMEM_BYTES = 56 << 20


def dot(left, right, left_dim=1, right_dim=0):
    return lax.dot_general(
        left, right, (((left_dim,), (right_dim,)), ((), ())), preferred_element_type=F32
    )


def layer_norm(values, gain):
    center = values - jnp.mean(values, axis=-1, keepdims=True)
    spread = jnp.mean(center * center, axis=-1, keepdims=True)
    return (center * lax.rsqrt(spread + EPSILON) * gain).astype(BF16)


def split(values):
    scaled = values.astype(F32) * SPLIT_SCALE
    high = scaled.astype(F8).astype(F32)
    low = scaled - high
    return high, low


def gelu(values):
    return 0.5 * values * (1.0 + lax.erf(values * (0.5**0.5)))


class Scratch:
    names = (
        "w_qkv", "w_proj", "w_up", "w_down", "key", "query", "key_split", "query_split",
        "value", "scene_col", "mask", "attended", "normed", "result", "sems", "out_sem",
    )

    def __init__(self, refs):
        for name, ref in zip(self.names, refs, strict=True):
            setattr(self, name, ref)


def scratch_shapes():
    return [
        pltpu.VMEM((C, 3 * C), BF16),
        pltpu.VMEM((C, C), BF16),
        pltpu.VMEM((C, FFN), BF16),
        pltpu.VMEM((FFN, C), BF16),
        pltpu.VMEM((2, ROWS, 128), BF16),
        pltpu.VMEM((2, 128, ROWS), BF16),
        pltpu.VMEM((HEADS // 2, ROWS, 128), F8),
        pltpu.VMEM((HEADS, 128, ROWS), F8),
        pltpu.VMEM((HEADS, 2 * HEAD, ROWS), BF16),
        pltpu.VMEM((ROWS, 128), F32),
        pltpu.VMEM((ROWS, QUERY_BLOCK), BF16),
        pltpu.VMEM((C, ROWS), BF16),
        pltpu.VMEM((ROWS, C), BF16),
        pltpu.VMEM((ROWS, C), BF16),
        pltpu.SemaphoreType.DMA((4,)),
        pltpu.SemaphoreType.DMA,
    ]


def start_weights(block, weights, s):
    copies = [
        pltpu.make_async_copy(source.at[block], target, s.sems.at[i])
        for i, (source, target) in enumerate(
            zip(weights, (s.w_qkv, s.w_proj, s.w_up, s.w_down), strict=True)
        )
    ]
    for copy in copies:
        copy.start()
    return copies


def project(x, gain, s):
    for start in range(0, ROWS, ROW_BLOCK):
        rows = slice(start, start + ROW_BLOCK)
        s.normed[rows] = layer_norm(x[rows].astype(F32), gain)
    normed = s.normed[...]
    query = dot(s.w_qkv[:, 0:C], normed, 0, 1).astype(BF16)
    value = dot(s.w_qkv[:, 2 * C : 3 * C], normed, 0, 1).astype(BF16)
    for head in range(HEADS):
        s.value[head, 0:HEAD, :] = value[HEAD * head : HEAD * (head + 1)]
        s.value[head, HEAD:, :] = jnp.ones((HEAD, ROWS), BF16)
    s.query[0] = query[0:128]
    s.query[1] = query[128:256]
    high, low = split(query)
    for head in range(HEADS):
        part = slice(HEAD * head, HEAD * (head + 1))
        both = jnp.concatenate([high[part].astype(BF16), low[part].astype(BF16)], axis=0).astype(F8)
        own, other = 64 * (head % 2), 64 * (1 - head % 2)
        s.query_split[head, own : own + 32, :] = both
        s.query_split[head, own + 32 : own + 64, :] = both
        s.query_split[head, other : other + 64, :] = jnp.zeros((64, ROWS), F8)
    squares = query.astype(F32) * query.astype(F32)
    query_norm = jnp.max(jnp.sum(squares.reshape(HEADS, HEAD, ROWS), axis=1), axis=1, keepdims=True)

    row = lax.broadcasted_iota(jnp.int32, (64, 256), 0)
    lane = lax.broadcasted_iota(jnp.int32, (64, 256), 1)
    same = row == (lane // 64) * HEAD + lane % HEAD
    spread_high = jnp.where(same & (lane % 64 < 32), 1.0, 0.0).astype(BF16)
    spread_low = jnp.where(same & (lane % 64 >= 32), 1.0, 0.0).astype(BF16)
    spread = jnp.concatenate([spread_high, spread_low], axis=0).astype(F8)
    channel = lax.broadcasted_iota(jnp.int32, (C, 128), 0)
    column = lax.broadcasted_iota(jnp.int32, (C, 128), 1)
    head_sum = jnp.where(channel // HEAD == column, 1.0, 0.0).astype(BF16)
    key_norm = jnp.zeros((1, 128), F32)
    highest = jnp.max(jnp.abs(query.astype(F32)))
    key_high = jnp.zeros((1, C), F32)
    for start in range(0, ROWS, ROW_BLOCK):
        rows = slice(start, start + ROW_BLOCK)
        key = dot(s.normed[rows], s.w_qkv[:, C : 2 * C]).astype(BF16)
        s.key[0, rows] = key[:, 0:128]
        s.key[1, rows] = key[:, 128:256]
        wide = key.astype(F32)
        key_high = jnp.maximum(key_high, jnp.max(jnp.abs(wide), axis=0, keepdims=True))
        norms = dot((wide * wide).astype(BF16), head_sum)
        key_norm = jnp.maximum(key_norm, jnp.max(norms, axis=0, keepdims=True))
        high, low = split(key)
        for quarter in range(4):
            lanes = slice(64 * quarter, 64 * quarter + 64)
            pair = jnp.concatenate([high[:, lanes], low[:, lanes]], axis=1).astype(F8)
            expanded = dot(pair, spread).astype(F8)
            s.key_split[2 * quarter, rows] = expanded[:, 0:128]
            s.key_split[2 * quarter + 1, rows] = expanded[:, 128:256]
    largest = jnp.maximum(highest, jnp.max(key_high))
    bound = 0.25 * 1.02 * jnp.sqrt(jnp.max(query_norm) * jnp.max(key_norm))
    return bound, largest


def make_mask(keys, count, queries, scene_row, s):
    row = scene_row[:, queries].astype(F32)
    for start in range(0, count, 128):
        col = s.scene_col[pl.ds(keys + start, 128), :]
        for lane in range(0, QUERY_BLOCK, 128):
            same = col == row[:, lane : lane + 128]
            s.mask[start : start + 128, lane : lane + 128] = jnp.where(same, 1.0, 0.0).astype(BF16)


def finish(head, queries, output, s):
    start = HEAD * head if isinstance(head, int) else pl.multiple_of(HEAD * head, HEAD)
    s.attended[pl.ds(start, HEAD), queries] = (
        output[0:HEAD] * (1.0 / output[HEAD : HEAD + 1])
    ).astype(BF16)


def attend_bounded(count, first_key, scene_row, s):
    def block(index, carry):
        queries = pl.ds(pl.multiple_of(index * QUERY_BLOCK, QUERY_BLOCK), QUERY_BLOCK)
        start = first_key(index)
        keys = pl.ds(start, count)
        make_mask(start, count, queries, scene_row, s)
        mask = s.mask[0:count]
        for head in range(HEADS):
            score = dot(s.key_split[head // 2, keys, :], s.query_split[head, :, queries])
            weight = jnp.exp(score * (0.25 / SPLIT_SCALE**2)).astype(BF16) * mask
            finish(head, queries, dot(s.value[head, :, keys], weight), s)
        return carry

    lax.fori_loop(0, ROWS // QUERY_BLOCK, block, 0)


def attend_any(scene_row, s):
    lane_head = lax.broadcasted_iota(jnp.int32, (1, 128), 1) // HEAD

    def block(index, carry):
        queries = pl.ds(pl.multiple_of(index * QUERY_BLOCK, QUERY_BLOCK), QUERY_BLOCK)
        make_mask(0, ROWS, queries, scene_row, s)

        def one_head(head, carry):
            group = head // 8
            lanes = jnp.where(lane_head == head % 8, 1.0, 0.0).astype(BF16)
            score = dot(s.key[group] * lanes, s.query[group, :, queries]) * 0.25
            score = jnp.where(s.mask[...] > 0, score, F32(-1e30))
            top = jnp.max(score, axis=0, keepdims=True)
            weight = jnp.exp(score - top).astype(BF16)
            finish(head, queries, dot(s.value[head], weight), s)
            return carry

        return lax.fori_loop(0, HEADS, one_head, carry)

    lax.fori_loop(0, ROWS // QUERY_BLOCK, block, 0)


def scene_columns(scene_row, s):
    for start in range(0, ROWS, 128):
        piece = scene_row[:, start : start + 128].astype(F32)
        s.scene_col[start : start + 128, :] = jnp.transpose(jnp.broadcast_to(piece, (128, 128)))


def mlp_rows(rows, x, gain, s):
    attended = jnp.transpose(s.attended[:, rows])
    middle = (x[rows].astype(F32) + dot(attended, s.w_proj[...])).astype(BF16)
    normed = layer_norm(middle.astype(F32), gain)
    hidden = gelu(dot(normed, s.w_up[...])).astype(BF16)
    s.result[rows] = (middle.astype(F32) + dot(hidden, s.w_down[...])).astype(BF16)


def first_kernel(
    me_ref, rank_ref, x, scene_row_ref, gains, w_qkv, w_proj, w_up, w_down,
    send, up, down, local, *scratch,
):
    s = Scratch(scratch)
    copies = start_weights(0, (w_qkv, w_proj, w_up, w_down), s)
    scene_row = scene_row_ref
    scene_columns(scene_row, s)
    copies[0].wait()
    bound, largest = project(x, gains[0, 0:1], s)
    quick = (bound <= SCORE_LIMIT) & (largest <= VALUE_LIMIT)

    @pl.when(quick)
    def _():
        attend_bounded(ROWS, lambda index: 0, scene_row, s)

    @pl.when(jnp.logical_not(quick))
    def _():
        attend_any(scene_row, s)

    for copy in copies[1:]:
        copy.wait()
    me = me_ref[0]
    above, below = lax.rem(me + 1, 128), lax.rem(me + 127, 128)
    slots = (jnp.int32(0), jnp.int32(0))
    for start in range(0, ROWS, ROW_BLOCK):
        mlp_rows(slice(start, start + ROW_BLOCK), x, gains[0, 1:2], s)

        def one_tile(tile, slots):
            owner = rank_ref[tile * TILE] // ROWS
            source = s.result.at[pl.ds(pl.multiple_of(tile * TILE, TILE), TILE)]

            def put(target, index):
                place = target.at[pl.ds(pl.multiple_of(index * TILE, TILE), TILE)]
                pltpu.make_async_copy(source, place, s.out_sem).start()

            is_up, is_down, stays = owner == above, owner == below, owner == me

            @pl.when(is_up)
            def _():
                put(up, jnp.minimum(slots[0], MOST_TILES - 1))

            @pl.when(is_down)
            def _():
                put(down, jnp.minimum(slots[1], MOST_TILES - 1))

            @pl.when(stays)
            def _():
                put(local, tile)

            @pl.when(jnp.logical_not(is_up | is_down | stays))
            def _():
                put(send, owner)

            return (slots[0] + is_up.astype(jnp.int32), slots[1] + is_down.astype(jnp.int32))

        slots = lax.fori_loop(start // TILE, (start + ROW_BLOCK) // TILE, one_tile, slots)
    pltpu.make_async_copy(s.result, local, s.out_sem).wait()


def second_kernel(
    me_ref, place_ref, source_ref, scene_ref, scene_row_ref, gains, received, from_below, from_above, local,
    w_qkv, w_proj, w_up, w_down, out, x, in_sem, *scratch,
):
    s = Scratch(scratch)
    me = me_ref[0]
    above, below = lax.rem(me + 1, 128), lax.rem(me + 127, 128)

    def fetch(index, slots):
        owner = source_ref[index]
        target = x.at[pl.ds(pl.multiple_of(index * TILE, TILE), TILE)]

        def get(source, tile):
            place = source.at[pl.ds(pl.multiple_of(tile * TILE, TILE), TILE)]
            pltpu.make_async_copy(place, target, in_sem).start()

        is_up, is_down, stays = owner == above, owner == below, owner == me

        @pl.when(is_up)
        def _():
            get(from_above, jnp.minimum(slots[0], MOST_TILES - 1))

        @pl.when(is_down)
        def _():
            get(from_below, jnp.minimum(slots[1], MOST_TILES - 1))

        @pl.when(stays)
        def _():
            get(local, place_ref[index])

        @pl.when(jnp.logical_not(is_up | is_down | stays))
        def _():
            get(received, owner)

        return (slots[0] + is_up.astype(jnp.int32), slots[1] + is_down.astype(jnp.int32))

    lax.fori_loop(0, TILES, fetch, (jnp.int32(0), jnp.int32(0)))
    copies = start_weights(1, (w_qkv, w_proj, w_up, w_down), s)
    scene_row = scene_row_ref
    scene_columns(scene_row, s)
    pltpu.make_async_copy(local, x, in_sem).wait()
    copies[0].wait()
    bound, largest = project(x, gains[1, 0:1], s)
    quick = (bound <= SCORE_LIMIT) & (largest <= VALUE_LIMIT)

    def window_start(index):
        first = scene_ref[index * QUERY_BLOCK]
        start = jnp.int32(0)
        for piece in range(1, (ROWS - WINDOW) // 128 + 1):
            start = start + (scene_ref[128 * piece - 1] < first).astype(jnp.int32)
        return pl.multiple_of(start * 128, 128)

    fits = quick
    for index in range(ROWS // QUERY_BLOCK):
        last = scene_ref[(index + 1) * QUERY_BLOCK - 1]
        end = window_start(index) + WINDOW
        after = scene_ref[jnp.minimum(end, ROWS - 1)]
        fits = fits & ((end >= ROWS) | (after > last))

    @pl.when(fits)
    def _():
        attend_bounded(WINDOW, window_start, scene_row, s)

    @pl.when(quick & jnp.logical_not(fits))
    def _():
        attend_bounded(ROWS, lambda index: 0, scene_row, s)

    @pl.when(jnp.logical_not(quick))
    def _():
        attend_any(scene_row, s)

    for copy in copies[1:]:
        copy.wait()
    for start in range(0, ROWS, ROW_BLOCK):
        mlp_rows(slice(start, start + ROW_BLOCK), x, gains[1, 1:2], s)

        def one_tile(index, carry):
            source = s.result.at[pl.ds(pl.multiple_of(index * TILE, TILE), TILE)]
            place = out.at[pl.ds(pl.multiple_of(place_ref[index] * TILE, TILE), TILE)]
            pltpu.make_async_copy(source, place, s.out_sem).start()
            return carry

        lax.fori_loop(start // TILE, (start + ROW_BLOCK) // TILE, one_tile, 0)
    pltpu.make_async_copy(s.result, out, s.out_sem).wait()


SMEM = pl.BlockSpec(memory_space=pltpu.SMEM)
VMEM = pl.BlockSpec(memory_space=pltpu.VMEM)
HBM = pl.BlockSpec(memory_space=pl.ANY)


def shards(point_feats, scene_id, hilbert_rank, norm_gains, w_qkv, w_proj, w_up, w_down):
    devices = lax.axis_size("seq")
    me = lax.axis_index("seq")
    me_array = me.reshape(1).astype(jnp.int32)
    weights = (w_qkv, w_proj, w_up, w_down)
    tagged = scene_id + (hilbert_rank // ROWS) * 128
    tags = lax.all_gather(tagged, "seq", tiled=True)
    params = pltpu.CompilerParams(vmem_limit_bytes=VMEM_BYTES)
    rows = jax.ShapeDtypeStruct((ROWS, C), BF16)
    few = jax.ShapeDtypeStruct((MOST_TILES * TILE, C), BF16)
    send, up, down, local = pl.pallas_call(
        first_kernel,
        in_specs=[SMEM, SMEM, VMEM, VMEM, VMEM, HBM, HBM, HBM, HBM],
        out_specs=[HBM] * 4,
        out_shape=[jax.ShapeDtypeStruct((devices * TILE, C), BF16), few, few, rows],
        scratch_shapes=scratch_shapes(),
        compiler_params=params,
        name="first_block",
    )(me_array, hilbert_rank, point_feats, scene_id.reshape(1, ROWS), norm_gains, *weights)

    received = lax.all_to_all(send, "seq", split_axis=0, concat_axis=0, tiled=True)
    ring = range(devices)
    from_below = lax.ppermute(up, "seq", [(i, (i + 1) % devices) for i in ring])
    from_above = lax.ppermute(down, "seq", [(i, (i - 1) % devices) for i in ring])

    tags, _ = lax.optimization_barrier((tags, local))
    tags = tags.reshape(devices, ROWS)
    mine = tags // 128 == me
    scenes = jnp.sum(jnp.where(mine, tags % 128, 0), axis=0).reshape(TILES, TILE)
    source = jnp.sum(jnp.where(mine, jnp.arange(devices, dtype=jnp.int32)[:, None], 0), axis=0)
    source = source.reshape(TILES, TILE)[:, 0]
    place = jnp.arange(TILES, dtype=jnp.int32)
    order = source * TILES + place
    rank = jnp.sum((order[None, :] < order[:, None]).astype(jnp.int32), axis=1)
    chosen = rank[None, :] == place[:, None]
    place_sorted = jnp.sum(jnp.where(chosen, place[None, :], 0), axis=1)
    source_sorted = jnp.sum(jnp.where(chosen, source[None, :], 0), axis=1)
    scene_sorted = jnp.sum(jnp.where(chosen[:, :, None], scenes[None], 0), axis=1).reshape(ROWS)

    return pl.pallas_call(
        second_kernel,
        in_specs=[SMEM, SMEM, SMEM, SMEM, VMEM, VMEM] + [HBM] * 8,
        out_specs=HBM,
        out_shape=rows,
        scratch_shapes=[pltpu.VMEM((ROWS, C), BF16), pltpu.SemaphoreType.DMA] + scratch_shapes(),
        compiler_params=params,
        name="second_block",
    )(
        me_array, place_sorted, source_sorted, scene_sorted, scene_sorted.reshape(1, ROWS), norm_gains,
        received, from_below, from_above, local, *weights,
    )


def solution(mesh):
    placed = (P("seq", None), P("seq"), P("seq"), P(), P(), P(), P(), P())
    return jax.shard_map(
        shards, mesh=mesh, in_specs=placed, out_specs=P("seq", None), check_vma=False
    )
```

```python
import functools

import jax
import jax.numpy as jnp
from jax import lax
from jax.experimental import pallas as pl
from jax.experimental.pallas import tpu as pltpu
from jax.sharding import PartitionSpec as P

C = 256
HEADS = 16
HEAD = 16
ROWS = 1024
FFN = 1024
TILES = 32
TILE = 32
MOST_TILES = 3
EPSILON = 1e-05
QUERY_BLOCK = 256
WINDOW = 512
ROW_BLOCK = 256
SPLIT_SCALE = 8.0
SCORE_LIMIT = 40.0
VALUE_LIMIT = 40.0
BF16 = jnp.bfloat16
F32 = jnp.float32
F8 = jnp.float8_e4m3fn
VMEM_BYTES = 56 << 20


def dot(left, right, left_dim=1, right_dim=0):
    return lax.dot_general(
        left, right, (((left_dim,), (right_dim,)), ((), ())), preferred_element_type=F32
    )


def layer_norm(values, gain):
    center = values - jnp.mean(values, axis=-1, keepdims=True)
    spread = jnp.mean(center * center, axis=-1, keepdims=True)
    return (center * lax.rsqrt(spread + EPSILON) * gain).astype(BF16)


def split(values):
    scaled = values.astype(F32) * SPLIT_SCALE
    high = scaled.astype(F8).astype(F32)
    low = scaled - high
    return high, low


def gelu(values):
    return 0.5 * values * (1.0 + lax.erf(values * (0.5**0.5)))


class Scratch:
    names = (
        "w_qkv", "w_proj", "w_up", "w_down", "key", "query", "key_split", "query_split",
        "value", "scene_col", "mask", "attended", "normed", "result", "sems", "out_sem",
    )

    def __init__(self, refs):
        for name, ref in zip(self.names, refs, strict=True):
            setattr(self, name, ref)


def scratch_shapes():
    return [
        pltpu.VMEM((C, 3 * C), BF16),
        pltpu.VMEM((C, C), BF16),
        pltpu.VMEM((C, FFN), BF16),
        pltpu.VMEM((FFN, C), BF16),
        pltpu.VMEM((2, ROWS, 128), BF16),
        pltpu.VMEM((2, 128, ROWS), BF16),
        pltpu.VMEM((HEADS // 2, ROWS, 128), F8),
        pltpu.VMEM((HEADS, 128, ROWS), F8),
        pltpu.VMEM((HEADS, 2 * HEAD, ROWS), BF16),
        pltpu.VMEM((ROWS, 128), F32),
        pltpu.VMEM((ROWS, QUERY_BLOCK), BF16),
        pltpu.VMEM((C, ROWS), BF16),
        pltpu.VMEM((ROWS, C), BF16),
        pltpu.VMEM((ROWS, C), BF16),
        pltpu.SemaphoreType.DMA((4,)),
        pltpu.SemaphoreType.DMA,
    ]


def start_weights(block, weights, s):
    copies = [
        pltpu.make_async_copy(source.at[block], target, s.sems.at[i])
        for i, (source, target) in enumerate(
            zip(weights, (s.w_qkv, s.w_proj, s.w_up, s.w_down), strict=True)
        )
    ]
    for copy in copies:
        copy.start()
    return copies


def project(x, gain, s):
    for start in range(0, ROWS, ROW_BLOCK):
        rows = slice(start, start + ROW_BLOCK)
        s.normed[rows] = layer_norm(x[rows].astype(F32), gain)
    normed = s.normed[...]
    query = dot(s.w_qkv[:, 0:C], normed, 0, 1).astype(BF16)
    value = dot(s.w_qkv[:, 2 * C : 3 * C], normed, 0, 1).astype(BF16)
    for head in range(HEADS):
        s.value[head, 0:HEAD, :] = value[HEAD * head : HEAD * (head + 1)]
        s.value[head, HEAD:, :] = jnp.ones((HEAD, ROWS), BF16)
    s.query[0] = query[0:128]
    s.query[1] = query[128:256]
    high, low = split(query)
    for head in range(HEADS):
        part = slice(HEAD * head, HEAD * (head + 1))
        both = jnp.concatenate([high[part].astype(BF16), low[part].astype(BF16)], axis=0).astype(F8)
        own, other = 64 * (head % 2), 64 * (1 - head % 2)
        s.query_split[head, own : own + 32, :] = both
        s.query_split[head, own + 32 : own + 64, :] = both
        s.query_split[head, other : other + 64, :] = jnp.zeros((64, ROWS), F8)
    squares = query.astype(F32) * query.astype(F32)
    query_norm = jnp.max(jnp.sum(squares.reshape(HEADS, HEAD, ROWS), axis=1), axis=1, keepdims=True)

    row = lax.broadcasted_iota(jnp.int32, (64, 256), 0)
    lane = lax.broadcasted_iota(jnp.int32, (64, 256), 1)
    same = row == (lane // 64) * HEAD + lane % HEAD
    spread_high = jnp.where(same & (lane % 64 < 32), 1.0, 0.0).astype(BF16)
    spread_low = jnp.where(same & (lane % 64 >= 32), 1.0, 0.0).astype(BF16)
    spread = jnp.concatenate([spread_high, spread_low], axis=0).astype(F8)
    channel = lax.broadcasted_iota(jnp.int32, (C, 128), 0)
    column = lax.broadcasted_iota(jnp.int32, (C, 128), 1)
    head_sum = jnp.where(channel // HEAD == column, 1.0, 0.0).astype(BF16)
    key_norm = jnp.zeros((1, 128), F32)
    highest = jnp.max(jnp.abs(query.astype(F32)))
    key_high = jnp.zeros((1, C), F32)
    for start in range(0, ROWS, ROW_BLOCK):
        rows = slice(start, start + ROW_BLOCK)
        key = dot(s.normed[rows], s.w_qkv[:, C : 2 * C]).astype(BF16)
        s.key[0, rows] = key[:, 0:128]
        s.key[1, rows] = key[:, 128:256]
        wide = key.astype(F32)
        key_high = jnp.maximum(key_high, jnp.max(jnp.abs(wide), axis=0, keepdims=True))
        norms = dot((wide * wide).astype(BF16), head_sum)
        key_norm = jnp.maximum(key_norm, jnp.max(norms, axis=0, keepdims=True))
        high, low = split(key)
        for quarter in range(4):
            lanes = slice(64 * quarter, 64 * quarter + 64)
            pair = jnp.concatenate([high[:, lanes], low[:, lanes]], axis=1).astype(F8)
            expanded = dot(pair, spread).astype(F8)
            s.key_split[2 * quarter, rows] = expanded[:, 0:128]
            s.key_split[2 * quarter + 1, rows] = expanded[:, 128:256]
    largest = jnp.maximum(highest, jnp.max(key_high))
    bound = 0.25 * 1.02 * jnp.sqrt(jnp.max(query_norm) * jnp.max(key_norm))
    return bound, largest


def make_mask(keys, count, index, scenes, s):
    for lane in range(0, QUERY_BLOCK, 128):
        row = scenes[pl.ds(index * (QUERY_BLOCK // 128) + lane // 128, 1), :].astype(F32)
        for start in range(0, count, 128):
            same = s.scene_col[pl.ds(keys + start, 128), :] == row
            s.mask[start : start + 128, lane : lane + 128] = jnp.where(same, 1.0, 0.0).astype(BF16)


def finish(head, queries, output, s):
    start = HEAD * head if isinstance(head, int) else pl.multiple_of(HEAD * head, HEAD)
    s.attended[pl.ds(start, HEAD), queries] = (
        output[0:HEAD] * (1.0 / output[HEAD : HEAD + 1])
    ).astype(BF16)


def attend_bounded(count, first_key, scenes, s):
    def block(index, carry):
        queries = pl.ds(pl.multiple_of(index * QUERY_BLOCK, QUERY_BLOCK), QUERY_BLOCK)
        start = first_key(index)
        keys = pl.ds(start, count)
        make_mask(start, count, index, scenes, s)
        mask = s.mask[0:count]
        for head in range(HEADS):
            score = dot(s.key_split[head // 2, keys, :], s.query_split[head, :, queries])
            weight = jnp.exp(score * (0.25 / SPLIT_SCALE**2)).astype(BF16) * mask
            finish(head, queries, dot(s.value[head, :, keys], weight), s)
        return carry

    lax.fori_loop(0, ROWS // QUERY_BLOCK, block, 0)


def attend_any(scenes, s):
    lane_head = lax.broadcasted_iota(jnp.int32, (1, 128), 1) // HEAD

    def block(index, carry):
        queries = pl.ds(pl.multiple_of(index * QUERY_BLOCK, QUERY_BLOCK), QUERY_BLOCK)
        make_mask(0, ROWS, index, scenes, s)

        def one_head(head, carry):
            group = head // 8
            lanes = jnp.where(lane_head == head % 8, 1.0, 0.0).astype(BF16)
            score = dot(s.key[group] * lanes, s.query[group, :, queries]) * 0.25
            score = jnp.where(s.mask[...] > 0, score, F32(-1e30))
            top = jnp.max(score, axis=0, keepdims=True)
            weight = jnp.exp(score - top).astype(BF16)
            finish(head, queries, dot(s.value[head], weight), s)
            return carry

        return lax.fori_loop(0, HEADS, one_head, carry)

    lax.fori_loop(0, ROWS // QUERY_BLOCK, block, 0)


def scene_columns(scenes, s):
    for start in range(0, ROWS, 128):
        piece = scenes[start // 128 : start // 128 + 1, :].astype(F32)
        s.scene_col[start : start + 128, :] = jnp.transpose(jnp.broadcast_to(piece, (128, 128)))


def mlp_rows(rows, x, gain, s):
    attended = jnp.transpose(s.attended[:, rows])
    middle = (x[rows].astype(F32) + dot(attended, s.w_proj[...])).astype(BF16)
    normed = layer_norm(middle.astype(F32), gain)
    hidden = gelu(dot(normed, s.w_up[...])).astype(BF16)
    s.result[rows] = (middle.astype(F32) + dot(hidden, s.w_down[...])).astype(BF16)


def neighbours(me):
    return lax.rem(me + 1, 128), lax.rem(me + 127, 128)


def write_notes(me, rank_ref, scenes, notes):
    notes[...] = jnp.zeros_like(notes)
    above, below = neighbours(me)
    group = lax.broadcasted_iota(jnp.int32, (1, 128), 1) // TILE
    slots = (jnp.int32(0), jnp.int32(0))
    for tile in range(TILES):
        owner = rank_ref[tile * TILE] // ROWS
        is_up, is_down = (owner == above).astype(jnp.int32), (owner == below).astype(jnp.int32)
        slot = is_up * slots[0] + is_down * slots[1]
        row = scenes[tile // 4 : tile // 4 + 1, (tile % 4) * TILE : (tile % 4 + 1) * TILE]
        row = jnp.concatenate([row] * 4, axis=1) + 128 * (tile + 1)
        notes[owner] = notes[owner] + jnp.where(group == slot, row, 0)
        slots = (slots[0] + is_up, slots[1] + is_down)


def plan_kernel(me_ref, rank_ref, scene_ref, notes_ref, notes, scenes, plan, scene_out):
    me = me_ref[0]
    group = lax.broadcasted_iota(jnp.int32, (1, 128), 1) // TILE
    scene_out[...] = jnp.zeros_like(scene_out)

    def clear(index, carry):
        plan[index] = 0
        return carry

    lax.fori_loop(0, 4 * TILES, clear, 0)

    def add(index, place, source, first, last, row, slot):
        plan[index] = place
        plan[TILES + index] = source
        plan[2 * TILES + index] = first
        plan[3 * TILES + index] = last
        lane = lax.rem(index, 4)
        moved = pltpu.roll(row, TILE * lax.rem(lane - slot + 4, 4), 1)
        line = pl.ds(index // 4, 1)
        scene_out[line, :] = jnp.where(group == lane, moved, scene_out[line, :])

    def one_source(source, count):
        def received(slot, count):
            note = notes_ref[source, 0, slot * TILE]

            @pl.when(note > 0)
            def _():
                last = notes_ref[source, 0, slot * TILE + TILE - 1]
                add(count, note // 128 - 1, source, note % 128, last % 128, notes[source] % 128, slot)

            return count + (note > 0).astype(jnp.int32)

        def stays(tile, count):
            keep = rank_ref[tile * TILE] // ROWS == me

            @pl.when(keep)
            def _():
                first, last = scene_ref[tile * TILE], scene_ref[tile * TILE + TILE - 1]
                row = scenes[pl.ds(tile // 4, 1), :]
                add(count, tile, me, first, last, row, lax.rem(tile, 4))

            return count + keep.astype(jnp.int32)

        mine = source == me
        count = lax.fori_loop(0, jnp.where(mine, 0, MOST_TILES), received, count)
        return lax.fori_loop(0, jnp.where(mine, TILES, 0), stays, count)

    lax.fori_loop(0, 128, one_source, jnp.int32(0))


def first_kernel(
    me_ref, rank_ref, x, scenes, gains, w_qkv, w_proj, w_up, w_down,
    send, notes, up, down, local, *scratch,
):
    s = Scratch(scratch)
    copies = start_weights(0, (w_qkv, w_proj, w_up, w_down), s)
    write_notes(me_ref[0], rank_ref, scenes, notes)
    scene_columns(scenes, s)
    copies[0].wait()
    bound, largest = project(x, gains[0, 0:1], s)
    quick = (bound <= SCORE_LIMIT) & (largest <= VALUE_LIMIT)

    @pl.when(quick)
    def _():
        attend_bounded(ROWS, lambda index: 0, scenes, s)

    @pl.when(jnp.logical_not(quick))
    def _():
        attend_any(scenes, s)

    for copy in copies[1:]:
        copy.wait()
    me = me_ref[0]
    above, below = neighbours(me)
    slots = (jnp.int32(0), jnp.int32(0))
    for start in range(0, ROWS, ROW_BLOCK):
        mlp_rows(slice(start, start + ROW_BLOCK), x, gains[0, 1:2], s)

        def one_tile(tile, slots):
            owner = rank_ref[tile * TILE] // ROWS
            source = s.result.at[pl.ds(pl.multiple_of(tile * TILE, TILE), TILE)]

            def put(target, index):
                place = target.at[pl.ds(pl.multiple_of(index * TILE, TILE), TILE)]
                pltpu.make_async_copy(source, place, s.out_sem).start()

            is_up, is_down, stays = owner == above, owner == below, owner == me

            @pl.when(is_up)
            def _():
                put(up, jnp.minimum(slots[0], MOST_TILES - 1))

            @pl.when(is_down)
            def _():
                put(down, jnp.minimum(slots[1], MOST_TILES - 1))

            @pl.when(stays)
            def _():
                put(local, tile)

            @pl.when(jnp.logical_not(is_up | is_down | stays))
            def _():
                put(send, owner)

            return (slots[0] + is_up.astype(jnp.int32), slots[1] + is_down.astype(jnp.int32))

        slots = lax.fori_loop(start // TILE, (start + ROW_BLOCK) // TILE, one_tile, slots)
    pltpu.make_async_copy(s.result, local, s.out_sem).wait()


def second_kernel(
    me_ref, plan, scenes, gains, received, from_below, from_above, local,
    w_qkv, w_proj, w_up, w_down, out, x, in_sem, *scratch,
):
    s = Scratch(scratch)
    me = me_ref[0]
    above, below = neighbours(me)

    def fetch(index, slots):
        owner = plan[TILES + index]
        target = x.at[pl.ds(pl.multiple_of(index * TILE, TILE), TILE)]

        def get(source, tile):
            place = source.at[pl.ds(pl.multiple_of(tile * TILE, TILE), TILE)]
            pltpu.make_async_copy(place, target, in_sem).start()

        is_up, is_down, stays = owner == above, owner == below, owner == me

        @pl.when(is_up)
        def _():
            get(from_above, jnp.minimum(slots[0], MOST_TILES - 1))

        @pl.when(is_down)
        def _():
            get(from_below, jnp.minimum(slots[1], MOST_TILES - 1))

        @pl.when(stays)
        def _():
            get(local, plan[index])

        @pl.when(jnp.logical_not(is_up | is_down | stays))
        def _():
            get(received, owner)

        return (slots[0] + is_up.astype(jnp.int32), slots[1] + is_down.astype(jnp.int32))

    lax.fori_loop(0, TILES, fetch, (jnp.int32(0), jnp.int32(0)))
    copies = start_weights(1, (w_qkv, w_proj, w_up, w_down), s)
    scene_columns(scenes, s)
    pltpu.make_async_copy(local, x, in_sem).wait()
    copies[0].wait()
    bound, largest = project(x, gains[1, 0:1], s)
    quick = (bound <= SCORE_LIMIT) & (largest <= VALUE_LIMIT)

    def window_start(index):
        first = plan[2 * TILES + index * (QUERY_BLOCK // TILE)]
        start = jnp.int32(0)
        for piece in range(1, (ROWS - WINDOW) // 128 + 1):
            start = start + (plan[3 * TILES + 4 * piece - 1] < first).astype(jnp.int32)
        return pl.multiple_of(start * 128, 128)

    fits = quick
    for index in range(ROWS // QUERY_BLOCK):
        last = plan[3 * TILES + (index + 1) * (QUERY_BLOCK // TILE) - 1]
        end = window_start(index) + WINDOW
        after = plan[2 * TILES + jnp.minimum(end // TILE, TILES - 1)]
        fits = fits & ((end >= ROWS) | (after > last))

    @pl.when(fits)
    def _():
        attend_bounded(WINDOW, window_start, scenes, s)

    @pl.when(quick & jnp.logical_not(fits))
    def _():
        attend_bounded(ROWS, lambda index: 0, scenes, s)

    @pl.when(jnp.logical_not(quick))
    def _():
        attend_any(scenes, s)

    for copy in copies[1:]:
        copy.wait()
    for start in range(0, ROWS, ROW_BLOCK):
        mlp_rows(slice(start, start + ROW_BLOCK), x, gains[1, 1:2], s)

        def one_tile(index, carry):
            source = s.result.at[pl.ds(pl.multiple_of(index * TILE, TILE), TILE)]
            place = out.at[pl.ds(pl.multiple_of(plan[index] * TILE, TILE), TILE)]
            pltpu.make_async_copy(source, place, s.out_sem).start()
            return carry

        lax.fori_loop(start // TILE, (start + ROW_BLOCK) // TILE, one_tile, 0)
    pltpu.make_async_copy(s.result, out, s.out_sem).wait()


SMEM = pl.BlockSpec(memory_space=pltpu.SMEM)
VMEM = pl.BlockSpec(memory_space=pltpu.VMEM)
HBM = pl.BlockSpec(memory_space=pl.ANY)


def shards(point_feats, scene_id, hilbert_rank, norm_gains, w_qkv, w_proj, w_up, w_down):
    devices = lax.axis_size("seq")
    me = lax.axis_index("seq")
    me_array = me.reshape(1).astype(jnp.int32)
    weights = (w_qkv, w_proj, w_up, w_down)
    scenes = scene_id.reshape(ROWS // 128, 128)
    params = pltpu.CompilerParams(vmem_limit_bytes=VMEM_BYTES)
    rows = jax.ShapeDtypeStruct((ROWS, C), BF16)
    few = jax.ShapeDtypeStruct((MOST_TILES * TILE, C), BF16)
    send, notes, up, down, local = pl.pallas_call(
        first_kernel,
        in_specs=[SMEM, SMEM, VMEM, VMEM, VMEM, HBM, HBM, HBM, HBM],
        out_specs=[HBM, VMEM, HBM, HBM, HBM],
        out_shape=[
            jax.ShapeDtypeStruct((devices * TILE, C), BF16),
            jax.ShapeDtypeStruct((devices, 1, 128), jnp.int32),
            few,
            few,
            rows,
        ],
        scratch_shapes=scratch_shapes(),
        compiler_params=params,
        name="first_block",
    )(me_array, hilbert_rank, point_feats, scenes, norm_gains, *weights)

    received = lax.all_to_all(send, "seq", split_axis=0, concat_axis=0, tiled=True)
    ring = range(devices)
    from_below = lax.ppermute(up, "seq", [(i, (i + 1) % devices) for i in ring])
    from_above = lax.ppermute(down, "seq", [(i, (i - 1) % devices) for i in ring])
    notes = lax.all_to_all(notes, "seq", split_axis=0, concat_axis=0, tiled=True)
    plan, scenes = pl.pallas_call(
        plan_kernel,
        in_specs=[SMEM, SMEM, SMEM, SMEM, VMEM, VMEM],
        out_specs=[SMEM, VMEM],
        out_shape=[
            jax.ShapeDtypeStruct((4 * TILES,), jnp.int32),
            jax.ShapeDtypeStruct((ROWS // 128, 128), jnp.int32),
        ],
        compiler_params=params,
        name="plan",
    )(me_array, hilbert_rank, scene_id, notes, notes, scenes)

    return pl.pallas_call(
        second_kernel,
        in_specs=[SMEM, SMEM, VMEM, VMEM] + [HBM] * 8,
        out_specs=HBM,
        out_shape=rows,
        scratch_shapes=[pltpu.VMEM((ROWS, C), BF16), pltpu.SemaphoreType.DMA] + scratch_shapes(),
        compiler_params=params,
        name="second_block",
    )(me_array, plan, scenes, norm_gains, received, from_below, from_above, local, *weights)


def solution(mesh):
    placed = (P("seq", None), P("seq"), P("seq"), P(), P(), P(), P(), P())
    return jax.shard_map(
        shards, mesh=mesh, in_specs=placed, out_specs=P("seq", None), check_vma=False
    )
```

```python
import functools

import jax
import jax.numpy as jnp
from jax import lax
from jax.experimental import pallas as pl
from jax.experimental.pallas import tpu as pltpu
from jax.sharding import PartitionSpec as P

C = 256
HEADS = 16
HEAD = 16
ROWS = 1024
FFN = 1024
TILES = 32
TILE = 32
MOST_TILES = 3
EPSILON = 1e-05
QUERY_BLOCK = 256
WINDOW = 512
ROW_BLOCK = 256
SPLIT_SCALE = 8.0
SCORE_LIMIT = 40.0
VALUE_LIMIT = 40.0
BF16 = jnp.bfloat16
F32 = jnp.float32
F8 = jnp.float8_e4m3fn
VMEM_BYTES = 56 << 20


def dot(left, right, left_dim=1, right_dim=0):
    return lax.dot_general(
        left, right, (((left_dim,), (right_dim,)), ((), ())), preferred_element_type=F32
    )


def layer_norm(values, gain):
    center = values - jnp.mean(values, axis=-1, keepdims=True)
    spread = jnp.mean(center * center, axis=-1, keepdims=True)
    return (center * lax.rsqrt(spread + EPSILON) * gain).astype(BF16)


def split(values):
    scaled = values.astype(F32) * SPLIT_SCALE
    high = scaled.astype(F8).astype(F32)
    low = scaled - high
    return high, low


def gelu(values):
    return 0.5 * values * (1.0 + lax.erf(values * (0.5**0.5)))


class Scratch:
    names = (
        "w_qkv", "w_proj", "w_up", "w_down", "key", "query", "key_split", "query_split",
        "value", "scene_col", "mask", "attended", "normed", "result", "sems", "out_sem",
    )

    def __init__(self, refs):
        for name, ref in zip(self.names, refs, strict=True):
            setattr(self, name, ref)


def scratch_shapes():
    return [
        pltpu.VMEM((C, 3 * C), BF16),
        pltpu.VMEM((C, C), BF16),
        pltpu.VMEM((C, FFN), BF16),
        pltpu.VMEM((FFN, C), BF16),
        pltpu.VMEM((2, ROWS, 128), BF16),
        pltpu.VMEM((2, 128, ROWS), BF16),
        pltpu.VMEM((HEADS // 2, ROWS, 128), F8),
        pltpu.VMEM((HEADS, 128, ROWS), F8),
        pltpu.VMEM((HEADS, 2 * HEAD, ROWS), BF16),
        pltpu.VMEM((ROWS, 128), F32),
        pltpu.VMEM((ROWS, QUERY_BLOCK), BF16),
        pltpu.VMEM((C, ROWS), BF16),
        pltpu.VMEM((ROWS, C), BF16),
        pltpu.VMEM((ROWS, C), BF16),
        pltpu.SemaphoreType.DMA((4,)),
        pltpu.SemaphoreType.DMA,
    ]


def start_weights(block, weights, s):
    copies = [
        pltpu.make_async_copy(source.at[block], target, s.sems.at[i])
        for i, (source, target) in enumerate(
            zip(weights, (s.w_qkv, s.w_proj, s.w_up, s.w_down), strict=True)
        )
    ]
    for copy in copies:
        copy.start()
    return copies


def project(x, gain, s):
    for start in range(0, ROWS, ROW_BLOCK):
        rows = slice(start, start + ROW_BLOCK)
        s.normed[rows] = layer_norm(x[rows].astype(F32), gain)
    normed = s.normed[...]
    query = dot(s.w_qkv[:, 0:C], normed, 0, 1).astype(BF16)
    value = dot(s.w_qkv[:, 2 * C : 3 * C], normed, 0, 1).astype(BF16)
    for head in range(HEADS):
        s.value[head, 0:HEAD, :] = value[HEAD * head : HEAD * (head + 1)]
        s.value[head, HEAD:, :] = jnp.ones((HEAD, ROWS), BF16)
    s.query[0] = query[0:128]
    s.query[1] = query[128:256]
    high, low = split(query)
    for head in range(HEADS):
        part = slice(HEAD * head, HEAD * (head + 1))
        both = jnp.concatenate([high[part].astype(BF16), low[part].astype(BF16)], axis=0).astype(F8)
        own, other = 64 * (head % 2), 64 * (1 - head % 2)
        s.query_split[head, own : own + 32, :] = both
        s.query_split[head, own + 32 : own + 64, :] = both
        s.query_split[head, other : other + 64, :] = jnp.zeros((64, ROWS), F8)
    squares = query.astype(F32) * query.astype(F32)
    query_norm = jnp.max(jnp.sum(squares.reshape(HEADS, HEAD, ROWS), axis=1), axis=1, keepdims=True)

    row = lax.broadcasted_iota(jnp.int32, (64, 256), 0)
    lane = lax.broadcasted_iota(jnp.int32, (64, 256), 1)
    same = row == (lane // 64) * HEAD + lane % HEAD
    spread_high = jnp.where(same & (lane % 64 < 32), 1.0, 0.0).astype(BF16)
    spread_low = jnp.where(same & (lane % 64 >= 32), 1.0, 0.0).astype(BF16)
    spread = jnp.concatenate([spread_high, spread_low], axis=0).astype(F8)
    channel = lax.broadcasted_iota(jnp.int32, (C, 128), 0)
    column = lax.broadcasted_iota(jnp.int32, (C, 128), 1)
    head_sum = jnp.where(channel // HEAD == column, 1.0, 0.0).astype(BF16)
    key_norm = jnp.zeros((1, 128), F32)
    highest = jnp.max(jnp.abs(query.astype(F32)))
    key_high = jnp.zeros((1, C), F32)
    for start in range(0, ROWS, ROW_BLOCK):
        rows = slice(start, start + ROW_BLOCK)
        key = dot(s.normed[rows], s.w_qkv[:, C : 2 * C]).astype(BF16)
        s.key[0, rows] = key[:, 0:128]
        s.key[1, rows] = key[:, 128:256]
        wide = key.astype(F32)
        key_high = jnp.maximum(key_high, jnp.max(jnp.abs(wide), axis=0, keepdims=True))
        norms = dot((wide * wide).astype(BF16), head_sum)
        key_norm = jnp.maximum(key_norm, jnp.max(norms, axis=0, keepdims=True))
        high, low = split(key)
        for quarter in range(4):
            lanes = slice(64 * quarter, 64 * quarter + 64)
            pair = jnp.concatenate([high[:, lanes], low[:, lanes]], axis=1).astype(F8)
            expanded = dot(pair, spread).astype(F8)
            s.key_split[2 * quarter, rows] = expanded[:, 0:128]
            s.key_split[2 * quarter + 1, rows] = expanded[:, 128:256]
    largest = jnp.maximum(highest, jnp.max(key_high))
    bound = 0.25 * 1.02 * jnp.sqrt(jnp.max(query_norm) * jnp.max(key_norm))
    return bound, largest


def make_mask(keys, count, index, scenes, s):
    for lane in range(0, QUERY_BLOCK, 128):
        row = scenes[pl.ds(index * (QUERY_BLOCK // 128) + lane // 128, 1), :].astype(F32)
        for start in range(0, count, 128):
            same = s.scene_col[pl.ds(keys + start, 128), :] == row
            s.mask[start : start + 128, lane : lane + 128] = jnp.where(same, 1.0, 0.0).astype(BF16)


def finish(head, queries, output, s):
    start = HEAD * head if isinstance(head, int) else pl.multiple_of(HEAD * head, HEAD)
    s.attended[pl.ds(start, HEAD), queries] = (
        output[0:HEAD] * (1.0 / output[HEAD : HEAD + 1])
    ).astype(BF16)


def attend_bounded(count, first_key, scenes, s):
    def block(index, carry):
        queries = pl.ds(pl.multiple_of(index * QUERY_BLOCK, QUERY_BLOCK), QUERY_BLOCK)
        start = first_key(index)
        keys = pl.ds(start, count)
        make_mask(start, count, index, scenes, s)
        mask = s.mask[0:count]
        for head in range(HEADS):
            score = dot(s.key_split[head // 2, keys, :], s.query_split[head, :, queries])
            weight = jnp.exp(score * (0.25 / SPLIT_SCALE**2)).astype(BF16) * mask
            finish(head, queries, dot(s.value[head, :, keys], weight), s)
        return carry

    lax.fori_loop(0, ROWS // QUERY_BLOCK, block, 0)


def attend_any(scenes, s):
    lane_head = lax.broadcasted_iota(jnp.int32, (1, 128), 1) // HEAD

    def block(index, carry):
        queries = pl.ds(pl.multiple_of(index * QUERY_BLOCK, QUERY_BLOCK), QUERY_BLOCK)
        make_mask(0, ROWS, index, scenes, s)

        def one_head(head, carry):
            group = head // 8
            lanes = jnp.where(lane_head == head % 8, 1.0, 0.0).astype(BF16)
            score = dot(s.key[group] * lanes, s.query[group, :, queries]) * 0.25
            score = jnp.where(s.mask[...] > 0, score, F32(-1e30))
            top = jnp.max(score, axis=0, keepdims=True)
            weight = jnp.exp(score - top).astype(BF16)
            finish(head, queries, dot(s.value[head], weight), s)
            return carry

        return lax.fori_loop(0, HEADS, one_head, carry)

    lax.fori_loop(0, ROWS // QUERY_BLOCK, block, 0)


def scene_columns(scenes, s):
    for start in range(0, ROWS, 128):
        piece = scenes[start // 128 : start // 128 + 1, :].astype(F32)
        s.scene_col[start : start + 128, :] = jnp.transpose(jnp.broadcast_to(piece, (128, 128)))


def mlp_rows(rows, x, gain, s):
    attended = jnp.transpose(s.attended[:, rows])
    middle = (x[rows].astype(F32) + dot(attended, s.w_proj[...])).astype(BF16)
    normed = layer_norm(middle.astype(F32), gain)
    hidden = gelu(dot(normed, s.w_up[...])).astype(BF16)
    s.result[rows] = (middle.astype(F32) + dot(hidden, s.w_down[...])).astype(BF16)


def neighbours(me):
    return lax.rem(me + 1, 128), lax.rem(me + 127, 128)


def write_notes(me, rank_ref, scenes, notes):
    notes[...] = jnp.zeros_like(notes)
    above, below = neighbours(me)
    group = lax.broadcasted_iota(jnp.int32, (1, 128), 1) // TILE
    slots = (jnp.int32(0), jnp.int32(0))
    for tile in range(TILES):
        owner = rank_ref[tile * TILE] // ROWS
        is_up, is_down = (owner == above).astype(jnp.int32), (owner == below).astype(jnp.int32)
        slot = is_up * slots[0] + is_down * slots[1]
        row = scenes[tile // 4 : tile // 4 + 1, (tile % 4) * TILE : (tile % 4 + 1) * TILE]
        row = jnp.concatenate([row] * 4, axis=1) + 128 * (tile + 1)
        line = owner ^ me
        notes[line] = notes[line] + jnp.where(group == slot, row, 0)
        slots = (slots[0] + is_up, slots[1] + is_down)


def plan_kernel(me_ref, rank_ref, scene_ref, notes_ref, notes, scenes, plan, scene_out, found):
    me = me_ref[0]
    stay = 4 * 128

    def received(source, count):
        for slot in range(MOST_TILES):
            found[count] = 4 * source + slot
            count = count + jnp.minimum(notes_ref[source ^ me, 0, slot * TILE], 1)
        return count

    def kept(tile, count):
        found[count] = stay + tile
        return count + (rank_ref[tile * TILE] // ROWS == me).astype(jnp.int32)

    count = lax.fori_loop(0, me, received, jnp.int32(0))
    count = lax.fori_loop(0, TILES, kept, count)
    lax.fori_loop(me + 1, 128, received, count)
    group = lax.broadcasted_iota(jnp.int32, (1, 128), 1) // TILE
    for index in range(TILES):
        code = found[index]
        keeps = code >= stay
        tile = jnp.where(keeps, code - stay, 0)
        source = jnp.where(keeps, me, jnp.minimum(code // 4, 127))
        slot = jnp.where(keeps, lax.rem(tile, 4), lax.rem(code, 4))
        start = notes_ref[source ^ me, 0, slot * TILE]
        end = notes_ref[source ^ me, 0, slot * TILE + TILE - 1]
        plan[index] = jnp.where(keeps, tile, start // 128 - 1)
        plan[TILES + index] = source
        plan[2 * TILES + index] = jnp.where(keeps, scene_ref[tile * TILE], lax.rem(start, 128))
        plan[3 * TILES + index] = jnp.where(keeps, scene_ref[tile * TILE + TILE - 1], lax.rem(end, 128))
        row = jnp.where(keeps, scenes[pl.ds(tile // 4, 1), :], notes[source ^ me] & 127)
        moved = pltpu.roll(row, TILE * lax.rem(index % 4 - slot + 4, 4), 1)
        line = slice(index // 4, index // 4 + 1)
        if index % 4 == 0:
            scene_out[line, :] = moved
        else:
            scene_out[line, :] = jnp.where(group == index % 4, moved, scene_out[line, :])


def first_kernel(
    me_ref, rank_ref, x, scenes, gains, w_qkv, w_proj, w_up, w_down,
    send, notes, up, down, local, *scratch,
):
    s = Scratch(scratch)
    copies = start_weights(0, (w_qkv, w_proj, w_up, w_down), s)
    write_notes(me_ref[0], rank_ref, scenes, notes)
    scene_columns(scenes, s)
    copies[0].wait()
    bound, largest = project(x, gains[0, 0:1], s)
    quick = (bound <= SCORE_LIMIT) & (largest <= VALUE_LIMIT)

    @pl.when(quick)
    def _():
        attend_bounded(ROWS, lambda index: 0, scenes, s)

    @pl.when(jnp.logical_not(quick))
    def _():
        attend_any(scenes, s)

    for copy in copies[1:]:
        copy.wait()
    me = me_ref[0]
    above, below = neighbours(me)
    slots = (jnp.int32(0), jnp.int32(0))
    for start in range(0, ROWS, ROW_BLOCK):
        mlp_rows(slice(start, start + ROW_BLOCK), x, gains[0, 1:2], s)

        def one_tile(tile, slots):
            owner = rank_ref[tile * TILE] // ROWS
            source = s.result.at[pl.ds(pl.multiple_of(tile * TILE, TILE), TILE)]

            def put(target, index):
                place = target.at[pl.ds(pl.multiple_of(index * TILE, TILE), TILE)]
                pltpu.make_async_copy(source, place, s.out_sem).start()

            is_up, is_down, stays = owner == above, owner == below, owner == me

            @pl.when(is_up)
            def _():
                put(up, jnp.minimum(slots[0], MOST_TILES - 1))

            @pl.when(is_down)
            def _():
                put(down, jnp.minimum(slots[1], MOST_TILES - 1))

            @pl.when(stays)
            def _():
                put(local, tile)

            @pl.when(jnp.logical_not(is_up | is_down | stays))
            def _():
                put(send, owner)

            return (slots[0] + is_up.astype(jnp.int32), slots[1] + is_down.astype(jnp.int32))

        slots = lax.fori_loop(start // TILE, (start + ROW_BLOCK) // TILE, one_tile, slots)
    pltpu.make_async_copy(s.result, local, s.out_sem).wait()


def second_kernel(
    me_ref, plan, scenes, gains, received, from_below, from_above, local,
    w_qkv, w_proj, w_up, w_down, out, x, in_sem, *scratch,
):
    s = Scratch(scratch)
    me = me_ref[0]
    above, below = neighbours(me)

    def fetch(index, slots):
        owner = plan[TILES + index]
        target = x.at[pl.ds(pl.multiple_of(index * TILE, TILE), TILE)]

        def get(source, tile):
            place = source.at[pl.ds(pl.multiple_of(tile * TILE, TILE), TILE)]
            pltpu.make_async_copy(place, target, in_sem).start()

        is_up, is_down, stays = owner == above, owner == below, owner == me

        @pl.when(is_up)
        def _():
            get(from_above, jnp.minimum(slots[0], MOST_TILES - 1))

        @pl.when(is_down)
        def _():
            get(from_below, jnp.minimum(slots[1], MOST_TILES - 1))

        @pl.when(stays)
        def _():
            get(local, plan[index])

        @pl.when(jnp.logical_not(is_up | is_down | stays))
        def _():
            get(received, owner)

        return (slots[0] + is_up.astype(jnp.int32), slots[1] + is_down.astype(jnp.int32))

    lax.fori_loop(0, TILES, fetch, (jnp.int32(0), jnp.int32(0)))
    copies = start_weights(1, (w_qkv, w_proj, w_up, w_down), s)
    scene_columns(scenes, s)
    pltpu.make_async_copy(local, x, in_sem).wait()
    copies[0].wait()
    bound, largest = project(x, gains[1, 0:1], s)
    quick = (bound <= SCORE_LIMIT) & (largest <= VALUE_LIMIT)

    def window_start(index):
        first = plan[2 * TILES + index * (QUERY_BLOCK // TILE)]
        start = jnp.int32(0)
        for piece in range(1, (ROWS - WINDOW) // 128 + 1):
            start = start + (plan[3 * TILES + 4 * piece - 1] < first).astype(jnp.int32)
        return pl.multiple_of(start * 128, 128)

    fits = quick
    for index in range(ROWS // QUERY_BLOCK):
        last = plan[3 * TILES + (index + 1) * (QUERY_BLOCK // TILE) - 1]
        end = window_start(index) + WINDOW
        after = plan[2 * TILES + jnp.minimum(end // TILE, TILES - 1)]
        fits = fits & ((end >= ROWS) | (after > last))

    @pl.when(fits)
    def _():
        attend_bounded(WINDOW, window_start, scenes, s)

    @pl.when(quick & jnp.logical_not(fits))
    def _():
        attend_bounded(ROWS, lambda index: 0, scenes, s)

    @pl.when(jnp.logical_not(quick))
    def _():
        attend_any(scenes, s)

    for copy in copies[1:]:
        copy.wait()
    for start in range(0, ROWS, ROW_BLOCK):
        mlp_rows(slice(start, start + ROW_BLOCK), x, gains[1, 1:2], s)

        def one_tile(index, carry):
            source = s.result.at[pl.ds(pl.multiple_of(index * TILE, TILE), TILE)]
            place = out.at[pl.ds(pl.multiple_of(plan[index] * TILE, TILE), TILE)]
            pltpu.make_async_copy(source, place, s.out_sem).start()
            return carry

        lax.fori_loop(start // TILE, (start + ROW_BLOCK) // TILE, one_tile, 0)
    pltpu.make_async_copy(s.result, out, s.out_sem).wait()


SMEM = pl.BlockSpec(memory_space=pltpu.SMEM)
VMEM = pl.BlockSpec(memory_space=pltpu.VMEM)
HBM = pl.BlockSpec(memory_space=pl.ANY)


def exchange(rows, devices):
    bits = devices.bit_length() - 1
    lanes = rows.shape[1:]
    shift = bits
    while shift:
        step = 2 if shift > 1 else 1
        shift -= step
        count = 1 << step
        parts = rows.reshape((count, devices // count) + lanes)
        pieces = [parts[0]] + [
            lax.ppermute(parts[v], "seq", [(i, i ^ (v << shift)) for i in range(devices)])
            for v in range(1, count)
        ]
        rows = jnp.stack(pieces, axis=1).reshape((devices,) + lanes)
    return rows


def shards(point_feats, scene_id, hilbert_rank, norm_gains, w_qkv, w_proj, w_up, w_down):
    devices = lax.axis_size("seq")
    me = lax.axis_index("seq")
    me_array = me.reshape(1).astype(jnp.int32)
    weights = (w_qkv, w_proj, w_up, w_down)
    scenes = scene_id.reshape(ROWS // 128, 128)
    params = pltpu.CompilerParams(vmem_limit_bytes=VMEM_BYTES)
    rows = jax.ShapeDtypeStruct((ROWS, C), BF16)
    few = jax.ShapeDtypeStruct((MOST_TILES * TILE, C), BF16)
    send, notes, up, down, local = pl.pallas_call(
        first_kernel,
        in_specs=[SMEM, SMEM, VMEM, VMEM, VMEM, HBM, HBM, HBM, HBM],
        out_specs=[HBM, VMEM, HBM, HBM, HBM],
        out_shape=[
            jax.ShapeDtypeStruct((devices * TILE, C), BF16),
            jax.ShapeDtypeStruct((devices, 1, 128), jnp.int32),
            few,
            few,
            rows,
        ],
        scratch_shapes=scratch_shapes(),
        compiler_params=params,
        name="first_block",
    )(me_array, hilbert_rank, point_feats, scenes, norm_gains, *weights)

    received = lax.all_to_all(send, "seq", split_axis=0, concat_axis=0, tiled=True)
    ring = range(devices)
    from_below = lax.ppermute(up, "seq", [(i, (i + 1) % devices) for i in ring])
    from_above = lax.ppermute(down, "seq", [(i, (i - 1) % devices) for i in ring])
    notes = exchange(notes, devices)
    plan, scenes = pl.pallas_call(
        plan_kernel,
        in_specs=[SMEM, SMEM, SMEM, SMEM, VMEM, VMEM],
        out_specs=[SMEM, VMEM],
        out_shape=[
            jax.ShapeDtypeStruct((4 * TILES,), jnp.int32),
            jax.ShapeDtypeStruct((ROWS // 128, 128), jnp.int32),
        ],
        scratch_shapes=[pltpu.SMEM((2 * TILES,), jnp.int32)],
        compiler_params=params,
        cost_estimate=pl.CostEstimate(flops=1, bytes_accessed=1, transcendentals=0),
        name="plan",
    )(me_array, hilbert_rank, scene_id, notes, notes, scenes)

    return pl.pallas_call(
        second_kernel,
        in_specs=[SMEM, SMEM, VMEM, VMEM] + [HBM] * 8,
        out_specs=HBM,
        out_shape=rows,
        scratch_shapes=[pltpu.VMEM((ROWS, C), BF16), pltpu.SemaphoreType.DMA] + scratch_shapes(),
        compiler_params=params,
        name="second_block",
    )(me_array, plan, scenes, norm_gains, received, from_below, from_above, local, *weights)


def solution(mesh):
    placed = (P("seq", None), P("seq"), P("seq"), P(), P(), P(), P(), P())
    return jax.shard_map(
        shards, mesh=mesh, in_specs=placed, out_specs=P("seq", None), check_vma=False
    )
```

```python
import functools

import jax
import jax.numpy as jnp
from jax import lax
from jax.experimental import pallas as pl
from jax.experimental.pallas import tpu as pltpu
from jax.sharding import PartitionSpec as P

C = 256
HEADS = 16
HEAD = 16
ROWS = 1024
FFN = 1024
TILES = 32
TILE = 32
MOST_TILES = 3
CHIPS = 64
STRIDE = 48
EPSILON = 1e-05
QUERY_BLOCK = 256
WINDOW = 512
ROW_BLOCK = 256
SPLIT_SCALE = 8.0
SCORE_LIMIT = 40.0
VALUE_LIMIT = 40.0
BF16 = jnp.bfloat16
F32 = jnp.float32
F8 = jnp.float8_e4m3fn
VMEM_BYTES = 56 << 20


def dot(left, right, left_dim=1, right_dim=0):
    return lax.dot_general(
        left, right, (((left_dim,), (right_dim,)), ((), ())), preferred_element_type=F32
    )


def layer_norm(values, gain):
    center = values - jnp.mean(values, axis=-1, keepdims=True)
    spread = jnp.mean(center * center, axis=-1, keepdims=True)
    return (center * lax.rsqrt(spread + EPSILON) * gain).astype(BF16)


def split(values):
    scaled = values.astype(F32) * SPLIT_SCALE
    high = scaled.astype(F8).astype(F32)
    low = scaled - high
    return high, low


def gelu(values):
    return 0.5 * values * (1.0 + lax.erf(values * (0.5**0.5)))


class Scratch:
    names = (
        "w_qkv", "w_proj", "w_up", "w_down", "key", "query", "key_split", "query_split",
        "value", "scene_col", "mask", "attended", "normed", "result", "sems", "out_sem",
    )

    def __init__(self, refs):
        for name, ref in zip(self.names, refs, strict=True):
            setattr(self, name, ref)


def scratch_shapes():
    return [
        pltpu.VMEM((C, 3 * C), BF16),
        pltpu.VMEM((C, C), BF16),
        pltpu.VMEM((C, FFN), BF16),
        pltpu.VMEM((FFN, C), BF16),
        pltpu.VMEM((2, ROWS, 128), BF16),
        pltpu.VMEM((2, 128, ROWS), BF16),
        pltpu.VMEM((HEADS // 2, ROWS, 128), F8),
        pltpu.VMEM((HEADS, 128, ROWS), F8),
        pltpu.VMEM((HEADS, 2 * HEAD, ROWS), BF16),
        pltpu.VMEM((ROWS, 128), F32),
        pltpu.VMEM((ROWS, QUERY_BLOCK), BF16),
        pltpu.VMEM((C, ROWS), BF16),
        pltpu.VMEM((ROWS, C), BF16),
        pltpu.VMEM((ROWS, C), BF16),
        pltpu.SemaphoreType.DMA((4,)),
        pltpu.SemaphoreType.DMA,
    ]


def start_weights(block, weights, s):
    copies = [
        pltpu.make_async_copy(source.at[block], target, s.sems.at[i])
        for i, (source, target) in enumerate(
            zip(weights, (s.w_qkv, s.w_proj, s.w_up, s.w_down), strict=True)
        )
    ]
    for copy in copies:
        copy.start()
    return copies


def project(x, gain, s):
    for start in range(0, ROWS, ROW_BLOCK):
        rows = slice(start, start + ROW_BLOCK)
        s.normed[rows] = layer_norm(x[rows].astype(F32), gain)
    normed = s.normed[...]
    query = dot(s.w_qkv[:, 0:C], normed, 0, 1).astype(BF16)
    value = dot(s.w_qkv[:, 2 * C : 3 * C], normed, 0, 1).astype(BF16)
    for head in range(HEADS):
        s.value[head, 0:HEAD, :] = value[HEAD * head : HEAD * (head + 1)]
        s.value[head, HEAD:, :] = jnp.ones((HEAD, ROWS), BF16)
    s.query[0] = query[0:128]
    s.query[1] = query[128:256]
    high, low = split(query)
    for head in range(HEADS):
        part = slice(HEAD * head, HEAD * (head + 1))
        both = jnp.concatenate([high[part].astype(BF16), low[part].astype(BF16)], axis=0).astype(F8)
        own, other = 64 * (head % 2), 64 * (1 - head % 2)
        s.query_split[head, own : own + 32, :] = both
        s.query_split[head, own + 32 : own + 64, :] = both
        s.query_split[head, other : other + 64, :] = jnp.zeros((64, ROWS), F8)
    squares = query.astype(F32) * query.astype(F32)
    query_norm = jnp.max(jnp.sum(squares.reshape(HEADS, HEAD, ROWS), axis=1), axis=1, keepdims=True)

    row = lax.broadcasted_iota(jnp.int32, (64, 256), 0)
    lane = lax.broadcasted_iota(jnp.int32, (64, 256), 1)
    same = row == (lane // 64) * HEAD + lane % HEAD
    spread_high = jnp.where(same & (lane % 64 < 32), 1.0, 0.0).astype(BF16)
    spread_low = jnp.where(same & (lane % 64 >= 32), 1.0, 0.0).astype(BF16)
    spread = jnp.concatenate([spread_high, spread_low], axis=0).astype(F8)
    channel = lax.broadcasted_iota(jnp.int32, (C, 128), 0)
    column = lax.broadcasted_iota(jnp.int32, (C, 128), 1)
    head_sum = jnp.where(channel // HEAD == column, 1.0, 0.0).astype(BF16)
    key_norm = jnp.zeros((1, 128), F32)
    highest = jnp.max(jnp.abs(query.astype(F32)))
    key_high = jnp.zeros((1, C), F32)
    for start in range(0, ROWS, ROW_BLOCK):
        rows = slice(start, start + ROW_BLOCK)
        key = dot(s.normed[rows], s.w_qkv[:, C : 2 * C]).astype(BF16)
        s.key[0, rows] = key[:, 0:128]
        s.key[1, rows] = key[:, 128:256]
        wide = key.astype(F32)
        key_high = jnp.maximum(key_high, jnp.max(jnp.abs(wide), axis=0, keepdims=True))
        norms = dot((wide * wide).astype(BF16), head_sum)
        key_norm = jnp.maximum(key_norm, jnp.max(norms, axis=0, keepdims=True))
        high, low = split(key)
        for quarter in range(4):
            lanes = slice(64 * quarter, 64 * quarter + 64)
            pair = jnp.concatenate([high[:, lanes], low[:, lanes]], axis=1).astype(F8)
            expanded = dot(pair, spread).astype(F8)
            s.key_split[2 * quarter, rows] = expanded[:, 0:128]
            s.key_split[2 * quarter + 1, rows] = expanded[:, 128:256]
    largest = jnp.maximum(highest, jnp.max(key_high))
    bound = 0.25 * 1.02 * jnp.sqrt(jnp.max(query_norm) * jnp.max(key_norm))
    return bound, largest


def make_mask(keys, count, index, scenes, s):
    for lane in range(0, QUERY_BLOCK, 128):
        row = scenes[pl.ds(index * (QUERY_BLOCK // 128) + lane // 128, 1), :].astype(F32)
        for start in range(0, count, 128):
            same = s.scene_col[pl.ds(keys + start, 128), :] == row
            s.mask[start : start + 128, lane : lane + 128] = jnp.where(same, 1.0, 0.0).astype(BF16)


def finish(head, queries, output, s):
    start = HEAD * head if isinstance(head, int) else pl.multiple_of(HEAD * head, HEAD)
    s.attended[pl.ds(start, HEAD), queries] = (
        output[0:HEAD] * (1.0 / output[HEAD : HEAD + 1])
    ).astype(BF16)


def attend_bounded(count, first_key, scenes, s):
    def block(index, carry):
        queries = pl.ds(pl.multiple_of(index * QUERY_BLOCK, QUERY_BLOCK), QUERY_BLOCK)
        start = first_key(index)
        keys = pl.ds(start, count)
        make_mask(start, count, index, scenes, s)
        mask = s.mask[0:count]
        for head in range(HEADS):
            score = dot(s.key_split[head // 2, keys, :], s.query_split[head, :, queries])
            weight = jnp.exp(score * (0.25 / SPLIT_SCALE**2)).astype(BF16) * mask
            finish(head, queries, dot(s.value[head, :, keys], weight), s)
        return carry

    lax.fori_loop(0, ROWS // QUERY_BLOCK, block, 0)


def attend_any(scenes, s):
    lane_head = lax.broadcasted_iota(jnp.int32, (1, 128), 1) // HEAD

    def block(index, carry):
        queries = pl.ds(pl.multiple_of(index * QUERY_BLOCK, QUERY_BLOCK), QUERY_BLOCK)
        make_mask(0, ROWS, index, scenes, s)

        def one_head(head, carry):
            group = head // 8
            lanes = jnp.where(lane_head == head % 8, 1.0, 0.0).astype(BF16)
            score = dot(s.key[group] * lanes, s.query[group, :, queries]) * 0.25
            score = jnp.where(s.mask[...] > 0, score, F32(-1e30))
            top = jnp.max(score, axis=0, keepdims=True)
            weight = jnp.exp(score - top).astype(BF16)
            finish(head, queries, dot(s.value[head], weight), s)
            return carry

        return lax.fori_loop(0, HEADS, one_head, carry)

    lax.fori_loop(0, ROWS // QUERY_BLOCK, block, 0)


def scene_columns(scenes, s):
    for start in range(0, ROWS, 128):
        piece = scenes[start // 128 : start // 128 + 1, :].astype(F32)
        s.scene_col[start : start + 128, :] = jnp.transpose(jnp.broadcast_to(piece, (128, 128)))


def mlp_rows(rows, x, gain, s):
    attended = jnp.transpose(s.attended[:, rows])
    middle = (x[rows].astype(F32) + dot(attended, s.w_proj[...])).astype(BF16)
    normed = layer_norm(middle.astype(F32), gain)
    hidden = gelu(dot(normed, s.w_up[...])).astype(BF16)
    s.result[rows] = (middle.astype(F32) + dot(hidden, s.w_down[...])).astype(BF16)


def neighbours(me):
    return lax.rem(me + 1, 128), lax.rem(me + 127, 128)


def note_kernel(me_ref, rank_ref, scenes, same, other, up, down, lines):
    me = me_ref[0]
    above, below = neighbours(me)
    lines[...] = jnp.zeros_like(lines)
    group = lax.broadcasted_iota(jnp.int32, (1, 128), 1) // TILE
    ups = downs = others = jnp.int32(0)
    for tile in range(TILES):
        owner = rank_ref[tile * TILE] // ROWS
        is_up, is_down = owner == above, owner == below
        crosses = ((owner ^ me) & 1 == 1) & jnp.logical_not(is_up | is_down)
        slot = jnp.where(is_up, ups, jnp.where(is_down, downs, 0))
        line = owner // 2 + jnp.where(crosses, CHIPS, 0)
        line = jnp.where(is_up, 2 * CHIPS, jnp.where(is_down, 2 * CHIPS + 1, line))
        line = jnp.where(owner == me, 2 * CHIPS + 2, line)
        row = scenes[tile // 4 : tile // 4 + 1, (tile % 4) * TILE : (tile % 4 + 1) * TILE]
        row = jnp.concatenate([row] * 4, axis=1) + 128 * (tile + 1)
        lines[line] = jnp.where(group == slot, row, lines[line])
        ups, downs = ups + is_up.astype(jnp.int32), downs + is_down.astype(jnp.int32)
        others = others + crosses.astype(jnp.int32)
    same[...] = jnp.where(group[None] == 3, others, lines[0:CHIPS])
    other[...] = lines[CHIPS : 2 * CHIPS]
    up[...] = lines[2 * CHIPS : 2 * CHIPS + 1]
    down[...] = lines[2 * CHIPS + 1 : 2 * CHIPS + 2]


def plan_kernel(
    me_ref, rank_ref, scene_ref, same_ref, other_ref, below_ref, above_ref, same, other, from_below, from_above, scenes,
    plan, scene_out, found, lines,
):
    me = me_ref[0]
    core = lax.rem(me, 2)
    above, below = neighbours(me)
    lines[0:CHIPS] = same[...]
    lines[CHIPS : 2 * CHIPS] = other[...]
    lines[2 * CHIPS : 2 * CHIPS + 1] = from_below[...]
    lines[2 * CHIPS + 1 : 2 * CHIPS + 2] = from_above[...]
    for line in range(ROWS // 128):
        lines[2 * CHIPS + 2 + line] = scenes[line : line + 1]
    one = jnp.int32(1)

    def add(count, line, slot, source, note, last, present):
        found[count] = 4 * line + slot
        plan[count] = jnp.int32(note // 128 - 1)
        plan[STRIDE + count] = source
        plan[2 * STRIDE + count] = note & 127
        plan[3 * STRIDE + count] = last & 127
        return count + present

    def beside(ref, line, source, count):
        for slot in range(MOST_TILES):
            note = ref[0, 0, slot * TILE]
            last = ref[0, 0, slot * TILE + TILE - 1]
            count = add(count, line, slot, source, note, last, jnp.minimum(note, 1))
        return count

    def mine(count):
        def kept(tile, count):
            keeps = (rank_ref[tile * TILE] // ROWS == me).astype(jnp.int32)
            note = scene_ref[tile * TILE] + 128 * (tile + 1)
            last = scene_ref[tile * TILE + TILE - 1]
            return add(count, 2 * CHIPS + 2 + tile // 4, lax.rem(tile, 4), me, note, last, keeps)

        return lax.fori_loop(0, TILES, kept, count)

    def chip(index, count):
        for side in range(2):
            source = 2 * index + side
            own = core == side

            def far(count, source=source, own=own):
                note = jnp.where(own, same_ref[index, 0, 0], other_ref[index, 0, 0])
                last = jnp.where(own, same_ref[index, 0, TILE - 1], other_ref[index, 0, TILE - 1])
                line = index + jnp.where(own, 0, CHIPS)
                return add(count, line, 0, source, note, last, jnp.minimum(note, one))

            kind = jnp.where(source == me, 1, jnp.where(source == below, 2, jnp.where(source == above, 3, 0)))
            count = lax.cond(
                kind == 0,
                far,
                lambda count: lax.cond(
                    kind == 1,
                    mine,
                    lambda count: lax.cond(
                        kind == 2,
                        lambda count: beside(below_ref, 2 * CHIPS, below, count),
                        lambda count: beside(above_ref, 2 * CHIPS + 1, above, count),
                        count,
                    ),
                    count,
                ),
                count,
            )
        return count

    lax.fori_loop(0, CHIPS, chip, jnp.int32(0))
    group = lax.broadcasted_iota(jnp.int32, (1, 128), 1) // TILE
    for index in range(TILES):
        code = found[index]
        row = lines[code // 4] & 127
        moved = pltpu.roll(row, TILE * lax.rem(index % 4 - lax.rem(code, 4) + 4, 4), 1)
        line = slice(index // 4, index // 4 + 1)
        if index % 4 == 0:
            scene_out[line, :] = moved
        else:
            scene_out[line, :] = jnp.where(group == index % 4, moved, scene_out[line, :])


def first_kernel(
    me_ref, rank_ref, x, scenes, gains, w_qkv, w_proj, w_up, w_down,
    send, send_other, up, down, local, *scratch,
):
    s = Scratch(scratch)
    copies = start_weights(0, (w_qkv, w_proj, w_up, w_down), s)
    scene_columns(scenes, s)
    copies[0].wait()
    bound, largest = project(x, gains[0, 0:1], s)
    quick = (bound <= SCORE_LIMIT) & (largest <= VALUE_LIMIT)

    @pl.when(quick)
    def _():
        attend_bounded(ROWS, lambda index: 0, scenes, s)

    @pl.when(jnp.logical_not(quick))
    def _():
        attend_any(scenes, s)

    for copy in copies[1:]:
        copy.wait()
    me = me_ref[0]
    above, below = neighbours(me)
    slots = (jnp.int32(0), jnp.int32(0))
    for start in range(0, ROWS, ROW_BLOCK):
        mlp_rows(slice(start, start + ROW_BLOCK), x, gains[0, 1:2], s)

        def one_tile(tile, slots):
            owner = rank_ref[tile * TILE] // ROWS
            source = s.result.at[pl.ds(pl.multiple_of(tile * TILE, TILE), TILE)]

            def put(target, index):
                place = target.at[pl.ds(pl.multiple_of(index * TILE, TILE), TILE)]
                pltpu.make_async_copy(source, place, s.out_sem).start()

            is_up, is_down, stays = owner == above, owner == below, owner == me

            @pl.when(is_up)
            def _():
                put(up, jnp.minimum(slots[0], MOST_TILES - 1))

            @pl.when(is_down)
            def _():
                put(down, jnp.minimum(slots[1], MOST_TILES - 1))

            @pl.when(stays)
            def _():
                put(local, tile)

            far = jnp.logical_not(is_up | is_down | stays)
            crosses = (owner ^ me) & 1 == 1

            @pl.when(far & jnp.logical_not(crosses))
            def _():
                put(send, owner // 2)

            @pl.when(far & crosses)
            def _():
                put(send_other, owner // 2)

            return (slots[0] + is_up.astype(jnp.int32), slots[1] + is_down.astype(jnp.int32))

        slots = lax.fori_loop(start // TILE, (start + ROW_BLOCK) // TILE, one_tile, slots)
    pltpu.make_async_copy(s.result, local, s.out_sem).wait()


def second_kernel(
    me_ref, plan, scenes, gains, received, received_other, from_below, from_above, local,
    w_qkv, w_proj, w_up, w_down, out, x, in_sem, *scratch,
):
    s = Scratch(scratch)
    me = me_ref[0]
    above, below = neighbours(me)

    def fetch(index, slots):
        owner = plan[STRIDE + index]
        target = x.at[pl.ds(pl.multiple_of(index * TILE, TILE), TILE)]

        def get(source, tile):
            place = source.at[pl.ds(pl.multiple_of(tile * TILE, TILE), TILE)]
            pltpu.make_async_copy(place, target, in_sem).start()

        is_up, is_down, stays = owner == above, owner == below, owner == me

        @pl.when(is_up)
        def _():
            get(from_above, jnp.minimum(slots[0], MOST_TILES - 1))

        @pl.when(is_down)
        def _():
            get(from_below, jnp.minimum(slots[1], MOST_TILES - 1))

        @pl.when(stays)
        def _():
            get(local, plan[index])

        far = jnp.logical_not(is_up | is_down | stays)
        crosses = (owner ^ me) & 1 == 1

        @pl.when(far & jnp.logical_not(crosses))
        def _():
            get(received, owner // 2)

        @pl.when(far & crosses)
        def _():
            get(received_other, owner // 2)

        return (slots[0] + is_up.astype(jnp.int32), slots[1] + is_down.astype(jnp.int32))

    lax.fori_loop(0, TILES, fetch, (jnp.int32(0), jnp.int32(0)))
    copies = start_weights(1, (w_qkv, w_proj, w_up, w_down), s)
    scene_columns(scenes, s)
    pltpu.make_async_copy(local, x, in_sem).wait()
    copies[0].wait()
    bound, largest = project(x, gains[1, 0:1], s)
    quick = (bound <= SCORE_LIMIT) & (largest <= VALUE_LIMIT)

    def window_start(index):
        first = plan[2 * STRIDE + index * (QUERY_BLOCK // TILE)]
        start = jnp.int32(0)
        for piece in range(1, (ROWS - WINDOW) // 128 + 1):
            start = start + (plan[3 * STRIDE + 4 * piece - 1] < first).astype(jnp.int32)
        return pl.multiple_of(start * 128, 128)

    fits = quick
    for index in range(ROWS // QUERY_BLOCK):
        last = plan[3 * STRIDE + (index + 1) * (QUERY_BLOCK // TILE) - 1]
        end = window_start(index) + WINDOW
        after = plan[2 * STRIDE + jnp.minimum(end // TILE, TILES - 1)]
        fits = fits & ((end >= ROWS) | (after > last))

    @pl.when(fits)
    def _():
        attend_bounded(WINDOW, window_start, scenes, s)

    @pl.when(quick & jnp.logical_not(fits))
    def _():
        attend_bounded(ROWS, lambda index: 0, scenes, s)

    @pl.when(jnp.logical_not(quick))
    def _():
        attend_any(scenes, s)

    for copy in copies[1:]:
        copy.wait()
    for start in range(0, ROWS, ROW_BLOCK):
        mlp_rows(slice(start, start + ROW_BLOCK), x, gains[1, 1:2], s)

        def one_tile(index, carry):
            source = s.result.at[pl.ds(pl.multiple_of(index * TILE, TILE), TILE)]
            place = out.at[pl.ds(pl.multiple_of(plan[index] * TILE, TILE), TILE)]
            pltpu.make_async_copy(source, place, s.out_sem).start()
            return carry

        lax.fori_loop(start // TILE, (start + ROW_BLOCK) // TILE, one_tile, 0)
    pltpu.make_async_copy(s.result, out, s.out_sem).wait()


SMEM = pl.BlockSpec(memory_space=pltpu.SMEM)
VMEM = pl.BlockSpec(memory_space=pltpu.VMEM)
HBM = pl.BlockSpec(memory_space=pl.ANY)


def shards(point_feats, scene_id, hilbert_rank, norm_gains, w_qkv, w_proj, w_up, w_down):
    devices = lax.axis_size("seq")
    me = lax.axis_index("seq")
    me_array = me.reshape(1).astype(jnp.int32)
    weights = (w_qkv, w_proj, w_up, w_down)
    scenes = scene_id.reshape(ROWS // 128, 128)
    params = pltpu.CompilerParams(vmem_limit_bytes=VMEM_BYTES)
    rows = jax.ShapeDtypeStruct((ROWS, C), BF16)
    few = jax.ShapeDtypeStruct((MOST_TILES * TILE, C), BF16)
    bins = jax.ShapeDtypeStruct((CHIPS * TILE, C), BF16)
    ring = range(devices)
    to_above = [(i, (i + 1) % devices) for i in ring]
    to_below = [(i, (i - 1) % devices) for i in ring]
    to_other = [(i, i ^ 1) for i in ring]
    cores = [list(range(core, devices, 2)) for core in range(2)]

    def among_chips(array):
        return lax.all_to_all(
            array, "seq", split_axis=0, concat_axis=0, tiled=True, axis_index_groups=cores
        )

    def note(count):
        return jax.ShapeDtypeStruct((count, 1, 128), jnp.int32)

    same, other, note_up, note_down = pl.pallas_call(
        note_kernel,
        in_specs=[SMEM, SMEM, VMEM],
        out_specs=[VMEM] * 4,
        out_shape=[note(CHIPS), note(CHIPS), note(1), note(1)],
        scratch_shapes=[pltpu.VMEM((2 * CHIPS + 3, 1, 128), jnp.int32)],
        compiler_params=params,
        name="notes",
    )(me_array, hilbert_rank, scenes)
    same = among_chips(same)
    note_below = lax.ppermute(note_up, "seq", to_above)
    note_above = lax.ppermute(note_down, "seq", to_below)

    send, send_other, up, down, local = pl.pallas_call(
        first_kernel,
        in_specs=[SMEM, SMEM, VMEM, VMEM, VMEM, HBM, HBM, HBM, HBM],
        out_specs=[HBM] * 5,
        out_shape=[bins, bins, few, few, rows],
        scratch_shapes=scratch_shapes(),
        compiler_params=params,
        name="first_block",
    )(me_array, hilbert_rank, point_feats, scenes, norm_gains, *weights)

    received = among_chips(send)
    from_below = lax.ppermute(up, "seq", to_above)
    from_above = lax.ppermute(down, "seq", to_below)
    crossing = jnp.max(same[:, :, 127], axis=0, keepdims=True)
    crossing = jnp.maximum(crossing, lax.ppermute(crossing, "seq", to_other))[0, 0] > 0

    def make_plan(other):
        return pl.pallas_call(
            plan_kernel,
            in_specs=[SMEM] * 7 + [VMEM] * 5,
            out_specs=[SMEM, VMEM],
            out_shape=[
                jax.ShapeDtypeStruct((4 * STRIDE,), jnp.int32),
                jax.ShapeDtypeStruct((ROWS // 128, 128), jnp.int32),
            ],
            scratch_shapes=[
                pltpu.SMEM((STRIDE,), jnp.int32),
                pltpu.VMEM((2 * CHIPS + 2 + ROWS // 128, 1, 128), jnp.int32),
            ],
            compiler_params=params,
            name="plan",
        )(
            me_array, hilbert_rank, scene_id, same, other, note_below, note_above,
            same, other, note_below, note_above, scenes,
        )

    def second(received, received_other, from_below, from_above, local, plan, scenes):
        return pl.pallas_call(
            second_kernel,
            in_specs=[SMEM, SMEM, VMEM, VMEM] + [HBM] * 9,
            out_specs=HBM,
            out_shape=rows,
            scratch_shapes=[pltpu.VMEM((ROWS, C), BF16), pltpu.SemaphoreType.DMA] + scratch_shapes(),
            compiler_params=params,
            name="second_block",
        )(
            me_array, plan, scenes, norm_gains,
            received, received_other, from_below, from_above, local, *weights,
        )

    def with_crossing(tiles, other, received, from_below, from_above, local, plan, scenes):
        tiles = among_chips(lax.ppermute(tiles, "seq", to_other))
        plan, scenes = make_plan(among_chips(lax.ppermute(other, "seq", to_other)))
        return second(received, tiles, from_below, from_above, local, plan, scenes)

    def without_crossing(tiles, other, received, *rest):
        return second(received, tiles, *rest)

    plan, scenes_sorted = make_plan(jnp.zeros_like(other))
    return lax.cond(
        crossing, with_crossing, without_crossing,
        send_other, other, received, from_below, from_above, local, plan, scenes_sorted,
    )


def solution(mesh):
    placed = (P("seq", None), P("seq"), P("seq"), P(), P(), P(), P(), P())
    return jax.shard_map(
        shards, mesh=mesh, in_specs=placed, out_specs=P("seq", None), check_vma=False
    )
```

```python
import functools

import jax
import jax.numpy as jnp
from jax import lax
from jax.experimental import pallas as pl
from jax.experimental.pallas import tpu as pltpu
from jax.sharding import PartitionSpec as P

C = 256
HEADS = 16
HEAD = 16
ROWS = 1024
FFN = 1024
TILES = 32
TILE = 32
MOST_TILES = 3
CHIPS = 64
NOTE = 8
EPSILON = 1e-05
QUERY_BLOCK = 256
WINDOW = 512
ROW_BLOCK = 256
SPLIT_SCALE = 8.0
SCORE_LIMIT = 40.0
VALUE_LIMIT = 40.0
BF16 = jnp.bfloat16
F32 = jnp.float32
F8 = jnp.float8_e4m3fn
VMEM_BYTES = 56 << 20


def dot(left, right, left_dim=1, right_dim=0):
    return lax.dot_general(
        left, right, (((left_dim,), (right_dim,)), ((), ())), preferred_element_type=F32
    )


def layer_norm(values, gain):
    center = values - jnp.mean(values, axis=-1, keepdims=True)
    spread = jnp.mean(center * center, axis=-1, keepdims=True)
    return (center * lax.rsqrt(spread + EPSILON) * gain).astype(BF16)


def split(values):
    scaled = values.astype(F32) * SPLIT_SCALE
    high = scaled.astype(F8).astype(F32)
    low = scaled - high
    return high, low


def gelu(values):
    return 0.5 * values * (1.0 + lax.erf(values * (0.5**0.5)))


class Scratch:
    names = (
        "w_qkv", "w_proj", "w_up", "w_down", "key", "query", "key_split", "query_split",
        "value", "scene_col", "mask", "attended", "normed", "sems", "out_sem",
    )

    def __init__(self, refs):
        for name, ref in zip(self.names, refs, strict=True):
            setattr(self, name, ref)


def scratch_shapes():
    return [
        pltpu.VMEM((C, 3 * C), BF16),
        pltpu.VMEM((C, C), BF16),
        pltpu.VMEM((C, FFN), BF16),
        pltpu.VMEM((FFN, C), BF16),
        pltpu.VMEM((2, ROWS, 128), BF16),
        pltpu.VMEM((2, 128, ROWS), BF16),
        pltpu.VMEM((HEADS // 2, ROWS, 128), F8),
        pltpu.VMEM((HEADS, 128, ROWS), F8),
        pltpu.VMEM((HEADS, 2 * HEAD, ROWS), BF16),
        pltpu.VMEM((ROWS, 128), F32),
        pltpu.VMEM((ROWS, QUERY_BLOCK), BF16),
        pltpu.VMEM((C, ROWS), BF16),
        pltpu.VMEM((ROWS, C), BF16),
        pltpu.SemaphoreType.DMA((4,)),
        pltpu.SemaphoreType.DMA,
    ]


def start_weights(block, weights, s):
    copies = [
        pltpu.make_async_copy(source.at[block], target, s.sems.at[i])
        for i, (source, target) in enumerate(
            zip(weights, (s.w_qkv, s.w_proj, s.w_up, s.w_down), strict=True)
        )
    ]
    for copy in copies:
        copy.start()
    return copies


def project(x, gain, s):
    for start in range(0, ROWS, ROW_BLOCK):
        rows = slice(start, start + ROW_BLOCK)
        s.normed[rows] = layer_norm(x[rows].astype(F32), gain)
    normed = s.normed[...]
    query = dot(s.w_qkv[:, 0:C], normed, 0, 1).astype(BF16)
    value = dot(s.w_qkv[:, 2 * C : 3 * C], normed, 0, 1).astype(BF16)
    for head in range(HEADS):
        s.value[head, 0:HEAD, :] = value[HEAD * head : HEAD * (head + 1)]
        s.value[head, HEAD:, :] = jnp.ones((HEAD, ROWS), BF16)
    s.query[0] = query[0:128]
    s.query[1] = query[128:256]
    high, low = split(query)
    for head in range(HEADS):
        part = slice(HEAD * head, HEAD * (head + 1))
        both = jnp.concatenate([high[part].astype(BF16), low[part].astype(BF16)], axis=0).astype(F8)
        own, other = 64 * (head % 2), 64 * (1 - head % 2)
        s.query_split[head, own : own + 32, :] = both
        s.query_split[head, own + 32 : own + 64, :] = both
        s.query_split[head, other : other + 64, :] = jnp.zeros((64, ROWS), F8)
    squares = query.astype(F32) * query.astype(F32)
    query_norm = jnp.max(jnp.sum(squares.reshape(HEADS, HEAD, ROWS), axis=1), axis=1, keepdims=True)

    row = lax.broadcasted_iota(jnp.int32, (64, 256), 0)
    lane = lax.broadcasted_iota(jnp.int32, (64, 256), 1)
    same = row == (lane // 64) * HEAD + lane % HEAD
    spread_high = jnp.where(same & (lane % 64 < 32), 1.0, 0.0).astype(BF16)
    spread_low = jnp.where(same & (lane % 64 >= 32), 1.0, 0.0).astype(BF16)
    spread = jnp.concatenate([spread_high, spread_low], axis=0).astype(F8)
    channel = lax.broadcasted_iota(jnp.int32, (C, 128), 0)
    column = lax.broadcasted_iota(jnp.int32, (C, 128), 1)
    head_sum = jnp.where(channel // HEAD == column, 1.0, 0.0).astype(BF16)
    key_norm = jnp.zeros((1, 128), F32)
    highest = jnp.max(jnp.abs(query.astype(F32)))
    key_high = jnp.zeros((1, C), F32)
    for start in range(0, ROWS, ROW_BLOCK):
        rows = slice(start, start + ROW_BLOCK)
        key = dot(s.normed[rows], s.w_qkv[:, C : 2 * C]).astype(BF16)
        s.key[0, rows] = key[:, 0:128]
        s.key[1, rows] = key[:, 128:256]
        wide = key.astype(F32)
        key_high = jnp.maximum(key_high, jnp.max(jnp.abs(wide), axis=0, keepdims=True))
        norms = dot((wide * wide).astype(BF16), head_sum)
        key_norm = jnp.maximum(key_norm, jnp.max(norms, axis=0, keepdims=True))
        high, low = split(key)
        for quarter in range(4):
            lanes = slice(64 * quarter, 64 * quarter + 64)
            pair = jnp.concatenate([high[:, lanes], low[:, lanes]], axis=1).astype(F8)
            expanded = dot(pair, spread).astype(F8)
            s.key_split[2 * quarter, rows] = expanded[:, 0:128]
            s.key_split[2 * quarter + 1, rows] = expanded[:, 128:256]
    largest = jnp.maximum(highest, jnp.max(key_high))
    bound = 0.25 * 1.02 * jnp.sqrt(jnp.max(query_norm) * jnp.max(key_norm))
    return bound, largest


def make_mask(keys, count, index, scenes, s):
    for lane in range(0, QUERY_BLOCK, 128):
        row = scenes[pl.ds(index * (QUERY_BLOCK // 128) + lane // 128, 1), :].astype(F32)
        for start in range(0, count, 128):
            same = s.scene_col[pl.ds(keys + start, 128), :] == row
            s.mask[start : start + 128, lane : lane + 128] = jnp.where(same, 1.0, 0.0).astype(BF16)


def finish(head, queries, output, s):
    start = HEAD * head if isinstance(head, int) else pl.multiple_of(HEAD * head, HEAD)
    s.attended[pl.ds(start, HEAD), queries] = (
        output[0:HEAD] * (1.0 / output[HEAD : HEAD + 1])
    ).astype(BF16)


def attend_bounded(count, first_key, scenes, s):
    def block(index, carry):
        queries = pl.ds(pl.multiple_of(index * QUERY_BLOCK, QUERY_BLOCK), QUERY_BLOCK)
        start = first_key(index)
        keys = pl.ds(start, count)
        make_mask(start, count, index, scenes, s)
        mask = s.mask[0:count]
        for head in range(HEADS):
            score = dot(s.key_split[head // 2, keys, :], s.query_split[head, :, queries])
            weight = jnp.exp(score * (0.25 / SPLIT_SCALE**2)).astype(BF16) * mask
            finish(head, queries, dot(s.value[head, :, keys], weight), s)
        return carry

    lax.fori_loop(0, ROWS // QUERY_BLOCK, block, 0)


def attend_any(scenes, s):
    lane_head = lax.broadcasted_iota(jnp.int32, (1, 128), 1) // HEAD

    def block(index, carry):
        queries = pl.ds(pl.multiple_of(index * QUERY_BLOCK, QUERY_BLOCK), QUERY_BLOCK)
        make_mask(0, ROWS, index, scenes, s)

        def one_head(head, carry):
            group = head // 8
            lanes = jnp.where(lane_head == head % 8, 1.0, 0.0).astype(BF16)
            score = dot(s.key[group] * lanes, s.query[group, :, queries]) * 0.25
            score = jnp.where(s.mask[...] > 0, score, F32(-1e30))
            top = jnp.max(score, axis=0, keepdims=True)
            weight = jnp.exp(score - top).astype(BF16)
            finish(head, queries, dot(s.value[head], weight), s)
            return carry

        return lax.fori_loop(0, HEADS, one_head, carry)

    lax.fori_loop(0, ROWS // QUERY_BLOCK, block, 0)


def scene_columns(scenes, s):
    for start in range(0, ROWS, 128):
        piece = scenes[start // 128 : start // 128 + 1, :].astype(F32)
        s.scene_col[start : start + 128, :] = jnp.transpose(jnp.broadcast_to(piece, (128, 128)))


def mlp_rows(rows, x, gain, s):
    attended = jnp.transpose(s.attended[:, rows])
    middle = (x[rows].astype(F32) + dot(attended, s.w_proj[...])).astype(BF16)
    normed = layer_norm(middle.astype(F32), gain)
    hidden = gelu(dot(normed, s.w_up[...])).astype(BF16)
    return (middle.astype(F32) + dot(hidden, s.w_down[...])).astype(BF16)


def neighbours(me):
    return lax.rem(me + 1, 128), lax.rem(me + 127, 128)


def write_notes(scenes, flag, notes):
    lane = lax.broadcasted_iota(jnp.int32, (1, 128), 1)
    flags = jnp.where(lane == TILE + 1, flag, 0)
    empty = jnp.broadcast_to(flags, (NOTE, 128)).astype(F32).astype(BF16)
    notes.empty[:, :, 0:128] = jnp.broadcast_to(empty[None], (CHIPS, NOTE, 128))
    notes.empty[:, :, 128:256] = jnp.zeros((CHIPS, NOTE, 128), BF16)
    for tile in range(TILES):
        row = scenes[tile // 4 : tile // 4 + 1, (tile % 4) * TILE : (tile % 4 + 1) * TILE]
        row = jnp.concatenate([row] * 4, axis=1)
        row = jnp.where(lane < TILE, row, jnp.where(lane == TILE, tile + 1, flags))
        row = jnp.broadcast_to(row, (NOTE, 128)).astype(F32).astype(BF16)
        notes.result[tile, TILE:, 0:128] = row
        notes.result[tile, TILE:, 128:256] = jnp.zeros((NOTE, 128), BF16)


def sort_tiles(me, entries, plan_out, scene_out):
    count = sum(notes.shape[0] for notes, _, _ in entries)
    total = -(-count // 128) * 128
    tables, sources = [], []
    for notes, first, step in entries:
        tables.append(notes[:, 0:1, :].astype(F32).reshape(notes.shape[0], 128))
        index = lax.broadcasted_iota(jnp.int32, (notes.shape[0], 1), 0)
        sources.append(first + step * index)
    if total > count:
        tables.append(jnp.zeros((total - count, 128), F32))
        sources.append(jnp.zeros((total - count, 1), jnp.int32))
    table = jnp.concatenate(tables, axis=0)
    source = jnp.concatenate(sources, axis=0)
    place = table[:, TILE : TILE + 1]
    far = F32(1 << 20)
    key = jnp.where(place > 0, source.astype(F32) * TILE + place, far)
    wide = jnp.broadcast_to(key, (total, 128))
    row = jnp.concatenate(
        [jnp.transpose(wide[start : start + 128])[0:1] for start in range(0, total, 128)], axis=1
    )
    rank = jnp.sum((key < row).astype(F32), axis=0, keepdims=True)
    rank = jnp.where(row < far, rank, -1.0)
    target = lax.broadcasted_iota(jnp.int32, (TILES, total), 0).astype(F32)
    chosen = jnp.where(rank == target, 1.0, 0.0).astype(BF16)
    lane = lax.broadcasted_iota(jnp.int32, (total, 128), 1)
    entry = lax.broadcasted_iota(jnp.int32, (total, 128), 0)
    table = jnp.where(lane == TILE + 2, entry % 128, jnp.where(lane == TILE + 3, entry // 128, table.astype(jnp.int32)))
    ordered = dot(chosen, table.astype(F32).astype(BF16)).astype(jnp.int32)
    plan_out[...] = ordered
    group = lax.broadcasted_iota(jnp.int32, (1, 128), 1) // TILE
    lines = jnp.zeros((ROWS // 128, 128), jnp.int32)
    for part in range(4):
        piece = plan_out[pl.ds(part, ROWS // 128, stride=4), :]
        piece = pltpu.roll(piece, TILE * part, 1) if part else piece
        lines = jnp.where(group == part, piece, lines)
    scene_out[...] = lines


class Notes:
    def __init__(self, empty, result):
        self.empty, self.result = empty, result


def first_kernel(
    me_ref, flag_ref, rank_ref, x, scenes, gains, w_qkv, w_proj, w_up, w_down,
    send, send_other, up, down, local, empty, result, fill_sem, *scratch,
):
    s = Scratch(scratch)
    copies = start_weights(0, (w_qkv, w_proj, w_up, w_down), s)
    write_notes(scenes, flag_ref[0], Notes(empty, result))
    fills = []
    for index, target in enumerate((send, send_other, up, down, local)):
        count = target.shape[0]
        fills.append(
            pltpu.make_async_copy(
                empty.at[0:count], target.at[:, TILE : TILE + NOTE], fill_sem.at[index]
            )
        )
        fills[-1].start()
    scene_columns(scenes, s)
    copies[0].wait()
    bound, largest = project(x, gains[0, 0:1], s)
    quick = (bound <= SCORE_LIMIT) & (largest <= VALUE_LIMIT)

    @pl.when(quick)
    def _():
        attend_bounded(ROWS, lambda index: 0, scenes, s)

    @pl.when(jnp.logical_not(quick))
    def _():
        attend_any(scenes, s)

    for copy in copies[1:] + fills:
        copy.wait()
    me = me_ref[0]
    above, below = neighbours(me)
    slots = (jnp.int32(0), jnp.int32(0))
    for start in range(0, ROWS, ROW_BLOCK):
        rows = mlp_rows(slice(start, start + ROW_BLOCK), x, gains[0, 1:2], s)
        tiles = slice(start // TILE, (start + ROW_BLOCK) // TILE)
        result[tiles, 0:TILE, :] = rows.reshape(ROW_BLOCK // TILE, TILE, C)

        def one_tile(tile, slots):
            owner = rank_ref[tile * TILE] // ROWS

            def put(target, index):
                pltpu.make_async_copy(result.at[tile], target.at[index], s.out_sem).start()

            is_up, is_down, stays = owner == above, owner == below, owner == me

            @pl.when(is_up)
            def _():
                put(up, jnp.minimum(slots[0], MOST_TILES - 1))

            @pl.when(is_down)
            def _():
                put(down, jnp.minimum(slots[1], MOST_TILES - 1))

            @pl.when(stays)
            def _():
                put(local, tile)

            far = jnp.logical_not(is_up | is_down | stays)
            crosses = (owner ^ me) & 1 == 1

            @pl.when(far & jnp.logical_not(crosses))
            def _():
                put(send, owner // 2)

            @pl.when(far & crosses)
            def _():
                put(send_other, owner // 2)

            return (slots[0] + is_up.astype(jnp.int32), slots[1] + is_down.astype(jnp.int32))

        slots = lax.fori_loop(start // TILE, (start + ROW_BLOCK) // TILE, one_tile, slots)
    pltpu.make_async_copy(result, local, s.out_sem).wait()


def second_kernel(
    me_ref, gains, *refs, sources,
):
    arrays, refs = refs[:sources], refs[sources:]
    w_qkv, w_proj, w_up, w_down, out, x, notes, plan_vmem, scenes, result, plan, note_sems, in_sem = refs[:13]
    s = Scratch(refs[13:])
    me = me_ref[0]
    core = lax.rem(me, 2)
    above, below = neighbours(me)
    firsts = ((core, 2), (1 - core, 2))[: sources - 3] + ((below, 0), (above, 0), (me, 0))
    starts, fetches = [], []
    start = 0
    for index, array in enumerate(arrays):
        count = array.shape[0]
        starts.append(start)
        fetches.append(
            pltpu.make_async_copy(
                array.at[:, TILE : TILE + NOTE, 0:128], notes.at[start : start + count], note_sems.at[index]
            )
        )
        fetches[-1].start()
        start += count
    copies = start_weights(1, (w_qkv, w_proj, w_up, w_down), s)
    for fetch in fetches:
        fetch.wait()
    ends = starts[1:] + [start]
    entries = [(notes[a:b], *first) for a, b, first in zip(starts, ends, firsts, strict=True)]
    sort_tiles(me, entries, plan_vmem, scenes)
    to_scalars = pltpu.make_async_copy(plan_vmem, plan, note_sems.at[0])
    to_scalars.start()
    to_scalars.wait()

    def fetch(index, carry):
        entry = plan[index, TILE + 2] + 128 * plan[index, TILE + 3]
        target = x.at[pl.ds(pl.multiple_of(index * TILE, TILE), TILE)]
        for array, first, end in zip(arrays, starts, ends, strict=True):

            @pl.when((entry >= first) & (entry < end))
            def _(array=array, first=first):
                pltpu.make_async_copy(array.at[entry - first, 0:TILE], target, in_sem).start()

        return carry

    lax.fori_loop(0, TILES, fetch, 0)
    scene_columns(scenes, s)
    pltpu.make_async_copy(result, x, in_sem).wait()
    copies[0].wait()
    bound, largest = project(x, gains[1, 0:1], s)
    quick = (bound <= SCORE_LIMIT) & (largest <= VALUE_LIMIT)

    def window_start(index):
        first = plan[index * (QUERY_BLOCK // TILE), 0]
        start = jnp.int32(0)
        for piece in range(1, (ROWS - WINDOW) // 128 + 1):
            start = start + (plan[4 * piece - 1, TILE - 1] < first).astype(jnp.int32)
        return pl.multiple_of(start * 128, 128)

    fits = quick
    for index in range(ROWS // QUERY_BLOCK):
        last = plan[(index + 1) * (QUERY_BLOCK // TILE) - 1, TILE - 1]
        end = window_start(index) + WINDOW
        after = plan[jnp.minimum(end // TILE, TILES - 1), 0]
        fits = fits & ((end >= ROWS) | (after > last))

    @pl.when(fits)
    def _():
        attend_bounded(WINDOW, window_start, scenes, s)

    @pl.when(quick & jnp.logical_not(fits))
    def _():
        attend_bounded(ROWS, lambda index: 0, scenes, s)

    @pl.when(jnp.logical_not(quick))
    def _():
        attend_any(scenes, s)

    for copy in copies[1:]:
        copy.wait()
    for start in range(0, ROWS, ROW_BLOCK):
        result[start : start + ROW_BLOCK] = mlp_rows(slice(start, start + ROW_BLOCK), x, gains[1, 1:2], s)

        def one_tile(index, carry):
            source = result.at[pl.ds(pl.multiple_of(index * TILE, TILE), TILE)]
            place = jnp.clip(plan[index, TILE] - 1, 0, TILES - 1)
            target = out.at[pl.ds(pl.multiple_of(place * TILE, TILE), TILE)]
            pltpu.make_async_copy(source, target, s.out_sem).start()
            return carry

        lax.fori_loop(start // TILE, (start + ROW_BLOCK) // TILE, one_tile, 0)
    pltpu.make_async_copy(result, out, s.out_sem).wait()


SMEM = pl.BlockSpec(memory_space=pltpu.SMEM)
VMEM = pl.BlockSpec(memory_space=pltpu.VMEM)
HBM = pl.BlockSpec(memory_space=pl.ANY)


def shards(point_feats, scene_id, hilbert_rank, norm_gains, w_qkv, w_proj, w_up, w_down):
    devices = lax.axis_size("seq")
    me = lax.axis_index("seq")
    me_array = me.reshape(1).astype(jnp.int32)
    weights = (w_qkv, w_proj, w_up, w_down)
    scenes = scene_id.reshape(ROWS // 128, 128)
    params = pltpu.CompilerParams(vmem_limit_bytes=VMEM_BYTES)
    rows = jax.ShapeDtypeStruct((ROWS, C), BF16)
    few = jax.ShapeDtypeStruct((MOST_TILES, TILE + NOTE, C), BF16)
    bins = jax.ShapeDtypeStruct((CHIPS, TILE + NOTE, C), BF16)
    own = jax.ShapeDtypeStruct((TILES, TILE + NOTE, C), BF16)
    ring = range(devices)
    to_above = [(i, (i + 1) % devices) for i in ring]
    to_below = [(i, (i - 1) % devices) for i in ring]
    to_other = [(i, i ^ 1) for i in ring]
    cores = [list(range(core, devices, 2)) for core in range(2)]

    def among_chips(array):
        return lax.all_to_all(
            array, "seq", split_axis=0, concat_axis=0, tiled=True, axis_index_groups=cores
        )

    owner = hilbert_rank // ROWS
    beside = (owner == (me + 1) % devices) | (owner == (me + devices - 1) % devices)
    crosses = jnp.max(jnp.where(beside, 0, (owner ^ me) & 1)).reshape(1)
    crosses = jnp.maximum(crosses, lax.ppermute(crosses, "seq", to_other))

    send, send_other, up, down, local = pl.pallas_call(
        first_kernel,
        in_specs=[SMEM, SMEM, SMEM, VMEM, VMEM, VMEM, HBM, HBM, HBM, HBM],
        out_specs=[HBM] * 5,
        out_shape=[bins, bins, few, few, own],
        scratch_shapes=[
            pltpu.VMEM((CHIPS, NOTE, C), BF16),
            pltpu.VMEM((TILES, TILE + NOTE, C), BF16),
            pltpu.SemaphoreType.DMA((5,)),
        ]
        + scratch_shapes(),
        compiler_params=params,
        name="first_block",
    )(me_array, crosses, hilbert_rank, point_feats, scenes, norm_gains, *weights)

    received = among_chips(send)
    from_below = lax.ppermute(up, "seq", to_above)
    from_above = lax.ppermute(down, "seq", to_below)

    def second(*arrays):
        noted = sum(array.shape[0] for array in arrays)
        return pl.pallas_call(
            functools.partial(second_kernel, sources=len(arrays)),
            in_specs=[SMEM, VMEM] + [HBM] * (len(arrays) + 4),
            out_specs=HBM,
            out_shape=rows,
            scratch_shapes=[
                pltpu.VMEM((ROWS, C), BF16),
                pltpu.VMEM((noted, NOTE, 128), BF16),
                pltpu.VMEM((TILES, 128), jnp.int32),
                pltpu.VMEM((ROWS // 128, 128), jnp.int32),
                pltpu.VMEM((ROWS, C), BF16),
                pltpu.SMEM((TILES, 128), jnp.int32),
                pltpu.SemaphoreType.DMA((5,)),
                pltpu.SemaphoreType.DMA,
            ]
            + scratch_shapes(),
            compiler_params=params,
            name="second_block",
        )(me_array, norm_gains, *arrays, *weights)

    def with_crossing(tiles, received, *rest):
        return second(received, among_chips(lax.ppermute(tiles, "seq", to_other)), *rest)

    def without_crossing(tiles, received, *rest):
        return second(received, *rest)

    return lax.cond(
        jnp.max(received[:, TILE, TILE + 1]) > 0, with_crossing, without_crossing,
        send_other, received, from_below, from_above, local,
    )


def solution(mesh):
    placed = (P("seq", None), P("seq"), P("seq"), P(), P(), P(), P(), P())
    return jax.shard_map(
        shards, mesh=mesh, in_specs=placed, out_specs=P("seq", None), check_vma=False
    )
```

```python
import functools
import math

import jax
import jax.numpy as jnp
from jax import lax
from jax.experimental import pallas as pl
from jax.experimental.pallas import tpu as pltpu
from jax.sharding import PartitionSpec as P

C = 256
HEADS = 16
HEAD = 16
ROWS = 1024
FFN = 1024
TILES = 32
TILE = 32
MOST_TILES = 3
CHIPS = 64
NOTE = 8
EPSILON = 1e-05
QUERY_BLOCK = 256
WINDOWS = (384, 512)
ROW_BLOCK = 512
MLP_BLOCK = 1024
SPLIT_SCALE = 8.0
EXPONENT_SCALE = 0.25 / SPLIT_SCALE**2 / math.log(2.0)
SCORE_LIMIT = 40.0
VALUE_LIMIT = 40.0
BF16 = jnp.bfloat16
F32 = jnp.float32
F8 = jnp.float8_e4m3fn
VMEM_BYTES = 56 << 20


def dot(left, right, left_dim=1, right_dim=0):
    return lax.dot_general(
        left, right, (((left_dim,), (right_dim,)), ((), ())), preferred_element_type=F32
    )


def layer_norm(values, gain):
    center = values - jnp.mean(values, axis=-1, keepdims=True)
    spread = jnp.mean(center * center, axis=-1, keepdims=True)
    return (center * lax.rsqrt(spread + EPSILON) * gain).astype(BF16)


def split(values):
    scaled = values.astype(F32) * SPLIT_SCALE
    high = scaled.astype(F8).astype(F32)
    low = scaled - high
    return high, low


def gelu(values):
    return 0.5 * values * (1.0 + lax.erf(values * (0.5**0.5)))


class Scratch:
    names = (
        "w_qkv", "w_proj", "w_up", "w_down", "key", "query", "key_split", "query_split",
        "value", "scene_col", "mask", "attended", "normed", "sems", "out_sem",
    )

    def __init__(self, refs):
        for name, ref in zip(self.names, refs, strict=True):
            setattr(self, name, ref)


def scratch_shapes():
    return [
        pltpu.VMEM((C, 3 * C), BF16),
        pltpu.VMEM((C, C), BF16),
        pltpu.VMEM((C, FFN), BF16),
        pltpu.VMEM((FFN, C), BF16),
        pltpu.VMEM((2, ROWS, 128), BF16),
        pltpu.VMEM((2, 128, ROWS), BF16),
        pltpu.VMEM((HEADS // 2, ROWS, 128), F8),
        pltpu.VMEM((HEADS, 128, ROWS), F8),
        pltpu.VMEM((HEADS, 2 * HEAD, ROWS), BF16),
        pltpu.VMEM((ROWS, 128), F32),
        pltpu.VMEM((ROWS, QUERY_BLOCK), BF16),
        pltpu.VMEM((C, ROWS), BF16),
        pltpu.VMEM((ROWS, C), BF16),
        pltpu.SemaphoreType.DMA((4,)),
        pltpu.SemaphoreType.DMA,
    ]


def start_weights(block, weights, s):
    copies = [
        pltpu.make_async_copy(source.at[block], target, s.sems.at[i])
        for i, (source, target) in enumerate(
            zip(weights, (s.w_qkv, s.w_proj, s.w_up, s.w_down), strict=True)
        )
    ]
    for copy in copies:
        copy.start()
    return copies


def project(x, gain, s):
    for start in range(0, ROWS, ROW_BLOCK):
        rows = slice(start, start + ROW_BLOCK)
        s.normed[rows] = layer_norm(x[rows].astype(F32), gain)
    normed = s.normed[...]
    query = dot(s.w_qkv[:, 0:C], normed, 0, 1).astype(BF16)
    value = dot(s.w_qkv[:, 2 * C : 3 * C], normed, 0, 1).astype(BF16)
    for head in range(HEADS):
        s.value[head, 0:HEAD, :] = value[HEAD * head : HEAD * (head + 1)]
        s.value[head, HEAD:, :] = jnp.ones((HEAD, ROWS), BF16)
    s.query[0] = query[0:128]
    s.query[1] = query[128:256]
    high, low = split(query)
    for head in range(HEADS):
        part = slice(HEAD * head, HEAD * (head + 1))
        both = jnp.concatenate([high[part].astype(BF16), low[part].astype(BF16)], axis=0).astype(F8)
        own, other = 64 * (head % 2), 64 * (1 - head % 2)
        s.query_split[head, own : own + 32, :] = both
        s.query_split[head, own + 32 : own + 64, :] = both
        s.query_split[head, other : other + 64, :] = jnp.zeros((64, ROWS), F8)
    squares = query.astype(F32) * query.astype(F32)
    query_norm = jnp.max(jnp.sum(squares.reshape(HEADS, HEAD, ROWS), axis=1), axis=1, keepdims=True)

    row = lax.broadcasted_iota(jnp.int32, (64, 256), 0)
    lane = lax.broadcasted_iota(jnp.int32, (64, 256), 1)
    same = row == (lane // 64) * HEAD + lane % HEAD
    spread_high = jnp.where(same & (lane % 64 < 32), 1.0, 0.0).astype(BF16)
    spread_low = jnp.where(same & (lane % 64 >= 32), 1.0, 0.0).astype(BF16)
    spread = jnp.concatenate([spread_high, spread_low], axis=0).astype(F8)
    channel = lax.broadcasted_iota(jnp.int32, (C, 128), 0)
    column = lax.broadcasted_iota(jnp.int32, (C, 128), 1)
    head_sum = jnp.where(channel // HEAD == column, 1.0, 0.0).astype(BF16)
    key_norm = jnp.zeros((1, 128), F32)
    highest = jnp.max(jnp.abs(query.astype(F32)))
    key_high = jnp.zeros((1, C), F32)
    for start in range(0, ROWS, ROW_BLOCK):
        rows = slice(start, start + ROW_BLOCK)
        key = dot(s.normed[rows], s.w_qkv[:, C : 2 * C]).astype(BF16)
        s.key[0, rows] = key[:, 0:128]
        s.key[1, rows] = key[:, 128:256]
        wide = key.astype(F32)
        key_high = jnp.maximum(key_high, jnp.max(jnp.abs(wide), axis=0, keepdims=True))
        norms = dot((wide * wide).astype(BF16), head_sum)
        key_norm = jnp.maximum(key_norm, jnp.max(norms, axis=0, keepdims=True))
        high, low = split(key)
        for quarter in range(4):
            lanes = slice(64 * quarter, 64 * quarter + 64)
            pair = jnp.concatenate([high[:, lanes], low[:, lanes]], axis=1).astype(F8)
            expanded = dot(pair, spread).astype(F8)
            s.key_split[2 * quarter, rows] = expanded[:, 0:128]
            s.key_split[2 * quarter + 1, rows] = expanded[:, 128:256]
    largest = jnp.maximum(highest, jnp.max(key_high))
    bound = 0.25 * 1.02 * jnp.sqrt(jnp.max(query_norm) * jnp.max(key_norm))
    return bound, largest


def make_mask(keys, count, index, scenes, s):
    for lane in range(0, QUERY_BLOCK, 128):
        row = scenes[pl.ds(index * (QUERY_BLOCK // 128) + lane // 128, 1), :].astype(F32)
        for start in range(0, count, 128):
            same = s.scene_col[pl.ds(keys + start, 128), :] == row
            s.mask[start : start + 128, lane : lane + 128] = jnp.where(same, 1.0, 0.0).astype(BF16)


def finish(head, queries, output, s):
    start = HEAD * head if isinstance(head, int) else pl.multiple_of(HEAD * head, HEAD)
    s.attended[pl.ds(start, HEAD), queries] = (
        output[0:HEAD] * (1.0 / output[HEAD : HEAD + 1])
    ).astype(BF16)


def attend_bounded(counts, choose, scenes, s):
    def block(index, carry):
        kind, start = choose(index)
        for number, count in enumerate(counts):

            @pl.when(kind == number)
            def _(count=count):
                attend_block(index, start, count, scenes, s)

        return carry

    lax.fori_loop(0, ROWS // QUERY_BLOCK, block, 0)


def attend_block(index, start, count, scenes, s):
    queries = pl.ds(pl.multiple_of(index * QUERY_BLOCK, QUERY_BLOCK), QUERY_BLOCK)
    keys = pl.ds(start, count)
    make_mask(start, count, index, scenes, s)
    mask = s.mask[0:count]
    for head in range(HEADS):
        score = dot(s.key_split[head // 2, keys, :], s.query_split[head, :, queries])
        weight = jnp.exp2(score * EXPONENT_SCALE).astype(BF16) * mask
        finish(head, queries, dot(s.value[head, :, keys], weight), s)


def attend_any(scenes, s):
    lane_head = lax.broadcasted_iota(jnp.int32, (1, 128), 1) // HEAD

    def block(index, carry):
        queries = pl.ds(pl.multiple_of(index * QUERY_BLOCK, QUERY_BLOCK), QUERY_BLOCK)
        make_mask(0, ROWS, index, scenes, s)

        def one_head(head, carry):
            group = head // 8
            lanes = jnp.where(lane_head == head % 8, 1.0, 0.0).astype(BF16)
            score = dot(s.key[group] * lanes, s.query[group, :, queries]) * 0.25
            score = jnp.where(s.mask[...] > 0, score, F32(-1e30))
            top = jnp.max(score, axis=0, keepdims=True)
            weight = jnp.exp(score - top).astype(BF16)
            finish(head, queries, dot(s.value[head], weight), s)
            return carry

        return lax.fori_loop(0, HEADS, one_head, carry)

    lax.fori_loop(0, ROWS // QUERY_BLOCK, block, 0)


def scene_columns(scenes, s):
    for start in range(0, ROWS, 128):
        piece = scenes[start // 128 : start // 128 + 1, :].astype(F32)
        s.scene_col[start : start + 128, :] = jnp.transpose(jnp.broadcast_to(piece, (128, 128)))


def mlp_rows(rows, x, gain, s):
    attended = jnp.transpose(s.attended[:, rows])
    middle = (x[rows].astype(F32) + dot(attended, s.w_proj[...])).astype(BF16)
    normed = layer_norm(middle.astype(F32), gain)
    hidden = gelu(dot(normed, s.w_up[...])).astype(BF16)
    return (middle.astype(F32) + dot(hidden, s.w_down[...])).astype(BF16)


def neighbours(me):
    return lax.rem(me + 1, 128), lax.rem(me + 127, 128)


def crossings(device, rank_ref):
    above, below = neighbours(device)
    flag = jnp.int32(0)
    for tile in range(TILES):
        owner = rank_ref[tile * TILE] >> 10
        crosses = ((owner ^ device) & 1) * ((owner != above) & (owner != below)).astype(jnp.int32)
        flag = flag | crosses
    return flag


def write_notes(scenes, flag, notes):
    lane = lax.broadcasted_iota(jnp.int32, (1, 128), 1)
    flags = jnp.where(lane == TILE + 1, flag, 0)
    empty = jnp.broadcast_to(flags, (NOTE, 128)).astype(F32).astype(BF16)
    notes.empty[:, :, 0:128] = jnp.broadcast_to(empty[None], (CHIPS, NOTE, 128))
    notes.empty[:, :, 128:256] = jnp.zeros((CHIPS, NOTE, 128), BF16)
    for tile in range(TILES):
        row = scenes[tile // 4 : tile // 4 + 1, (tile % 4) * TILE : (tile % 4 + 1) * TILE]
        row = jnp.concatenate([row] * 4, axis=1)
        row = jnp.where(lane < TILE, row, jnp.where(lane == TILE, tile + 1, flags))
        row = jnp.broadcast_to(row, (NOTE, 128)).astype(F32).astype(BF16)
        notes.result[tile, TILE:, 0:128] = row
        notes.result[tile, TILE:, 128:256] = jnp.zeros((NOTE, 128), BF16)


def sort_tiles(me, entries, plan_out, scene_out):
    count = sum(notes.shape[0] for notes, _, _ in entries)
    total = -(-count // 128) * 128
    tables, sources = [], []
    for notes, first, step in entries:
        tables.append(notes[:, 0:1, :].astype(F32).reshape(notes.shape[0], 128))
        index = lax.broadcasted_iota(jnp.int32, (notes.shape[0], 1), 0)
        sources.append(first + step * index)
    if total > count:
        tables.append(jnp.zeros((total - count, 128), F32))
        sources.append(jnp.zeros((total - count, 1), jnp.int32))
    table = jnp.concatenate(tables, axis=0)
    source = jnp.concatenate(sources, axis=0)
    place = table[:, TILE : TILE + 1]
    far = F32(1 << 20)
    key = jnp.where(place > 0, source.astype(F32) * TILE + place, far)
    wide = jnp.broadcast_to(key, (total, 128))
    row = jnp.concatenate(
        [jnp.transpose(wide[start : start + 128])[0:1] for start in range(0, total, 128)], axis=1
    )
    rank = jnp.sum((key < row).astype(F32), axis=0, keepdims=True)
    rank = jnp.where(row < far, rank, -1.0)
    target = lax.broadcasted_iota(jnp.int32, (TILES, total), 0).astype(F32)
    chosen = jnp.where(rank == target, 1.0, 0.0).astype(BF16)
    lane = lax.broadcasted_iota(jnp.int32, (total, 128), 1)
    entry = lax.broadcasted_iota(jnp.int32, (total, 128), 0)
    table = jnp.where(lane == TILE + 2, entry % 128, jnp.where(lane == TILE + 3, entry // 128, table.astype(jnp.int32)))
    ordered = dot(chosen, table.astype(F32).astype(BF16)).astype(jnp.int32)
    plan_out[...] = ordered
    group = lax.broadcasted_iota(jnp.int32, (1, 128), 1) // TILE
    lines = jnp.zeros((ROWS // 128, 128), jnp.int32)
    for part in range(4):
        piece = plan_out[pl.ds(part, ROWS // 128, stride=4), :]
        piece = pltpu.roll(piece, TILE * part, 1) if part else piece
        lines = jnp.where(group == part, piece, lines)
    scene_out[...] = lines


class Notes:
    def __init__(self, empty, result):
        self.empty, self.result = empty, result


def first_kernel(
    me_ref, rank_ref, other_rank_ref, x, scenes, gains, w_qkv, w_proj, w_up, w_down,
    send, send_other, up, down, local, empty, result, fill_sem, *scratch,
):
    s = Scratch(scratch)
    copies = start_weights(0, (w_qkv, w_proj, w_up, w_down), s)
    me = me_ref[0]
    flag = crossings(me, rank_ref) | crossings(me ^ 1, other_rank_ref)
    write_notes(scenes, flag, Notes(empty, result))
    fills = []
    for index, target in enumerate((send, send_other, up, down, local)):
        count = target.shape[0]
        fills.append(
            pltpu.make_async_copy(
                empty.at[0:count], target.at[:, TILE : TILE + NOTE], fill_sem.at[index]
            )
        )
        fills[-1].start()
    scene_columns(scenes, s)
    copies[0].wait()
    bound, largest = project(x, gains[0, 0:1], s)
    quick = (bound <= SCORE_LIMIT) & (largest <= VALUE_LIMIT)

    @pl.when(quick)
    def _():
        attend_bounded((ROWS,), lambda index: (0, 0), scenes, s)

    @pl.when(jnp.logical_not(quick))
    def _():
        attend_any(scenes, s)

    for copy in copies[1:] + fills:
        copy.wait()
    above, below = neighbours(me)
    slots = (jnp.int32(0), jnp.int32(0))
    for start in range(0, ROWS, MLP_BLOCK):
        rows = mlp_rows(slice(start, start + MLP_BLOCK), x, gains[0, 1:2], s)
        tiles = slice(start // TILE, (start + MLP_BLOCK) // TILE)
        result[tiles, 0:TILE, :] = rows.reshape(MLP_BLOCK // TILE, TILE, C)

        def one_tile(tile, slots):
            owner = rank_ref[tile * TILE] >> 10

            def put(target, index):
                pltpu.make_async_copy(result.at[tile], target.at[index], s.out_sem).start()

            is_up, is_down, stays = owner == above, owner == below, owner == me

            @pl.when(is_up)
            def _():
                put(up, jnp.minimum(slots[0], MOST_TILES - 1))

            @pl.when(is_down)
            def _():
                put(down, jnp.minimum(slots[1], MOST_TILES - 1))

            @pl.when(stays)
            def _():
                put(local, tile)

            far = jnp.logical_not(is_up | is_down | stays)
            crosses = (owner ^ me) & 1 == 1

            @pl.when(far & jnp.logical_not(crosses))
            def _():
                put(send, owner // 2)

            @pl.when(far & crosses)
            def _():
                put(send_other, owner // 2)

            return (slots[0] + is_up.astype(jnp.int32), slots[1] + is_down.astype(jnp.int32))

        slots = lax.fori_loop(start // TILE, (start + MLP_BLOCK) // TILE, one_tile, slots)
    pltpu.make_async_copy(result, local, s.out_sem).wait()


def second_kernel(
    me_ref, gains, *refs, sources,
):
    arrays, refs = refs[:sources], refs[sources:]
    w_qkv, w_proj, w_up, w_down, out, x, notes, plan_vmem, scenes, result, plan, note_sems, in_sem = refs[:13]
    s = Scratch(refs[13:])
    me = me_ref[0]
    core = lax.rem(me, 2)
    above, below = neighbours(me)
    firsts = ((core, 2), (1 - core, 2))[: sources - 3] + ((below, 0), (above, 0), (me, 0))
    starts, fetches = [], []
    start = 0
    for index, array in enumerate(arrays):
        count = array.shape[0]
        starts.append(start)
        fetches.append(
            pltpu.make_async_copy(
                array.at[:, TILE : TILE + NOTE, 0:128], notes.at[start : start + count], note_sems.at[index]
            )
        )
        fetches[-1].start()
        start += count
    copies = start_weights(1, (w_qkv, w_proj, w_up, w_down), s)
    for fetch in fetches:
        fetch.wait()
    ends = starts[1:] + [start]
    entries = [(notes[a:b], *first) for a, b, first in zip(starts, ends, firsts, strict=True)]
    sort_tiles(me, entries, plan_vmem, scenes)
    to_scalars = pltpu.make_async_copy(plan_vmem, plan, note_sems.at[0])
    to_scalars.start()
    to_scalars.wait()

    def fetch(index, carry):
        entry = plan[index, TILE + 2] + 128 * plan[index, TILE + 3]
        target = x.at[pl.ds(pl.multiple_of(index * TILE, TILE), TILE)]
        for array, first, end in zip(arrays, starts, ends, strict=True):

            @pl.when((entry >= first) & (entry < end))
            def _(array=array, first=first):
                pltpu.make_async_copy(array.at[entry - first, 0:TILE], target, in_sem).start()

        return carry

    lax.fori_loop(0, TILES, fetch, 0)
    scene_columns(scenes, s)
    pltpu.make_async_copy(result, x, in_sem).wait()
    copies[0].wait()
    bound, largest = project(x, gains[1, 0:1], s)
    quick = (bound <= SCORE_LIMIT) & (largest <= VALUE_LIMIT)

    def window(index, count):
        first = plan[index * (QUERY_BLOCK // TILE), 0]
        last = plan[(index + 1) * (QUERY_BLOCK // TILE) - 1, TILE - 1]
        start = jnp.int32(0)
        for piece in range(1, (ROWS - count) // 128 + 1):
            start = start + (plan[4 * piece - 1, TILE - 1] < first).astype(jnp.int32)
        end = start * 128 + count
        fits = (end >= ROWS) | (plan[jnp.minimum(end // TILE, TILES - 1), 0] > last)
        return pl.multiple_of(start * 128, 128), fits

    def choose(index):
        short, enough = window(index, WINDOWS[0])
        wide, _ = window(index, WINDOWS[1])
        return jnp.where(enough, 0, 1), pl.multiple_of(jnp.where(enough, short, wide), 128)

    fits = quick
    for index in range(ROWS // QUERY_BLOCK):
        fits = fits & window(index, WINDOWS[1])[1]

    @pl.when(fits)
    def _():
        attend_bounded(WINDOWS, choose, scenes, s)

    @pl.when(quick & jnp.logical_not(fits))
    def _():
        attend_bounded((ROWS,), lambda index: (0, 0), scenes, s)

    @pl.when(jnp.logical_not(quick))
    def _():
        attend_any(scenes, s)

    for copy in copies[1:]:
        copy.wait()
    for start in range(0, ROWS, MLP_BLOCK):
        result[start : start + MLP_BLOCK] = mlp_rows(slice(start, start + MLP_BLOCK), x, gains[1, 1:2], s)

        def one_tile(index, carry):
            source = result.at[pl.ds(pl.multiple_of(index * TILE, TILE), TILE)]
            place = jnp.clip(plan[index, TILE] - 1, 0, TILES - 1)
            target = out.at[pl.ds(pl.multiple_of(place * TILE, TILE), TILE)]
            pltpu.make_async_copy(source, target, s.out_sem).start()
            return carry

        lax.fori_loop(start // TILE, (start + MLP_BLOCK) // TILE, one_tile, 0)
    pltpu.make_async_copy(result, out, s.out_sem).wait()


SMEM = pl.BlockSpec(memory_space=pltpu.SMEM)
VMEM = pl.BlockSpec(memory_space=pltpu.VMEM)
HBM = pl.BlockSpec(memory_space=pl.ANY)


def shards(point_feats, scene_id, hilbert_rank, norm_gains, w_qkv, w_proj, w_up, w_down):
    devices = lax.axis_size("seq")
    me = lax.axis_index("seq")
    me_array = me.reshape(1).astype(jnp.int32)
    weights = (w_qkv, w_proj, w_up, w_down)
    scenes = scene_id.reshape(ROWS // 128, 128)
    params = pltpu.CompilerParams(vmem_limit_bytes=VMEM_BYTES)
    rows = jax.ShapeDtypeStruct((ROWS, C), BF16)
    few = jax.ShapeDtypeStruct((MOST_TILES, TILE + NOTE, C), BF16)
    bins = jax.ShapeDtypeStruct((CHIPS, TILE + NOTE, C), BF16)
    own = jax.ShapeDtypeStruct((TILES, TILE + NOTE, C), BF16)
    ring = range(devices)
    to_above = [(i, (i + 1) % devices) for i in ring]
    to_below = [(i, (i - 1) % devices) for i in ring]
    to_other = [(i, i ^ 1) for i in ring]
    cores = [list(range(core, devices, 2)) for core in range(2)]

    def among_chips(array):
        return lax.all_to_all(
            array, "seq", split_axis=0, concat_axis=0, tiled=True, axis_index_groups=cores
        )

    other_rank = lax.ppermute(hilbert_rank, "seq", to_other)

    send, send_other, up, down, local = pl.pallas_call(
        first_kernel,
        in_specs=[SMEM, SMEM, SMEM, VMEM, VMEM, VMEM, HBM, HBM, HBM, HBM],
        out_specs=[HBM] * 5,
        out_shape=[bins, bins, few, few, own],
        scratch_shapes=[
            pltpu.VMEM((CHIPS, NOTE, C), BF16),
            pltpu.VMEM((TILES, TILE + NOTE, C), BF16),
            pltpu.SemaphoreType.DMA((5,)),
        ]
        + scratch_shapes(),
        compiler_params=params,
        name="first_block",
    )(me_array, hilbert_rank, other_rank, point_feats, scenes, norm_gains, *weights)

    received = among_chips(send)
    from_below = lax.ppermute(up, "seq", to_above)
    from_above = lax.ppermute(down, "seq", to_below)

    def second(*arrays):
        noted = sum(array.shape[0] for array in arrays)
        return pl.pallas_call(
            functools.partial(second_kernel, sources=len(arrays)),
            in_specs=[SMEM, VMEM] + [HBM] * (len(arrays) + 4),
            out_specs=pl.BlockSpec(memory_space=pltpu.HBM),
            out_shape=rows,
            scratch_shapes=[
                pltpu.VMEM((ROWS, C), BF16),
                pltpu.VMEM((noted, NOTE, 128), BF16),
                pltpu.VMEM((TILES, 128), jnp.int32),
                pltpu.VMEM((ROWS // 128, 128), jnp.int32),
                pltpu.VMEM((ROWS, C), BF16),
                pltpu.SMEM((TILES, 128), jnp.int32),
                pltpu.SemaphoreType.DMA((5,)),
                pltpu.SemaphoreType.DMA,
            ]
            + scratch_shapes(),
            compiler_params=params,
            name="second_block",
        )(me_array, norm_gains, *arrays, *weights)

    def with_crossing(tiles, received, *rest):
        return second(received, among_chips(lax.ppermute(tiles, "seq", to_other)), *rest)

    def without_crossing(tiles, received, *rest):
        return second(received, *rest)

    return lax.cond(
        jnp.max(received[:, TILE, TILE + 1]) > 0, with_crossing, without_crossing,
        send_other, received, from_below, from_above, local,
    )


def solution(mesh):
    placed = (P("seq", None), P("seq"), P("seq"), P(), P(), P(), P(), P())
    return jax.shard_map(
        shards, mesh=mesh, in_specs=placed, out_specs=P("seq", None), check_vma=False
    )
```

```python
import functools
import math

import jax
import jax.numpy as jnp
from jax import lax
from jax.experimental import pallas as pl
from jax.experimental.pallas import tpu as pltpu
from jax.sharding import PartitionSpec as P

C = 256
HEADS = 16
HEAD = 16
ROWS = 1024
FFN = 1024
TILES = 32
TILE = 32
MOST_TILES = 3
CHIPS = 64
NOTE = 8
EPSILON = 1e-05
QUERY_BLOCK = 256
WINDOWS = (384, 512)
ROW_BLOCK = 512
MLP_BLOCK = 1024
SPLIT_SCALE = 8.0
EXPONENT_SCALE = 0.25 / SPLIT_SCALE**2 / math.log(2.0)
SCORE_LIMIT = 40.0
VALUE_LIMIT = 40.0
BF16 = jnp.bfloat16
F32 = jnp.float32
F8 = jnp.float8_e4m3fn
VMEM_BYTES = 56 << 20


def dot(left, right, left_dim=1, right_dim=0):
    return lax.dot_general(
        left, right, (((left_dim,), (right_dim,)), ((), ())), preferred_element_type=F32
    )


def layer_norm(values, gain):
    center = values - jnp.mean(values, axis=-1, keepdims=True)
    spread = jnp.mean(center * center, axis=-1, keepdims=True)
    return (center * lax.rsqrt(spread + EPSILON) * gain).astype(BF16)


def split(values):
    scaled = values.astype(F32) * SPLIT_SCALE
    high = scaled.astype(F8).astype(F32)
    low = scaled - high
    return high, low


def gelu(values):
    return 0.5 * values * (1.0 + lax.erf(values * (0.5**0.5)))


class Scratch:
    names = (
        "w_qkv", "w_proj", "w_up", "w_down", "key", "query", "key_split", "query_split",
        "value", "scene_col", "mask", "attended", "normed", "sems", "out_sem",
    )

    def __init__(self, refs):
        for name, ref in zip(self.names, refs, strict=True):
            setattr(self, name, ref)


def scratch_shapes():
    return [
        pltpu.VMEM((C, 3 * C), BF16),
        pltpu.VMEM((C, C), BF16),
        pltpu.VMEM((C, FFN), BF16),
        pltpu.VMEM((FFN, C), BF16),
        pltpu.VMEM((2, ROWS, 128), BF16),
        pltpu.VMEM((2, 128, ROWS), BF16),
        pltpu.VMEM((HEADS // 2, ROWS, 128), F8),
        pltpu.VMEM((HEADS, 128, ROWS), F8),
        pltpu.VMEM((HEADS, 2 * HEAD, ROWS), BF16),
        pltpu.VMEM((ROWS, 128), F32),
        pltpu.VMEM((ROWS, QUERY_BLOCK), BF16),
        pltpu.VMEM((C, ROWS), BF16),
        pltpu.VMEM((ROWS, C), BF16),
        pltpu.SemaphoreType.DMA((4,)),
        pltpu.SemaphoreType.DMA,
    ]


def start_weights(block, weights, targets, s):
    copies = [
        pltpu.make_async_copy(source.at[block], target, s.sems.at[i])
        for i, (source, target) in enumerate(zip(weights, targets, strict=True))
    ]
    for copy in copies:
        copy.start()
    return copies


def project(x, gain, w_qkv, s):
    for start in range(0, ROWS, ROW_BLOCK):
        rows = slice(start, start + ROW_BLOCK)
        s.normed[rows] = layer_norm(x[rows].astype(F32), gain)
    normed = s.normed[...]
    query = dot(w_qkv[:, 0:C], normed, 0, 1).astype(BF16)
    value = dot(w_qkv[:, 2 * C : 3 * C], normed, 0, 1).astype(BF16)
    for head in range(HEADS):
        s.value[head, 0:HEAD, :] = value[HEAD * head : HEAD * (head + 1)]
        s.value[head, HEAD:, :] = jnp.ones((HEAD, ROWS), BF16)
    s.query[0] = query[0:128]
    s.query[1] = query[128:256]
    high, low = split(query)
    for head in range(HEADS):
        part = slice(HEAD * head, HEAD * (head + 1))
        both = jnp.concatenate([high[part].astype(BF16), low[part].astype(BF16)], axis=0).astype(F8)
        own, other = 64 * (head % 2), 64 * (1 - head % 2)
        s.query_split[head, own : own + 32, :] = both
        s.query_split[head, own + 32 : own + 64, :] = both
        s.query_split[head, other : other + 64, :] = jnp.zeros((64, ROWS), F8)
    squares = query.astype(F32) * query.astype(F32)
    query_norm = jnp.max(jnp.sum(squares.reshape(HEADS, HEAD, ROWS), axis=1), axis=1, keepdims=True)

    row = lax.broadcasted_iota(jnp.int32, (64, 256), 0)
    lane = lax.broadcasted_iota(jnp.int32, (64, 256), 1)
    same = row == (lane // 64) * HEAD + lane % HEAD
    spread_high = jnp.where(same & (lane % 64 < 32), 1.0, 0.0).astype(BF16)
    spread_low = jnp.where(same & (lane % 64 >= 32), 1.0, 0.0).astype(BF16)
    spread = jnp.concatenate([spread_high, spread_low], axis=0).astype(F8)
    channel = lax.broadcasted_iota(jnp.int32, (C, 128), 0)
    column = lax.broadcasted_iota(jnp.int32, (C, 128), 1)
    head_sum = jnp.where(channel // HEAD == column, 1.0, 0.0).astype(BF16)
    key_norm = jnp.zeros((1, 128), F32)
    highest = jnp.max(jnp.abs(query.astype(F32)))
    key_high = jnp.zeros((1, C), F32)
    for start in range(0, ROWS, ROW_BLOCK):
        rows = slice(start, start + ROW_BLOCK)
        key = dot(s.normed[rows], w_qkv[:, C : 2 * C]).astype(BF16)
        s.key[0, rows] = key[:, 0:128]
        s.key[1, rows] = key[:, 128:256]
        wide = key.astype(F32)
        key_high = jnp.maximum(key_high, jnp.max(jnp.abs(wide), axis=0, keepdims=True))
        norms = dot((wide * wide).astype(BF16), head_sum)
        key_norm = jnp.maximum(key_norm, jnp.max(norms, axis=0, keepdims=True))
        high, low = split(key)
        for quarter in range(4):
            lanes = slice(64 * quarter, 64 * quarter + 64)
            pair = jnp.concatenate([high[:, lanes], low[:, lanes]], axis=1).astype(F8)
            expanded = dot(pair, spread).astype(F8)
            s.key_split[2 * quarter, rows] = expanded[:, 0:128]
            s.key_split[2 * quarter + 1, rows] = expanded[:, 128:256]
    largest = jnp.maximum(highest, jnp.max(key_high))
    bound = 0.25 * 1.02 * jnp.sqrt(jnp.max(query_norm) * jnp.max(key_norm))
    return bound, largest


def make_mask(keys, count, index, scenes, s):
    for lane in range(0, QUERY_BLOCK, 128):
        row = scenes[pl.ds(index * (QUERY_BLOCK // 128) + lane // 128, 1), :].astype(F32)
        for start in range(0, count, 128):
            same = s.scene_col[pl.ds(keys + start, 128), :] == row
            s.mask[start : start + 128, lane : lane + 128] = jnp.where(same, 1.0, 0.0).astype(BF16)


def finish(head, queries, output, s):
    start = HEAD * head if isinstance(head, int) else pl.multiple_of(HEAD * head, HEAD)
    s.attended[pl.ds(start, HEAD), queries] = (
        output[0:HEAD] * (1.0 / output[HEAD : HEAD + 1])
    ).astype(BF16)


def attend_bounded(counts, choose, scenes, s):
    def block(index, carry):
        kind, start = choose(index)
        for number, count in enumerate(counts):

            @pl.when(kind == number)
            def _(count=count):
                attend_block(index, start, count, scenes, s)

        return carry

    lax.fori_loop(0, ROWS // QUERY_BLOCK, block, 0)


def attend_block(index, start, count, scenes, s):
    queries = pl.ds(pl.multiple_of(index * QUERY_BLOCK, QUERY_BLOCK), QUERY_BLOCK)
    keys = pl.ds(start, count)
    make_mask(start, count, index, scenes, s)
    mask = s.mask[0:count]
    for head in range(HEADS):
        score = dot(s.key_split[head // 2, keys, :], s.query_split[head, :, queries])
        weight = jnp.exp2(score * EXPONENT_SCALE).astype(BF16) * mask
        finish(head, queries, dot(s.value[head, :, keys], weight), s)


def attend_any(scenes, s):
    lane_head = lax.broadcasted_iota(jnp.int32, (1, 128), 1) // HEAD

    def block(index, carry):
        queries = pl.ds(pl.multiple_of(index * QUERY_BLOCK, QUERY_BLOCK), QUERY_BLOCK)
        make_mask(0, ROWS, index, scenes, s)

        def one_head(head, carry):
            group = head // 8
            lanes = jnp.where(lane_head == head % 8, 1.0, 0.0).astype(BF16)
            score = dot(s.key[group] * lanes, s.query[group, :, queries]) * 0.25
            score = jnp.where(s.mask[...] > 0, score, F32(-1e30))
            top = jnp.max(score, axis=0, keepdims=True)
            weight = jnp.exp(score - top).astype(BF16)
            finish(head, queries, dot(s.value[head], weight), s)
            return carry

        return lax.fori_loop(0, HEADS, one_head, carry)

    lax.fori_loop(0, ROWS // QUERY_BLOCK, block, 0)


def scene_columns(scenes, s):
    for start in range(0, ROWS, 128):
        piece = scenes[start // 128 : start // 128 + 1, :].astype(F32)
        s.scene_col[start : start + 128, :] = jnp.transpose(jnp.broadcast_to(piece, (128, 128)))


def mlp_rows(rows, x, gain, s):
    attended = jnp.transpose(s.attended[:, rows])
    middle = (x[rows].astype(F32) + dot(attended, s.w_proj[...])).astype(BF16)
    normed = layer_norm(middle.astype(F32), gain)
    hidden = gelu(dot(normed, s.w_up[...])).astype(BF16)
    return (middle.astype(F32) + dot(hidden, s.w_down[...])).astype(BF16)


def neighbours(me):
    return lax.rem(me + 1, 128), lax.rem(me + 127, 128)


def crossings(device, rank_ref):
    above, below = neighbours(device)
    flag = jnp.int32(0)
    for tile in range(TILES):
        owner = rank_ref[tile * TILE] >> 10
        crosses = ((owner ^ device) & 1) * ((owner != above) & (owner != below)).astype(jnp.int32)
        flag = flag | crosses
    return flag


def write_notes(scenes, flag, notes):
    lane = lax.broadcasted_iota(jnp.int32, (1, 128), 1)
    flags = jnp.where(lane == TILE + 1, flag, 0)
    empty = jnp.broadcast_to(flags, (NOTE, 128)).astype(F32).astype(BF16)
    notes.empty[:, :, 0:128] = jnp.broadcast_to(empty[None], (CHIPS, NOTE, 128))
    notes.empty[:, :, 128:256] = jnp.zeros((CHIPS, NOTE, 128), BF16)
    for tile in range(TILES):
        row = scenes[tile // 4 : tile // 4 + 1, (tile % 4) * TILE : (tile % 4 + 1) * TILE]
        row = jnp.concatenate([row] * 4, axis=1)
        row = jnp.where(lane < TILE, row, jnp.where(lane == TILE, tile + 1, flags))
        row = jnp.broadcast_to(row, (NOTE, 128)).astype(F32).astype(BF16)
        notes.result[tile, TILE:, 0:128] = row
        notes.result[tile, TILE:, 128:256] = jnp.zeros((NOTE, 128), BF16)


def sort_tiles(me, entries, plan_out, scene_out):
    count = sum(notes.shape[0] for notes, _, _ in entries)
    total = -(-count // 128) * 128
    tables, sources = [], []
    for notes, first, step in entries:
        tables.append(notes[:, 0:1, :].astype(F32).reshape(notes.shape[0], 128))
        index = lax.broadcasted_iota(jnp.int32, (notes.shape[0], 1), 0)
        sources.append(first + step * index)
    if total > count:
        tables.append(jnp.zeros((total - count, 128), F32))
        sources.append(jnp.zeros((total - count, 1), jnp.int32))
    table = jnp.concatenate(tables, axis=0)
    source = jnp.concatenate(sources, axis=0)
    place = table[:, TILE : TILE + 1]
    far = F32(1 << 20)
    key = jnp.where(place > 0, source.astype(F32) * TILE + place, far)
    wide = jnp.broadcast_to(key, (total, 128))
    row = jnp.concatenate(
        [jnp.transpose(wide[start : start + 128])[0:1] for start in range(0, total, 128)], axis=1
    )
    rank = jnp.sum((key < row).astype(F32), axis=0, keepdims=True)
    rank = jnp.where(row < far, rank, -1.0)
    target = lax.broadcasted_iota(jnp.int32, (TILES, total), 0).astype(F32)
    chosen = jnp.where(rank == target, 1.0, 0.0).astype(BF16)
    lane = lax.broadcasted_iota(jnp.int32, (total, 128), 1)
    entry = lax.broadcasted_iota(jnp.int32, (total, 128), 0)
    table = jnp.where(lane == TILE + 2, entry % 128, jnp.where(lane == TILE + 3, entry // 128, table.astype(jnp.int32)))
    ordered = dot(chosen, table.astype(F32).astype(BF16)).astype(jnp.int32)
    plan_out[...] = ordered
    group = lax.broadcasted_iota(jnp.int32, (1, 128), 1) // TILE
    lines = jnp.zeros((ROWS // 128, 128), jnp.int32)
    for part in range(4):
        piece = plan_out[pl.ds(part, ROWS // 128, stride=4), :]
        piece = pltpu.roll(piece, TILE * part, 1) if part else piece
        lines = jnp.where(group == part, piece, lines)
    scene_out[...] = lines


class Notes:
    def __init__(self, empty, result):
        self.empty, self.result = empty, result


def first_kernel(
    me_ref, rank_ref, x, scenes, gains, w_qkv, w_proj, w_up, w_down,
    send, send_other, up, down, local, empty, result, fill_sem, *scratch,
):
    s = Scratch(scratch)
    copies = start_weights(0, (w_proj, w_up, w_down), (s.w_proj, s.w_up, s.w_down), s)
    me = me_ref[0]
    write_notes(scenes, crossings(me, rank_ref), Notes(empty, result))
    fills = []
    for index, target in enumerate((send, send_other, up, down, local)):
        count = target.shape[0]
        fills.append(
            pltpu.make_async_copy(
                empty.at[0:count], target.at[:, TILE : TILE + NOTE], fill_sem.at[index]
            )
        )
        fills[-1].start()
    scene_columns(scenes, s)
    bound, largest = project(x, gains[0, 0:1], w_qkv.at[0], s)
    quick = (bound <= SCORE_LIMIT) & (largest <= VALUE_LIMIT)

    @pl.when(quick)
    def _():
        attend_bounded((ROWS,), lambda index: (0, 0), scenes, s)

    @pl.when(jnp.logical_not(quick))
    def _():
        attend_any(scenes, s)

    for copy in copies + fills:
        copy.wait()
    above, below = neighbours(me)
    slots = (jnp.int32(0), jnp.int32(0))
    for start in range(0, ROWS, MLP_BLOCK):
        rows = mlp_rows(slice(start, start + MLP_BLOCK), x, gains[0, 1:2], s)
        tiles = slice(start // TILE, (start + MLP_BLOCK) // TILE)
        result[tiles, 0:TILE, :] = rows.reshape(MLP_BLOCK // TILE, TILE, C)

        def one_tile(tile, slots):
            owner = rank_ref[tile * TILE] >> 10

            def put(target, index):
                pltpu.make_async_copy(result.at[tile], target.at[index], s.out_sem).start()

            is_up, is_down, stays = owner == above, owner == below, owner == me

            @pl.when(is_up)
            def _():
                put(up, jnp.minimum(slots[0], MOST_TILES - 1))

            @pl.when(is_down)
            def _():
                put(down, jnp.minimum(slots[1], MOST_TILES - 1))

            @pl.when(stays)
            def _():
                put(local, tile)

            far = jnp.logical_not(is_up | is_down | stays)
            crosses = (owner ^ me) & 1 == 1

            @pl.when(far & jnp.logical_not(crosses))
            def _():
                put(send, owner // 2)

            @pl.when(far & crosses)
            def _():
                put(send_other, owner // 2)

            return (slots[0] + is_up.astype(jnp.int32), slots[1] + is_down.astype(jnp.int32))

        slots = lax.fori_loop(start // TILE, (start + MLP_BLOCK) // TILE, one_tile, slots)
    pltpu.make_async_copy(result, local, s.out_sem).wait()


def second_kernel(
    me_ref, gains, *refs, sources,
):
    arrays, refs = refs[:sources], refs[sources:]
    w_qkv, w_proj, w_up, w_down, out, x, notes, plan_vmem, scenes, result, plan, note_sems, in_sem = refs[:13]
    s = Scratch(refs[13:])
    me = me_ref[0]
    core = lax.rem(me, 2)
    above, below = neighbours(me)
    firsts = ((core, 2), (1 - core, 2))[: sources - 3] + ((below, 0), (above, 0), (me, 0))
    starts, fetches = [], []
    start = 0
    for index, array in enumerate(arrays):
        count = array.shape[0]
        starts.append(start)
        fetches.append(
            pltpu.make_async_copy(
                array.at[:, TILE : TILE + NOTE, 0:128], notes.at[start : start + count], note_sems.at[index]
            )
        )
        fetches[-1].start()
        start += count
    copies = start_weights(
        1, (w_qkv, w_proj, w_up, w_down), (s.w_qkv, s.w_proj, s.w_up, s.w_down), s
    )
    for fetch in fetches:
        fetch.wait()
    ends = starts[1:] + [start]
    entries = [(notes[a:b], *first) for a, b, first in zip(starts, ends, firsts, strict=True)]
    sort_tiles(me, entries, plan_vmem, scenes)
    to_scalars = pltpu.make_async_copy(plan_vmem, plan, note_sems.at[0])
    to_scalars.start()
    to_scalars.wait()

    def fetch(index, carry):
        entry = plan[index, TILE + 2] + 128 * plan[index, TILE + 3]
        target = x.at[pl.ds(pl.multiple_of(index * TILE, TILE), TILE)]
        for array, first, end in zip(arrays, starts, ends, strict=True):

            @pl.when((entry >= first) & (entry < end))
            def _(array=array, first=first):
                pltpu.make_async_copy(array.at[entry - first, 0:TILE], target, in_sem).start()

        return carry

    lax.fori_loop(0, TILES, fetch, 0)
    scene_columns(scenes, s)
    pltpu.make_async_copy(result, x, in_sem).wait()
    copies[0].wait()
    bound, largest = project(x, gains[1, 0:1], s.w_qkv, s)
    quick = (bound <= SCORE_LIMIT) & (largest <= VALUE_LIMIT)

    def window(index, count):
        first = plan[index * (QUERY_BLOCK // TILE), 0]
        last = plan[(index + 1) * (QUERY_BLOCK // TILE) - 1, TILE - 1]
        start = jnp.int32(0)
        for piece in range(1, (ROWS - count) // 128 + 1):
            start = start + (plan[4 * piece - 1, TILE - 1] < first).astype(jnp.int32)
        end = start * 128 + count
        fits = (end >= ROWS) | (plan[jnp.minimum(end // TILE, TILES - 1), 0] > last)
        return pl.multiple_of(start * 128, 128), fits

    def choose(index):
        short, enough = window(index, WINDOWS[0])
        wide, _ = window(index, WINDOWS[1])
        return jnp.where(enough, 0, 1), pl.multiple_of(jnp.where(enough, short, wide), 128)

    fits = quick
    for index in range(ROWS // QUERY_BLOCK):
        fits = fits & window(index, WINDOWS[1])[1]

    @pl.when(fits)
    def _():
        attend_bounded(WINDOWS, choose, scenes, s)

    @pl.when(quick & jnp.logical_not(fits))
    def _():
        attend_bounded((ROWS,), lambda index: (0, 0), scenes, s)

    @pl.when(jnp.logical_not(quick))
    def _():
        attend_any(scenes, s)

    for copy in copies[1:]:
        copy.wait()
    for start in range(0, ROWS, MLP_BLOCK):
        result[start : start + MLP_BLOCK] = mlp_rows(slice(start, start + MLP_BLOCK), x, gains[1, 1:2], s)

        def one_tile(index, carry):
            source = result.at[pl.ds(pl.multiple_of(index * TILE, TILE), TILE)]
            place = jnp.clip(plan[index, TILE] - 1, 0, TILES - 1)
            target = out.at[pl.ds(pl.multiple_of(place * TILE, TILE), TILE)]
            pltpu.make_async_copy(source, target, s.out_sem).start()
            return carry

        lax.fori_loop(start // TILE, (start + MLP_BLOCK) // TILE, one_tile, 0)
    pltpu.make_async_copy(result, out, s.out_sem).wait()


SMEM = pl.BlockSpec(memory_space=pltpu.SMEM)
VMEM = pl.BlockSpec(memory_space=pltpu.VMEM)
HBM = pl.BlockSpec(memory_space=pl.ANY)


def shards(point_feats, scene_id, hilbert_rank, norm_gains, w_qkv, w_proj, w_up, w_down):
    devices = lax.axis_size("seq")
    me = lax.axis_index("seq")
    me_array = me.reshape(1).astype(jnp.int32)
    weights = (w_qkv, w_proj, w_up, w_down)
    scenes = scene_id.reshape(ROWS // 128, 128)
    params = pltpu.CompilerParams(vmem_limit_bytes=VMEM_BYTES)
    rows = jax.ShapeDtypeStruct((ROWS, C), BF16)
    few = jax.ShapeDtypeStruct((MOST_TILES, TILE + NOTE, C), BF16)
    bins = jax.ShapeDtypeStruct((CHIPS, TILE + NOTE, C), BF16)
    own = jax.ShapeDtypeStruct((TILES, TILE + NOTE, C), BF16)
    ring = range(devices)
    to_above = [(i, (i + 1) % devices) for i in ring]
    to_below = [(i, (i - 1) % devices) for i in ring]
    to_other = [(i, i ^ 1) for i in ring]
    cores = [list(range(core, devices, 2)) for core in range(2)]

    def among_chips(array):
        return lax.all_to_all(
            array, "seq", split_axis=0, concat_axis=0, tiled=True, axis_index_groups=cores
        )

    send, send_other, up, down, local = pl.pallas_call(
        first_kernel,
        in_specs=[SMEM, SMEM, VMEM, VMEM, VMEM, VMEM, HBM, HBM, HBM],
        out_specs=[HBM] * 5,
        out_shape=[bins, bins, few, few, own],
        scratch_shapes=[
            pltpu.VMEM((CHIPS, NOTE, C), BF16),
            pltpu.VMEM((TILES, TILE + NOTE, C), BF16),
            pltpu.SemaphoreType.DMA((5,)),
        ]
        + scratch_shapes(),
        compiler_params=params,
        name="first_block",
    )(me_array, hilbert_rank, point_feats, scenes, norm_gains, *weights)

    received = among_chips(send)
    from_below = lax.ppermute(up, "seq", to_above)
    from_above = lax.ppermute(down, "seq", to_below)

    def second(*arrays):
        noted = sum(array.shape[0] for array in arrays)
        return pl.pallas_call(
            functools.partial(second_kernel, sources=len(arrays)),
            in_specs=[SMEM, VMEM] + [HBM] * (len(arrays) + 4),
            out_specs=HBM,
            out_shape=pltpu.HBM((ROWS, C), BF16),
            scratch_shapes=[
                pltpu.VMEM((ROWS, C), BF16),
                pltpu.VMEM((noted, NOTE, 128), BF16),
                pltpu.VMEM((TILES, 128), jnp.int32),
                pltpu.VMEM((ROWS // 128, 128), jnp.int32),
                pltpu.VMEM((ROWS, C), BF16),
                pltpu.SMEM((TILES, 128), jnp.int32),
                pltpu.SemaphoreType.DMA((5,)),
                pltpu.SemaphoreType.DMA,
            ]
            + scratch_shapes(),
            compiler_params=params,
            name="second_block",
        )(me_array, norm_gains, *arrays, *weights)

    crossing = jnp.max(received[:, TILE, TILE + 1].astype(jnp.int32)).reshape(1)
    crossing_other = lax.ppermute(crossing, "seq", to_other)
    out = second(received, from_below, from_above, local)

    def with_crossing(out, tiles, received, *rest):
        return second(received, among_chips(lax.ppermute(tiles, "seq", to_other)), *rest)

    def without_crossing(out, *rest):
        return out

    return lax.cond(
        jnp.maximum(crossing, crossing_other)[0] > 0, with_crossing, without_crossing,
        out, send_other, received, from_below, from_above, local,
    )


def solution(mesh):
    placed = (P("seq", None), P("seq"), P("seq"), P(), P(), P(), P(), P())
    return jax.shard_map(
        shards, mesh=mesh, in_specs=placed, out_specs=P("seq", None), check_vma=False
    )
```

```python
import functools
import math

import jax
import jax.numpy as jnp
from jax import lax
from jax.experimental import pallas as pl
from jax.experimental.pallas import tpu as pltpu
from jax.sharding import PartitionSpec as P

C = 256
HEADS = 16
HEAD = 16
ROWS = 1024
FFN = 1024
TILES = 32
TILE = 32
MOST_TILES = 3
CHIPS = 64
GROUPS = 4
GROUP_ROWS = TILE // GROUPS
NOTE = GROUPS * C
LANES = NOTE + 128
EPSILON = 1e-05
QUERY_BLOCK = 256
WINDOWS = (384, 512)
ROW_BLOCK = 512
MLP_BLOCK = 1024
SPLIT_SCALE = 8.0
EXPONENT_SCALE = 0.25 / SPLIT_SCALE**2 / math.log(2.0)
SCORE_LIMIT = 40.0
VALUE_LIMIT = 40.0
BF16 = jnp.bfloat16
F32 = jnp.float32
F8 = jnp.float8_e4m3fn
VMEM_BYTES = 56 << 20


def dot(left, right, left_dim=1, right_dim=0):
    return lax.dot_general(
        left, right, (((left_dim,), (right_dim,)), ((), ())), preferred_element_type=F32
    )


def layer_norm(values, gain):
    center = values - jnp.mean(values, axis=-1, keepdims=True)
    spread = jnp.mean(center * center, axis=-1, keepdims=True)
    return (center * lax.rsqrt(spread + EPSILON) * gain).astype(BF16)


def split(values):
    scaled = values.astype(F32) * SPLIT_SCALE
    high = scaled.astype(F8).astype(F32)
    low = scaled - high
    return high, low


def gelu(values):
    return 0.5 * values * (1.0 + lax.erf(values * (0.5**0.5)))


class Scratch:
    names = (
        "w_qkv", "w_proj", "w_up", "w_down", "key", "query", "key_split", "query_split",
        "value", "scene_col", "mask", "attended", "normed", "sems", "out_sem",
    )

    def __init__(self, refs):
        for name, ref in zip(self.names, refs, strict=True):
            setattr(self, name, ref)


def scratch_shapes():
    return [
        pltpu.VMEM((C, 3 * C), BF16),
        pltpu.VMEM((C, C), BF16),
        pltpu.VMEM((C, FFN), BF16),
        pltpu.VMEM((FFN, C), BF16),
        pltpu.VMEM((2, ROWS, 128), BF16),
        pltpu.VMEM((2, 128, ROWS), BF16),
        pltpu.VMEM((HEADS // 2, ROWS, 128), F8),
        pltpu.VMEM((HEADS, 128, ROWS), F8),
        pltpu.VMEM((HEADS, 2 * HEAD, ROWS), BF16),
        pltpu.VMEM((ROWS, 128), F32),
        pltpu.VMEM((ROWS, QUERY_BLOCK), BF16),
        pltpu.VMEM((C, ROWS), BF16),
        pltpu.VMEM((ROWS, C), BF16),
        pltpu.SemaphoreType.DMA((4,)),
        pltpu.SemaphoreType.DMA,
    ]


def start_weights(block, weights, targets, s):
    copies = [
        pltpu.make_async_copy(source.at[block], target, s.sems.at[i])
        for i, (source, target) in enumerate(zip(weights, targets, strict=True))
    ]
    for copy in copies:
        copy.start()
    return copies


def project(x, gain, w_qkv, s):
    for start in range(0, ROWS, ROW_BLOCK):
        rows = slice(start, start + ROW_BLOCK)
        s.normed[rows] = layer_norm(x[rows].astype(F32), gain)
    normed = s.normed[...]
    query = dot(w_qkv[:, 0:C], normed, 0, 1).astype(BF16)
    value = dot(w_qkv[:, 2 * C : 3 * C], normed, 0, 1).astype(BF16)
    for head in range(HEADS):
        s.value[head, 0:HEAD, :] = value[HEAD * head : HEAD * (head + 1)]
        s.value[head, HEAD:, :] = jnp.ones((HEAD, ROWS), BF16)
    s.query[0] = query[0:128]
    s.query[1] = query[128:256]
    high, low = split(query)
    for head in range(HEADS):
        part = slice(HEAD * head, HEAD * (head + 1))
        both = jnp.concatenate([high[part].astype(BF16), low[part].astype(BF16)], axis=0).astype(F8)
        own, other = 64 * (head % 2), 64 * (1 - head % 2)
        s.query_split[head, own : own + 32, :] = both
        s.query_split[head, own + 32 : own + 64, :] = both
        s.query_split[head, other : other + 64, :] = jnp.zeros((64, ROWS), F8)
    squares = query.astype(F32) * query.astype(F32)
    query_norm = jnp.max(jnp.sum(squares.reshape(HEADS, HEAD, ROWS), axis=1), axis=1, keepdims=True)

    row = lax.broadcasted_iota(jnp.int32, (64, 256), 0)
    lane = lax.broadcasted_iota(jnp.int32, (64, 256), 1)
    same = row == (lane // 64) * HEAD + lane % HEAD
    spread_high = jnp.where(same & (lane % 64 < 32), 1.0, 0.0).astype(BF16)
    spread_low = jnp.where(same & (lane % 64 >= 32), 1.0, 0.0).astype(BF16)
    spread = jnp.concatenate([spread_high, spread_low], axis=0).astype(F8)
    channel = lax.broadcasted_iota(jnp.int32, (C, 128), 0)
    column = lax.broadcasted_iota(jnp.int32, (C, 128), 1)
    head_sum = jnp.where(channel // HEAD == column, 1.0, 0.0).astype(BF16)
    key_norm = jnp.zeros((1, 128), F32)
    highest = jnp.max(jnp.abs(query.astype(F32)))
    key_high = jnp.zeros((1, C), F32)
    for start in range(0, ROWS, ROW_BLOCK):
        rows = slice(start, start + ROW_BLOCK)
        key = dot(s.normed[rows], w_qkv[:, C : 2 * C]).astype(BF16)
        s.key[0, rows] = key[:, 0:128]
        s.key[1, rows] = key[:, 128:256]
        wide = key.astype(F32)
        key_high = jnp.maximum(key_high, jnp.max(jnp.abs(wide), axis=0, keepdims=True))
        norms = dot((wide * wide).astype(BF16), head_sum)
        key_norm = jnp.maximum(key_norm, jnp.max(norms, axis=0, keepdims=True))
        high, low = split(key)
        for quarter in range(4):
            lanes = slice(64 * quarter, 64 * quarter + 64)
            pair = jnp.concatenate([high[:, lanes], low[:, lanes]], axis=1).astype(F8)
            expanded = dot(pair, spread).astype(F8)
            s.key_split[2 * quarter, rows] = expanded[:, 0:128]
            s.key_split[2 * quarter + 1, rows] = expanded[:, 128:256]
    largest = jnp.maximum(highest, jnp.max(key_high))
    bound = 0.25 * 1.02 * jnp.sqrt(jnp.max(query_norm) * jnp.max(key_norm))
    return bound, largest


def make_mask(keys, count, index, scenes, s):
    for lane in range(0, QUERY_BLOCK, 128):
        row = scenes[pl.ds(index * (QUERY_BLOCK // 128) + lane // 128, 1), :].astype(F32)
        for start in range(0, count, 128):
            same = s.scene_col[pl.ds(keys + start, 128), :] == row
            s.mask[start : start + 128, lane : lane + 128] = jnp.where(same, 1.0, 0.0).astype(BF16)


def finish(head, queries, output, s):
    start = HEAD * head if isinstance(head, int) else pl.multiple_of(HEAD * head, HEAD)
    s.attended[pl.ds(start, HEAD), queries] = (
        output[0:HEAD] * (1.0 / output[HEAD : HEAD + 1])
    ).astype(BF16)


def attend_bounded(counts, choose, scenes, s):
    def block(index, carry):
        kind, start = choose(index)
        for number, count in enumerate(counts):

            @pl.when(kind == number)
            def _(count=count):
                attend_block(index, start, count, scenes, s)

        return carry

    lax.fori_loop(0, ROWS // QUERY_BLOCK, block, 0)


def attend_block(index, start, count, scenes, s):
    queries = pl.ds(pl.multiple_of(index * QUERY_BLOCK, QUERY_BLOCK), QUERY_BLOCK)
    keys = pl.ds(start, count)
    make_mask(start, count, index, scenes, s)
    mask = s.mask[0:count]
    for head in range(HEADS):
        score = dot(s.key_split[head // 2, keys, :], s.query_split[head, :, queries])
        weight = jnp.exp2(score * EXPONENT_SCALE).astype(BF16) * mask
        finish(head, queries, dot(s.value[head, :, keys], weight), s)


def attend_any(scenes, s):
    lane_head = lax.broadcasted_iota(jnp.int32, (1, 128), 1) // HEAD

    def block(index, carry):
        queries = pl.ds(pl.multiple_of(index * QUERY_BLOCK, QUERY_BLOCK), QUERY_BLOCK)
        make_mask(0, ROWS, index, scenes, s)

        def one_head(head, carry):
            group = head // 8
            lanes = jnp.where(lane_head == head % 8, 1.0, 0.0).astype(BF16)
            score = dot(s.key[group] * lanes, s.query[group, :, queries]) * 0.25
            score = jnp.where(s.mask[...] > 0, score, F32(-1e30))
            top = jnp.max(score, axis=0, keepdims=True)
            weight = jnp.exp(score - top).astype(BF16)
            finish(head, queries, dot(s.value[head], weight), s)
            return carry

        return lax.fori_loop(0, HEADS, one_head, carry)

    lax.fori_loop(0, ROWS // QUERY_BLOCK, block, 0)


def scene_columns(scenes, s):
    for start in range(0, ROWS, 128):
        piece = scenes[start // 128 : start // 128 + 1, :].astype(F32)
        s.scene_col[start : start + 128, :] = jnp.transpose(jnp.broadcast_to(piece, (128, 128)))


def mlp_rows(rows, x, gain, s):
    attended = jnp.transpose(s.attended[:, rows])
    middle = (x[rows].astype(F32) + dot(attended, s.w_proj[...])).astype(BF16)
    normed = layer_norm(middle.astype(F32), gain)
    hidden = gelu(dot(normed, s.w_up[...])).astype(BF16)
    return middle.astype(F32) + dot(hidden, s.w_down[...])


def neighbours(me):
    return lax.rem(me + 1, 128), lax.rem(me + 127, 128)


def crossings(device, rank_ref):
    above, below = neighbours(device)
    flag = jnp.int32(0)
    for tile in range(TILES):
        owner = rank_ref[tile * TILE] >> 10
        crosses = ((owner ^ device) & 1) * ((owner != above) & (owner != below)).astype(jnp.int32)
        flag = flag | crosses
    return flag


def write_notes(scenes, flag, notes):
    lane = lax.broadcasted_iota(jnp.int32, (1, 128), 1)
    flags = jnp.where(lane == TILE + 1, flag, 0)
    notes.empty[...] = jnp.broadcast_to(flags, notes.empty.shape).astype(F32).astype(BF16)
    for tile in range(TILES):
        row = scenes[tile // 4 : tile // 4 + 1, (tile % 4) * TILE : (tile % 4 + 1) * TILE]
        row = jnp.concatenate([row] * 4, axis=1)
        row = jnp.where(lane < TILE, row, jnp.where(lane == TILE, tile + 1, flags))
        row = jnp.broadcast_to(row, (GROUP_ROWS, 128)).astype(F32).astype(BF16)
        notes.result[tile, :, NOTE:LANES] = row


def sort_tiles(entries, plan_out, scene_out):
    count = sum(notes.shape[0] for notes, _, _ in entries)
    total = -(-count // 128) * 128
    tables, sources = [], []
    for notes, first, step in entries:
        tables.append(notes[:, 0:1, NOTE:LANES].astype(F32).reshape(notes.shape[0], 128))
        index = lax.broadcasted_iota(jnp.int32, (notes.shape[0], 1), 0)
        sources.append(first + step * index)
    if total > count:
        tables.append(jnp.zeros((total - count, 128), F32))
        sources.append(jnp.zeros((total - count, 1), jnp.int32))
    table = jnp.concatenate(tables, axis=0)
    source = jnp.concatenate(sources, axis=0)
    place = table[:, TILE : TILE + 1]
    far = F32(1 << 20)
    key = jnp.where(place > 0, source.astype(F32) * TILE + place, far)
    wide = jnp.broadcast_to(key, (total, 128))
    row = jnp.concatenate(
        [jnp.transpose(wide[start : start + 128])[0:1] for start in range(0, total, 128)], axis=1
    )
    rank = jnp.sum((key < row).astype(F32), axis=0, keepdims=True)
    rank = jnp.where(row < far, rank, -1.0)
    target = lax.broadcasted_iota(jnp.int32, (TILES, total), 0).astype(F32)
    chosen = jnp.where(rank == target, 1.0, 0.0).astype(BF16)
    lane = lax.broadcasted_iota(jnp.int32, (total, 128), 1)
    entry = lax.broadcasted_iota(jnp.int32, (total, 128), 0)
    table = jnp.where(lane == TILE + 2, entry % 128, jnp.where(lane == TILE + 3, entry // 128, table.astype(jnp.int32)))
    ordered = dot(chosen, table.astype(F32).astype(BF16)).astype(jnp.int32)
    plan_out[...] = ordered
    group = lax.broadcasted_iota(jnp.int32, (1, 128), 1) // TILE
    lines = jnp.zeros((ROWS // 128, 128), jnp.int32)
    for part in range(4):
        piece = plan_out[pl.ds(part, ROWS // 128, stride=4), :]
        piece = pltpu.roll(piece, TILE * part, 1) if part else piece
        lines = jnp.where(group == part, piece, lines)
    scene_out[...] = lines


class Notes:
    def __init__(self, empty, result):
        self.empty, self.result = empty, result


def first_kernel(
    me_ref, rank_ref, x, scenes, gains, w_qkv, w_proj, w_up, w_down,
    send, send_other, up, down, local, empty, result, fill_sem, *scratch,
):
    s = Scratch(scratch)
    copies = start_weights(0, (w_proj, w_up, w_down), (s.w_proj, s.w_up, s.w_down), s)
    me = me_ref[0]
    write_notes(scenes, crossings(me, rank_ref), Notes(empty, result))
    fills = []
    for index, target in enumerate((send, send_other, up, down, local)):
        count = target.shape[0]
        fills.append(
            pltpu.make_async_copy(
                empty.at[0:count], target.at[:, :, NOTE:LANES], fill_sem.at[index]
            )
        )
        fills[-1].start()
    scene_columns(scenes, s)
    bound, largest = project(x, gains[0, 0:1], w_qkv.at[0], s)
    quick = (bound <= SCORE_LIMIT) & (largest <= VALUE_LIMIT)

    @pl.when(quick)
    def _():
        attend_bounded((ROWS,), lambda index: (0, 0), scenes, s)

    @pl.when(jnp.logical_not(quick))
    def _():
        attend_any(scenes, s)

    for copy in copies + fills:
        copy.wait()
    above, below = neighbours(me)
    slots = (jnp.int32(0), jnp.int32(0))
    for start in range(0, ROWS, MLP_BLOCK):
        rows = mlp_rows(slice(start, start + MLP_BLOCK), x, gains[0, 1:2], s)
        tiles = slice(start // TILE, (start + MLP_BLOCK) // TILE)
        rows = rows.reshape(MLP_BLOCK // TILE, GROUPS, GROUP_ROWS, C)
        for group in range(GROUPS):
            result[tiles, :, C * group : C * (group + 1)] = rows[:, group].astype(BF16)

        def one_tile(tile, slots):
            owner = rank_ref[tile * TILE] >> 10

            def put(target, index):
                pltpu.make_async_copy(result.at[tile], target.at[index], s.out_sem).start()

            is_up, is_down, stays = owner == above, owner == below, owner == me

            @pl.when(is_up)
            def _():
                put(up, jnp.minimum(slots[0], MOST_TILES - 1))

            @pl.when(is_down)
            def _():
                put(down, jnp.minimum(slots[1], MOST_TILES - 1))

            @pl.when(stays)
            def _():
                put(local, tile)

            far = jnp.logical_not(is_up | is_down | stays)
            crosses = (owner ^ me) & 1 == 1

            @pl.when(far & jnp.logical_not(crosses))
            def _():
                put(send, owner // 2)

            @pl.when(far & crosses)
            def _():
                put(send_other, owner // 2)

            return (slots[0] + is_up.astype(jnp.int32), slots[1] + is_down.astype(jnp.int32))

        slots = lax.fori_loop(start // TILE, (start + MLP_BLOCK) // TILE, one_tile, slots)
    pltpu.make_async_copy(result, local, s.out_sem).wait()


def second_kernel(
    me_ref, gains, *refs, sources,
):
    arrays, refs = refs[:sources], refs[sources:]
    w_qkv, w_proj, w_up, w_down, out, x, plan_vmem, scenes, result, plan, plan_sem = refs[:11]
    s = Scratch(refs[11:])
    me = me_ref[0]
    core = lax.rem(me, 2)
    above, below = neighbours(me)
    firsts = ((core, 2), (1 - core, 2))[: sources - 3] + ((below, 0), (above, 0), (me, 0))
    copies = start_weights(
        1, (w_qkv, w_proj, w_up, w_down), (s.w_qkv, s.w_proj, s.w_up, s.w_down), s
    )
    entries = [(array, *first) for array, first in zip(arrays, firsts, strict=True)]
    sort_tiles(entries, plan_vmem, scenes)
    to_scalars = pltpu.make_async_copy(plan_vmem, plan, plan_sem)
    to_scalars.start()
    scene_columns(scenes, s)
    to_scalars.wait()

    def fetch(index, carry):
        entry = plan[index, TILE + 2] + 128 * plan[index, TILE + 3]
        first = 0
        for array in arrays:
            end = first + array.shape[0]

            @pl.when((entry >= first) & (entry < end))
            def _(array=array, first=first):
                for group in range(GROUPS):
                    target = pl.ds(pl.multiple_of(index * TILE + group * GROUP_ROWS, GROUP_ROWS), GROUP_ROWS)
                    x[target, :] = array[entry - first, :, C * group : C * (group + 1)].astype(F32)

            first = end
        return carry

    lax.fori_loop(0, TILES, fetch, 0)
    copies[0].wait()
    bound, largest = project(x, gains[1, 0:1], s.w_qkv, s)
    quick = (bound <= SCORE_LIMIT) & (largest <= VALUE_LIMIT)

    def window(index, count):
        first = plan[index * (QUERY_BLOCK // TILE), 0]
        last = plan[(index + 1) * (QUERY_BLOCK // TILE) - 1, TILE - 1]
        start = jnp.int32(0)
        for piece in range(1, (ROWS - count) // 128 + 1):
            start = start + (plan[4 * piece - 1, TILE - 1] < first).astype(jnp.int32)
        end = start * 128 + count
        fits = (end >= ROWS) | (plan[jnp.minimum(end // TILE, TILES - 1), 0] > last)
        return pl.multiple_of(start * 128, 128), fits

    def choose(index):
        short, enough = window(index, WINDOWS[0])
        wide, _ = window(index, WINDOWS[1])
        return jnp.where(enough, 0, 1), pl.multiple_of(jnp.where(enough, short, wide), 128)

    fits = quick
    for index in range(ROWS // QUERY_BLOCK):
        fits = fits & window(index, WINDOWS[1])[1]

    @pl.when(fits)
    def _():
        attend_bounded(WINDOWS, choose, scenes, s)

    @pl.when(quick & jnp.logical_not(fits))
    def _():
        attend_bounded((ROWS,), lambda index: (0, 0), scenes, s)

    @pl.when(jnp.logical_not(quick))
    def _():
        attend_any(scenes, s)

    for copy in copies[1:]:
        copy.wait()
    for start in range(0, ROWS, MLP_BLOCK):
        rows = mlp_rows(slice(start, start + MLP_BLOCK), x, gains[1, 1:2], s)
        result[start : start + MLP_BLOCK] = rows.astype(BF16)

        def one_tile(index, carry):
            source = result.at[pl.ds(pl.multiple_of(index * TILE, TILE), TILE)]
            place = jnp.clip(plan[index, TILE] - 1, 0, TILES - 1)
            target = out.at[pl.ds(pl.multiple_of(place * TILE, TILE), TILE)]
            pltpu.make_async_copy(source, target, s.out_sem).start()
            return carry

        lax.fori_loop(start // TILE, (start + MLP_BLOCK) // TILE, one_tile, 0)
    pltpu.make_async_copy(result, out, s.out_sem).wait()


SMEM = pl.BlockSpec(memory_space=pltpu.SMEM)
VMEM = pl.BlockSpec(memory_space=pltpu.VMEM)
HBM = pl.BlockSpec(memory_space=pl.ANY)


def shards(point_feats, scene_id, hilbert_rank, norm_gains, w_qkv, w_proj, w_up, w_down):
    devices = lax.axis_size("seq")
    me = lax.axis_index("seq")
    me_array = me.reshape(1).astype(jnp.int32)
    weights = (w_qkv, w_proj, w_up, w_down)
    scenes = scene_id.reshape(ROWS // 128, 128)
    params = pltpu.CompilerParams(vmem_limit_bytes=VMEM_BYTES)
    rows = jax.ShapeDtypeStruct((ROWS, C), BF16)
    few = jax.ShapeDtypeStruct((MOST_TILES, GROUP_ROWS, LANES), BF16)
    bins = jax.ShapeDtypeStruct((CHIPS, GROUP_ROWS, LANES), BF16)
    own = jax.ShapeDtypeStruct((TILES, GROUP_ROWS, LANES), BF16)
    ring = range(devices)
    to_above = [(i, (i + 1) % devices) for i in ring]
    to_below = [(i, (i - 1) % devices) for i in ring]
    to_other = [(i, i ^ 1) for i in ring]
    cores = [list(range(core, devices, 2)) for core in range(2)]

    def among_chips(array):
        return lax.all_to_all(
            array, "seq", split_axis=0, concat_axis=0, tiled=True, axis_index_groups=cores
        )

    send, send_other, up, down, local = pl.pallas_call(
        first_kernel,
        in_specs=[SMEM, SMEM, VMEM, VMEM, VMEM, VMEM, HBM, HBM, HBM],
        out_specs=[HBM] * 5,
        out_shape=[bins, bins, few, few, own],
        scratch_shapes=[
            pltpu.VMEM((CHIPS, GROUP_ROWS, 128), BF16),
            pltpu.VMEM((TILES, GROUP_ROWS, LANES), BF16),
            pltpu.SemaphoreType.DMA((5,)),
        ]
        + scratch_shapes(),
        compiler_params=params,
        name="first_block",
    )(me_array, hilbert_rank, point_feats, scenes, norm_gains, *weights)

    received = among_chips(send)
    from_below = lax.ppermute(up, "seq", to_above)
    from_above = lax.ppermute(down, "seq", to_below)

    def second(*arrays):
        return pl.pallas_call(
            functools.partial(second_kernel, sources=len(arrays)),
            in_specs=[SMEM, VMEM] + [VMEM] * len(arrays) + [HBM] * 4,
            out_specs=HBM,
            out_shape=pltpu.HBM((ROWS, C), BF16),
            scratch_shapes=[
                pltpu.VMEM((ROWS, C), F32),
                pltpu.VMEM((TILES, 128), jnp.int32),
                pltpu.VMEM((ROWS // 128, 128), jnp.int32),
                pltpu.VMEM((ROWS, C), BF16),
                pltpu.SMEM((TILES, 128), jnp.int32),
                pltpu.SemaphoreType.DMA,
            ]
            + scratch_shapes(),
            compiler_params=params,
            name="second_block",
        )(me_array, norm_gains, *arrays, *weights)

    crossing = jnp.max(received[:, 0, NOTE + TILE + 1].astype(jnp.int32)).reshape(1)
    crossing_other = lax.ppermute(crossing, "seq", to_other)
    out = second(received, from_below, from_above, local)

    def with_crossing(out, tiles, received, *rest):
        return second(received, among_chips(lax.ppermute(tiles, "seq", to_other)), *rest)

    def without_crossing(out, *rest):
        return out

    return lax.cond(
        jnp.maximum(crossing, crossing_other)[0] > 0, with_crossing, without_crossing,
        out, send_other, received, from_below, from_above, local,
    )


def solution(mesh):
    placed = (P("seq", None), P("seq"), P("seq"), P(), P(), P(), P(), P())
    return jax.shard_map(
        shards, mesh=mesh, in_specs=placed, out_specs=P("seq", None), check_vma=False
    )
```

```python
import functools
import math

import jax
import jax.numpy as jnp
from jax import lax
from jax.experimental import pallas as pl
from jax.experimental.pallas import tpu as pltpu
from jax.sharding import PartitionSpec as P

C = 256
HEADS = 16
HEAD = 16
ROWS = 1024
FFN = 1024
TILES = 32
TILE = 32
MOST_TILES = 3
CHIPS = 64
GROUPS = 4
GROUP_ROWS = TILE // GROUPS
NOTE = GROUPS * C
LANES = NOTE + 128
EPSILON = 1e-05
QUERY_BLOCK = 256
WINDOWS = (384, 512)
ROW_BLOCK = 512
MLP_BLOCK = 1024
SPLIT_SCALE = 8.0
EXPONENT_SCALE = 0.25 / SPLIT_SCALE**2 / math.log(2.0)
SCORE_LIMIT = 40.0
VALUE_LIMIT = 40.0
BF16 = jnp.bfloat16
F32 = jnp.float32
F8 = jnp.float8_e4m3fn
VMEM_BYTES = 56 << 20


def dot(left, right, left_dim=1, right_dim=0):
    return lax.dot_general(
        left, right, (((left_dim,), (right_dim,)), ((), ())), preferred_element_type=F32
    )


def layer_norm(values, gain):
    center = values - jnp.mean(values, axis=-1, keepdims=True)
    spread = jnp.mean(center * center, axis=-1, keepdims=True)
    return (center * lax.rsqrt(spread + EPSILON) * gain).astype(BF16)


def split(values):
    scaled = values.astype(F32) * SPLIT_SCALE
    high = scaled.astype(F8).astype(F32)
    low = scaled - high
    return high, low


def gelu(values):
    return 0.5 * values * (1.0 + lax.erf(values * (0.5**0.5)))


class Scratch:
    names = (
        "w_qkv", "w_proj", "w_up", "w_down", "key", "query", "key_split", "query_split",
        "value", "scene_col", "mask", "attended", "normed", "sems", "out_sem",
    )

    def __init__(self, refs):
        for name, ref in zip(self.names, refs, strict=True):
            setattr(self, name, ref)


def scratch_shapes():
    return [
        pltpu.VMEM((C, 3 * C), BF16),
        pltpu.VMEM((C, C), BF16),
        pltpu.VMEM((C, FFN), BF16),
        pltpu.VMEM((FFN, C), BF16),
        pltpu.VMEM((2, ROWS, 128), BF16),
        pltpu.VMEM((2, 128, ROWS), BF16),
        pltpu.VMEM((HEADS // 2, ROWS, 128), F8),
        pltpu.VMEM((HEADS, 128, ROWS), F8),
        pltpu.VMEM((HEADS, 2 * HEAD, ROWS), BF16),
        pltpu.VMEM((ROWS, 128), F32),
        pltpu.VMEM((ROWS, QUERY_BLOCK), BF16),
        pltpu.VMEM((C, ROWS), BF16),
        pltpu.VMEM((ROWS, C), BF16),
        pltpu.SemaphoreType.DMA((4,)),
        pltpu.SemaphoreType.DMA,
    ]


def start_weights(block, weights, targets, s):
    copies = [
        pltpu.make_async_copy(source.at[block], target, s.sems.at[i])
        for i, (source, target) in enumerate(zip(weights, targets, strict=True))
    ]
    for copy in copies:
        copy.start()
    return copies


def project(x, gain, w_qkv, s):
    for start in range(0, ROWS, ROW_BLOCK):
        rows = slice(start, start + ROW_BLOCK)
        s.normed[rows] = layer_norm(x[rows].astype(F32), gain)
    normed = s.normed[...]
    query = dot(w_qkv[:, 0:C], normed, 0, 1).astype(BF16)
    value = dot(w_qkv[:, 2 * C : 3 * C], normed, 0, 1).astype(BF16)
    for head in range(HEADS):
        s.value[head, 0:HEAD, :] = value[HEAD * head : HEAD * (head + 1)]
        s.value[head, HEAD:, :] = jnp.ones((HEAD, ROWS), BF16)
    s.query[0] = query[0:128]
    s.query[1] = query[128:256]
    high, low = split(query)
    for head in range(HEADS):
        part = slice(HEAD * head, HEAD * (head + 1))
        both = jnp.concatenate([high[part].astype(BF16), low[part].astype(BF16)], axis=0).astype(F8)
        own, other = 64 * (head % 2), 64 * (1 - head % 2)
        s.query_split[head, own : own + 32, :] = both
        s.query_split[head, own + 32 : own + 64, :] = both
        s.query_split[head, other : other + 64, :] = jnp.zeros((64, ROWS), F8)

    row = lax.broadcasted_iota(jnp.int32, (64, 256), 0)
    lane = lax.broadcasted_iota(jnp.int32, (64, 256), 1)
    same = row == (lane // 64) * HEAD + lane % HEAD
    spread_high = jnp.where(same & (lane % 64 < 32), 1.0, 0.0).astype(BF16)
    spread_low = jnp.where(same & (lane % 64 >= 32), 1.0, 0.0).astype(BF16)
    spread = jnp.concatenate([spread_high, spread_low], axis=0).astype(F8)
    channel = lax.broadcasted_iota(jnp.int32, (C, 128), 0)
    column = lax.broadcasted_iota(jnp.int32, (C, 128), 1)
    head_sum = jnp.where(channel // HEAD == column, 1.0, 0.0).astype(BF16)
    key_norm = jnp.zeros((1, 128), F32)
    query_norm = dot(head_sum, query * query, 0, 0)
    for start in range(0, ROWS, ROW_BLOCK):
        rows = slice(start, start + ROW_BLOCK)
        key = dot(s.normed[rows], w_qkv[:, C : 2 * C]).astype(BF16)
        s.key[0, rows] = key[:, 0:128]
        s.key[1, rows] = key[:, 128:256]
        norms = dot(key * key, head_sum)
        key_norm = jnp.maximum(key_norm, jnp.max(norms, axis=0, keepdims=True))
        high, low = split(key)
        for quarter in range(4):
            lanes = slice(64 * quarter, 64 * quarter + 64)
            pair = jnp.concatenate([high[:, lanes], low[:, lanes]], axis=1).astype(F8)
            expanded = dot(pair, spread).astype(F8)
            s.key_split[2 * quarter, rows] = expanded[:, 0:128]
            s.key_split[2 * quarter + 1, rows] = expanded[:, 128:256]
    query_norm, key_norm = jnp.max(query_norm), jnp.max(key_norm)
    bound = 0.25 * 1.02 * jnp.sqrt(query_norm * key_norm)
    return bound, 1.02 * jnp.sqrt(jnp.maximum(query_norm, key_norm))


def make_mask(keys, count, index, scenes, s):
    for lane in range(0, QUERY_BLOCK, 128):
        row = scenes[pl.ds(index * (QUERY_BLOCK // 128) + lane // 128, 1), :].astype(F32)
        for start in range(0, count, 128):
            same = s.scene_col[pl.ds(keys + start, 128), :] == row
            s.mask[start : start + 128, lane : lane + 128] = jnp.where(same, 1.0, 0.0).astype(BF16)


def finish(head, queries, output, s):
    start = HEAD * head if isinstance(head, int) else pl.multiple_of(HEAD * head, HEAD)
    s.attended[pl.ds(start, HEAD), queries] = (
        output[0:HEAD] * (1.0 / output[HEAD : HEAD + 1])
    ).astype(BF16)


def attend_bounded(counts, choose, scenes, s):
    def block(index, carry):
        kind, start = choose(index)
        for number, count in enumerate(counts):

            @pl.when(kind == number)
            def _(count=count):
                attend_block(index, start, count, scenes, s)

        return carry

    lax.fori_loop(0, ROWS // QUERY_BLOCK, block, 0)


def attend_block(index, start, count, scenes, s):
    queries = pl.ds(pl.multiple_of(index * QUERY_BLOCK, QUERY_BLOCK), QUERY_BLOCK)
    keys = pl.ds(start, count)
    make_mask(start, count, index, scenes, s)
    mask = s.mask[0:count]
    for head in range(HEADS):
        score = dot(s.key_split[head // 2, keys, :], s.query_split[head, :, queries])
        weight = jnp.exp2(score * EXPONENT_SCALE).astype(BF16) * mask
        finish(head, queries, dot(s.value[head, :, keys], weight), s)


def attend_any(scenes, s):
    lane_head = lax.broadcasted_iota(jnp.int32, (1, 128), 1) // HEAD

    def block(index, carry):
        queries = pl.ds(pl.multiple_of(index * QUERY_BLOCK, QUERY_BLOCK), QUERY_BLOCK)
        make_mask(0, ROWS, index, scenes, s)

        def one_head(head, carry):
            group = head // 8
            lanes = jnp.where(lane_head == head % 8, 1.0, 0.0).astype(BF16)
            score = dot(s.key[group] * lanes, s.query[group, :, queries]) * 0.25
            score = jnp.where(s.mask[...] > 0, score, F32(-1e30))
            top = jnp.max(score, axis=0, keepdims=True)
            weight = jnp.exp(score - top).astype(BF16)
            finish(head, queries, dot(s.value[head], weight), s)
            return carry

        return lax.fori_loop(0, HEADS, one_head, carry)

    lax.fori_loop(0, ROWS // QUERY_BLOCK, block, 0)


def scene_columns(scenes, s):
    for start in range(0, ROWS, 128):
        piece = scenes[start // 128 : start // 128 + 1, :].astype(F32)
        s.scene_col[start : start + 128, :] = jnp.transpose(jnp.broadcast_to(piece, (128, 128)))


def mlp_rows(rows, x, gain, s):
    attended = jnp.transpose(s.attended[:, rows])
    middle = (x[rows].astype(F32) + dot(attended, s.w_proj[...])).astype(BF16)
    normed = layer_norm(middle.astype(F32), gain)
    hidden = gelu(dot(normed, s.w_up[...])).astype(BF16)
    return middle.astype(F32) + dot(hidden, s.w_down[...])


def neighbours(me):
    return lax.rem(me + 1, 128), lax.rem(me + 127, 128)


def crossings(device, rank_ref):
    above, below = neighbours(device)
    flag = jnp.int32(0)
    for tile in range(TILES):
        owner = rank_ref[tile * TILE] >> 10
        crosses = ((owner ^ device) & 1) * ((owner != above) & (owner != below)).astype(jnp.int32)
        flag = flag | crosses
    return flag


def write_notes(scenes, flag, notes):
    lane = lax.broadcasted_iota(jnp.int32, (1, 128), 1)
    flags = jnp.where(lane == TILE + 1, flag, 0)
    notes.empty[...] = jnp.broadcast_to(flags, notes.empty.shape).astype(F32).astype(BF16)
    for tile in range(TILES):
        row = scenes[tile // 4 : tile // 4 + 1, (tile % 4) * TILE : (tile % 4 + 1) * TILE]
        row = jnp.concatenate([row] * 4, axis=1)
        row = jnp.where(lane < TILE, row, jnp.where(lane == TILE, tile + 1, flags))
        row = jnp.broadcast_to(row, (GROUP_ROWS, 128)).astype(F32).astype(BF16)
        notes.result[tile, :, NOTE:LANES] = row


def sort_tiles(entries, plan_out, scene_out):
    count = sum(notes.shape[0] for notes, _, _ in entries)
    total = -(-count // 128) * 128
    tables, sources = [], []
    for notes, first, step in entries:
        tables.append(notes[:, 0:1, NOTE:LANES].astype(F32).reshape(notes.shape[0], 128))
        index = lax.broadcasted_iota(jnp.int32, (notes.shape[0], 1), 0)
        sources.append(first + step * index)
    if total > count:
        tables.append(jnp.zeros((total - count, 128), F32))
        sources.append(jnp.zeros((total - count, 1), jnp.int32))
    table = jnp.concatenate(tables, axis=0)
    source = jnp.concatenate(sources, axis=0)
    place = table[:, TILE : TILE + 1]
    far = F32(1 << 20)
    key = jnp.where(place > 0, source.astype(F32) * TILE + place, far)
    wide = jnp.broadcast_to(key, (total, 128))
    row = jnp.concatenate(
        [jnp.transpose(wide[start : start + 128])[0:1] for start in range(0, total, 128)], axis=1
    )
    rank = jnp.sum((key < row).astype(F32), axis=0, keepdims=True)
    rank = jnp.where(row < far, rank, -1.0)
    target = lax.broadcasted_iota(jnp.int32, (TILES, total), 0).astype(F32)
    chosen = jnp.where(rank == target, 1.0, 0.0).astype(BF16)
    lane = lax.broadcasted_iota(jnp.int32, (total, 128), 1)
    entry = lax.broadcasted_iota(jnp.int32, (total, 128), 0)
    table = jnp.where(lane == TILE + 2, entry % 128, jnp.where(lane == TILE + 3, entry // 128, table.astype(jnp.int32)))
    ordered = dot(chosen, table.astype(F32).astype(BF16)).astype(jnp.int32)
    plan_out[...] = ordered
    group = lax.broadcasted_iota(jnp.int32, (1, 128), 1) // TILE
    lines = jnp.zeros((ROWS // 128, 128), jnp.int32)
    for part in range(4):
        piece = plan_out[pl.ds(part, ROWS // 128, stride=4), :]
        piece = pltpu.roll(piece, TILE * part, 1) if part else piece
        lines = jnp.where(group == part, piece, lines)
    scene_out[...] = lines


class Notes:
    def __init__(self, empty, result):
        self.empty, self.result = empty, result


def first_kernel(
    me_ref, rank_ref, x, scenes, gains, w_qkv, w_proj, w_up, w_down,
    send, send_other, up, down, local, empty, result, fill_sem, *scratch,
):
    s = Scratch(scratch)
    copies = start_weights(0, (w_proj, w_up, w_down), (s.w_proj, s.w_up, s.w_down), s)
    me = me_ref[0]
    write_notes(scenes, crossings(me, rank_ref), Notes(empty, result))
    fills = []
    for index, target in enumerate((send, send_other, up, down, local)):
        count = target.shape[0]
        fills.append(
            pltpu.make_async_copy(
                empty.at[0:count], target.at[:, :, NOTE:LANES], fill_sem.at[index]
            )
        )
        fills[-1].start()
    scene_columns(scenes, s)
    bound, largest = project(x, gains[0, 0:1], w_qkv.at[0], s)
    quick = (bound <= SCORE_LIMIT) & (largest <= VALUE_LIMIT)

    @pl.when(quick)
    def _():
        attend_bounded((ROWS,), lambda index: (0, 0), scenes, s)

    @pl.when(jnp.logical_not(quick))
    def _():
        attend_any(scenes, s)

    for copy in copies + fills:
        copy.wait()
    above, below = neighbours(me)
    slots = (jnp.int32(0), jnp.int32(0))
    for start in range(0, ROWS, MLP_BLOCK):
        rows = mlp_rows(slice(start, start + MLP_BLOCK), x, gains[0, 1:2], s)
        tiles = slice(start // TILE, (start + MLP_BLOCK) // TILE)
        rows = rows.reshape(MLP_BLOCK // TILE, GROUPS, GROUP_ROWS, C)
        for group in range(GROUPS):
            result[tiles, :, C * group : C * (group + 1)] = rows[:, group].astype(BF16)

        def one_tile(tile, slots):
            owner = rank_ref[tile * TILE] >> 10

            def put(target, index):
                pltpu.make_async_copy(result.at[tile], target.at[index], s.out_sem).start()

            is_up, is_down, stays = owner == above, owner == below, owner == me

            @pl.when(is_up)
            def _():
                put(up, jnp.minimum(slots[0], MOST_TILES - 1))

            @pl.when(is_down)
            def _():
                put(down, jnp.minimum(slots[1], MOST_TILES - 1))

            @pl.when(stays)
            def _():
                put(local, tile)

            far = jnp.logical_not(is_up | is_down | stays)
            crosses = (owner ^ me) & 1 == 1

            @pl.when(far & jnp.logical_not(crosses))
            def _():
                put(send, owner // 2)

            @pl.when(far & crosses)
            def _():
                put(send_other, owner // 2)

            return (slots[0] + is_up.astype(jnp.int32), slots[1] + is_down.astype(jnp.int32))

        slots = lax.fori_loop(start // TILE, (start + MLP_BLOCK) // TILE, one_tile, slots)
    pltpu.make_async_copy(result, local, s.out_sem).wait()


def second_kernel(
    me_ref, gains, *refs, sources,
):
    arrays, refs = refs[:sources], refs[sources:]
    w_qkv, w_proj, w_up, w_down, out, x, plan_vmem, scenes, result, plan, plan_sem = refs[:11]
    s = Scratch(refs[11:])
    me = me_ref[0]
    core = lax.rem(me, 2)
    above, below = neighbours(me)
    firsts = ((core, 2), (1 - core, 2))[: sources - 3] + ((below, 0), (above, 0), (me, 0))
    copies = start_weights(
        1, (w_qkv, w_proj, w_up, w_down), (s.w_qkv, s.w_proj, s.w_up, s.w_down), s
    )
    entries = [(array, *first) for array, first in zip(arrays, firsts, strict=True)]
    sort_tiles(entries, plan_vmem, scenes)
    to_scalars = pltpu.make_async_copy(plan_vmem, plan, plan_sem)
    to_scalars.start()
    scene_columns(scenes, s)
    to_scalars.wait()

    def fetch(index, carry):
        entry = plan[index, TILE + 2] + 128 * plan[index, TILE + 3]
        first = 0
        for array in arrays:
            end = first + array.shape[0]

            @pl.when((entry >= first) & (entry < end))
            def _(array=array, first=first):
                for group in range(GROUPS):
                    target = pl.ds(pl.multiple_of(index * TILE + group * GROUP_ROWS, GROUP_ROWS), GROUP_ROWS)
                    x[target, :] = array[entry - first, :, C * group : C * (group + 1)].astype(F32)

            first = end
        return carry

    lax.fori_loop(0, TILES, fetch, 0)
    copies[0].wait()
    bound, largest = project(x, gains[1, 0:1], s.w_qkv, s)
    quick = (bound <= SCORE_LIMIT) & (largest <= VALUE_LIMIT)

    def window(index, count):
        first = plan[index * (QUERY_BLOCK // TILE), 0]
        last = plan[(index + 1) * (QUERY_BLOCK // TILE) - 1, TILE - 1]
        start = jnp.int32(0)
        for piece in range(1, (ROWS - count) // 128 + 1):
            start = start + (plan[4 * piece - 1, TILE - 1] < first).astype(jnp.int32)
        end = start * 128 + count
        fits = (end >= ROWS) | (plan[jnp.minimum(end // TILE, TILES - 1), 0] > last)
        return pl.multiple_of(start * 128, 128), fits

    def choose(index):
        short, enough = window(index, WINDOWS[0])
        wide, _ = window(index, WINDOWS[1])
        return jnp.where(enough, 0, 1), pl.multiple_of(jnp.where(enough, short, wide), 128)

    fits = quick
    for index in range(ROWS // QUERY_BLOCK):
        fits = fits & window(index, WINDOWS[1])[1]

    @pl.when(fits)
    def _():
        attend_bounded(WINDOWS, choose, scenes, s)

    @pl.when(quick & jnp.logical_not(fits))
    def _():
        attend_bounded((ROWS,), lambda index: (0, 0), scenes, s)

    @pl.when(jnp.logical_not(quick))
    def _():
        attend_any(scenes, s)

    for copy in copies[1:]:
        copy.wait()
    for start in range(0, ROWS, MLP_BLOCK):
        rows = mlp_rows(slice(start, start + MLP_BLOCK), x, gains[1, 1:2], s)
        result[start : start + MLP_BLOCK] = rows.astype(BF16)

        def one_tile(index, carry):
            source = result.at[pl.ds(pl.multiple_of(index * TILE, TILE), TILE)]
            place = jnp.clip(plan[index, TILE] - 1, 0, TILES - 1)
            target = out.at[pl.ds(pl.multiple_of(place * TILE, TILE), TILE)]
            pltpu.make_async_copy(source, target, s.out_sem).start()
            return carry

        lax.fori_loop(start // TILE, (start + MLP_BLOCK) // TILE, one_tile, 0)
    pltpu.make_async_copy(result, out, s.out_sem).wait()


SMEM = pl.BlockSpec(memory_space=pltpu.SMEM)
VMEM = pl.BlockSpec(memory_space=pltpu.VMEM)
HBM = pl.BlockSpec(memory_space=pl.ANY)


def shards(point_feats, scene_id, hilbert_rank, norm_gains, w_qkv, w_proj, w_up, w_down):
    devices = lax.axis_size("seq")
    me = lax.axis_index("seq")
    me_array = me.reshape(1).astype(jnp.int32)
    weights = (w_qkv, w_proj, w_up, w_down)
    scenes = scene_id.reshape(ROWS // 128, 128)
    params = pltpu.CompilerParams(vmem_limit_bytes=VMEM_BYTES)
    rows = jax.ShapeDtypeStruct((ROWS, C), BF16)
    few = jax.ShapeDtypeStruct((MOST_TILES, GROUP_ROWS, LANES), BF16)
    bins = jax.ShapeDtypeStruct((CHIPS, GROUP_ROWS, LANES), BF16)
    own = jax.ShapeDtypeStruct((TILES, GROUP_ROWS, LANES), BF16)
    ring = range(devices)
    to_above = [(i, (i + 1) % devices) for i in ring]
    to_below = [(i, (i - 1) % devices) for i in ring]
    to_other = [(i, i ^ 1) for i in ring]
    cores = [list(range(core, devices, 2)) for core in range(2)]

    def among_chips(array):
        return lax.all_to_all(
            array, "seq", split_axis=0, concat_axis=0, tiled=True, axis_index_groups=cores
        )

    send, send_other, up, down, local = pl.pallas_call(
        first_kernel,
        in_specs=[SMEM, SMEM, VMEM, VMEM, VMEM, VMEM, HBM, HBM, HBM],
        out_specs=[HBM] * 5,
        out_shape=[bins, bins, few, few, own],
        scratch_shapes=[
            pltpu.VMEM((CHIPS, GROUP_ROWS, 128), BF16),
            pltpu.VMEM((TILES, GROUP_ROWS, LANES), BF16),
            pltpu.SemaphoreType.DMA((5,)),
        ]
        + scratch_shapes(),
        compiler_params=params,
        name="first_block",
    )(me_array, hilbert_rank, point_feats, scenes, norm_gains, *weights)

    received = among_chips(send)
    from_below = lax.ppermute(up, "seq", to_above)
    from_above = lax.ppermute(down, "seq", to_below)

    def second(*arrays):
        return pl.pallas_call(
            functools.partial(second_kernel, sources=len(arrays)),
            in_specs=[SMEM, VMEM] + [VMEM] * len(arrays) + [HBM] * 4,
            out_specs=HBM,
            out_shape=pltpu.HBM((ROWS, C), BF16),
            scratch_shapes=[
                pltpu.VMEM((ROWS, C), F32),
                pltpu.VMEM((TILES, 128), jnp.int32),
                pltpu.VMEM((ROWS // 128, 128), jnp.int32),
                pltpu.VMEM((ROWS, C), BF16),
                pltpu.SMEM((TILES, 128), jnp.int32),
                pltpu.SemaphoreType.DMA,
            ]
            + scratch_shapes(),
            compiler_params=params,
            name="second_block",
        )(me_array, norm_gains, *arrays, *weights)

    crossing = jnp.max(received[:, 0, NOTE + TILE + 1].astype(jnp.int32)).reshape(1)
    crossing_other = lax.ppermute(crossing, "seq", to_other)
    out = second(received, from_below, from_above, local)

    def with_crossing(out, tiles, received, *rest):
        return second(received, among_chips(lax.ppermute(tiles, "seq", to_other)), *rest)

    def without_crossing(out, *rest):
        return out

    return lax.cond(
        jnp.max(jnp.concatenate([crossing, crossing_other])) > 0, with_crossing, without_crossing,
        out, send_other, received, from_below, from_above, local,
    )


def solution(mesh):
    placed = (P("seq", None), P("seq"), P("seq"), P(), P(), P(), P(), P())
    return jax.shard_map(
        shards, mesh=mesh, in_specs=placed, out_specs=P("seq", None), check_vma=False
    )
```

```python
import functools
import math

import jax
import jax.numpy as jnp
from jax import lax
from jax.experimental import pallas as pl
from jax.experimental.pallas import tpu as pltpu
from jax.sharding import PartitionSpec as P

C = 256
HEADS = 16
HEAD = 16
ROWS = 1024
FFN = 1024
TILES = 32
TILE = 32
MOST_TILES = 3
CHIPS = 64
GROUPS = 4
GROUP_ROWS = TILE // GROUPS
NOTE = GROUPS * C
LANES = NOTE + 128
EPSILON = 1e-05
QUERY_BLOCK = 256
WINDOWS = (384, 512)
ROW_BLOCK = 512
MLP_BLOCK = 1024
SPLIT_SCALE = 8.0
EXPONENT_SCALE = 0.25 / SPLIT_SCALE**2 / math.log(2.0)
SCORE_LIMIT = 40.0
VALUE_LIMIT = 40.0
BF16 = jnp.bfloat16
F32 = jnp.float32
F8 = jnp.float8_e4m3fn
VMEM_BYTES = 56 << 20


def dot(left, right, left_dim=1, right_dim=0):
    return lax.dot_general(
        left, right, (((left_dim,), (right_dim,)), ((), ())), preferred_element_type=F32
    )


def layer_norm(values, gain):
    center = values - jnp.mean(values, axis=-1, keepdims=True)
    spread = jnp.mean(center * center, axis=-1, keepdims=True)
    return (center * lax.rsqrt(spread + EPSILON) * gain).astype(BF16)


def split(values):
    scaled = values.astype(F32) * SPLIT_SCALE
    high = scaled.astype(F8).astype(F32)
    low = scaled - high
    return high, low


def gelu(values):
    return 0.5 * values * (1.0 + lax.erf(values * (0.5**0.5)))


class Scratch:
    names = (
        "w_qkv", "w_proj", "w_up", "w_down", "key", "query", "key_split", "query_split",
        "value", "scene_col", "mask", "attended", "normed", "sems", "out_sem",
    )

    def __init__(self, refs):
        for name, ref in zip(self.names, refs, strict=True):
            setattr(self, name, ref)


def scratch_shapes():
    return [
        pltpu.VMEM((C, 3 * C), BF16),
        pltpu.VMEM((C, C), BF16),
        pltpu.VMEM((C, FFN), BF16),
        pltpu.VMEM((FFN, C), BF16),
        pltpu.VMEM((2, ROWS, 128), BF16),
        pltpu.VMEM((2, 128, ROWS), BF16),
        pltpu.VMEM((HEADS // 2, ROWS, 128), F8),
        pltpu.VMEM((HEADS, 128, ROWS), F8),
        pltpu.VMEM((HEADS, 2 * HEAD, ROWS), BF16),
        pltpu.VMEM((ROWS, 128), F32),
        pltpu.VMEM((ROWS, QUERY_BLOCK), BF16),
        pltpu.VMEM((C, ROWS), BF16),
        pltpu.VMEM((ROWS, C), BF16),
        pltpu.SemaphoreType.DMA((4,)),
        pltpu.SemaphoreType.DMA,
    ]


def start_weights(block, weights, targets, s):
    copies = [
        pltpu.make_async_copy(source.at[block], target, s.sems.at[i])
        for i, (source, target) in enumerate(zip(weights, targets, strict=True))
    ]
    for copy in copies:
        copy.start()
    return copies


def project(x, gain, w_qkv, s):
    for start in range(0, ROWS, ROW_BLOCK):
        rows = slice(start, start + ROW_BLOCK)
        s.normed[rows] = layer_norm(x[rows].astype(F32), gain)
    normed = s.normed[...]
    query = dot(w_qkv[:, 0:C], normed, 0, 1).astype(BF16)
    value = dot(w_qkv[:, 2 * C : 3 * C], normed, 0, 1).astype(BF16)
    for head in range(HEADS):
        s.value[head, 0:HEAD, :] = value[HEAD * head : HEAD * (head + 1)]
        s.value[head, HEAD:, :] = jnp.ones((HEAD, ROWS), BF16)
    s.query[0] = query[0:128]
    s.query[1] = query[128:256]
    high, low = split(query)
    for head in range(HEADS):
        part = slice(HEAD * head, HEAD * (head + 1))
        both = jnp.concatenate([high[part].astype(BF16), low[part].astype(BF16)], axis=0).astype(F8)
        own, other = 64 * (head % 2), 64 * (1 - head % 2)
        s.query_split[head, own : own + 32, :] = both
        s.query_split[head, own + 32 : own + 64, :] = both
        s.query_split[head, other : other + 64, :] = jnp.zeros((64, ROWS), F8)
    squares = query.astype(F32) * query.astype(F32)
    query_norm = jnp.max(jnp.sum(squares.reshape(HEADS, HEAD, ROWS), axis=1), axis=1, keepdims=True)

    row = lax.broadcasted_iota(jnp.int32, (64, 256), 0)
    lane = lax.broadcasted_iota(jnp.int32, (64, 256), 1)
    same = row == (lane // 64) * HEAD + lane % HEAD
    spread_high = jnp.where(same & (lane % 64 < 32), 1.0, 0.0).astype(BF16)
    spread_low = jnp.where(same & (lane % 64 >= 32), 1.0, 0.0).astype(BF16)
    spread = jnp.concatenate([spread_high, spread_low], axis=0).astype(F8)
    channel = lax.broadcasted_iota(jnp.int32, (C, 128), 0)
    column = lax.broadcasted_iota(jnp.int32, (C, 128), 1)
    head_sum = jnp.where(channel // HEAD == column, 1.0, 0.0).astype(BF16)
    key_norm = jnp.zeros((1, 128), F32)
    highest = jnp.max(jnp.abs(query.astype(F32)))
    key_high = jnp.zeros((1, C), F32)
    for start in range(0, ROWS, ROW_BLOCK):
        rows = slice(start, start + ROW_BLOCK)
        key = dot(s.normed[rows], w_qkv[:, C : 2 * C]).astype(BF16)
        s.key[0, rows] = key[:, 0:128]
        s.key[1, rows] = key[:, 128:256]
        wide = key.astype(F32)
        key_high = jnp.maximum(key_high, jnp.max(jnp.abs(wide), axis=0, keepdims=True))
        norms = dot((wide * wide).astype(BF16), head_sum)
        key_norm = jnp.maximum(key_norm, jnp.max(norms, axis=0, keepdims=True))
        high, low = split(key)
        for quarter in range(4):
            lanes = slice(64 * quarter, 64 * quarter + 64)
            pair = jnp.concatenate([high[:, lanes], low[:, lanes]], axis=1).astype(F8)
            expanded = dot(pair, spread).astype(F8)
            s.key_split[2 * quarter, rows] = expanded[:, 0:128]
            s.key_split[2 * quarter + 1, rows] = expanded[:, 128:256]
    largest = jnp.maximum(highest, jnp.max(key_high))
    bound = 0.25 * 1.02 * jnp.sqrt(jnp.max(query_norm) * jnp.max(key_norm))
    return bound, largest


def make_mask(keys, count, index, scenes, s):
    for lane in range(0, QUERY_BLOCK, 128):
        row = scenes[pl.ds(index * (QUERY_BLOCK // 128) + lane // 128, 1), :].astype(F32)
        for start in range(0, count, 128):
            same = s.scene_col[pl.ds(keys + start, 128), :] == row
            s.mask[start : start + 128, lane : lane + 128] = jnp.where(same, 1.0, 0.0).astype(BF16)


def finish(head, queries, output, s):
    start = HEAD * head if isinstance(head, int) else pl.multiple_of(HEAD * head, HEAD)
    s.attended[pl.ds(start, HEAD), queries] = (
        output[0:HEAD] * (1.0 / output[HEAD : HEAD + 1])
    ).astype(BF16)


def attend_bounded(counts, choose, scenes, s):
    def block(index, carry):
        kind, start = choose(index)
        for number, count in enumerate(counts):

            @pl.when(kind == number)
            def _(count=count):
                attend_block(index, start, count, scenes, s)

        return carry

    lax.fori_loop(0, ROWS // QUERY_BLOCK, block, 0)


def attend_block(index, start, count, scenes, s):
    queries = pl.ds(pl.multiple_of(index * QUERY_BLOCK, QUERY_BLOCK), QUERY_BLOCK)
    keys = pl.ds(start, count)
    make_mask(start, count, index, scenes, s)
    mask = s.mask[0:count]
    for head in range(HEADS):
        score = dot(s.key_split[head // 2, keys, :], s.query_split[head, :, queries])
        weight = jnp.exp2(score * EXPONENT_SCALE).astype(BF16) * mask
        finish(head, queries, dot(s.value[head, :, keys], weight), s)


def attend_any(scenes, s):
    lane_head = lax.broadcasted_iota(jnp.int32, (1, 128), 1) // HEAD

    def block(index, carry):
        queries = pl.ds(pl.multiple_of(index * QUERY_BLOCK, QUERY_BLOCK), QUERY_BLOCK)
        make_mask(0, ROWS, index, scenes, s)

        def one_head(head, carry):
            group = head // 8
            lanes = jnp.where(lane_head == head % 8, 1.0, 0.0).astype(BF16)
            score = dot(s.key[group] * lanes, s.query[group, :, queries]) * 0.25
            score = jnp.where(s.mask[...] > 0, score, F32(-1e30))
            top = jnp.max(score, axis=0, keepdims=True)
            weight = jnp.exp(score - top).astype(BF16)
            finish(head, queries, dot(s.value[head], weight), s)
            return carry

        return lax.fori_loop(0, HEADS, one_head, carry)

    lax.fori_loop(0, ROWS // QUERY_BLOCK, block, 0)


def scene_columns(scenes, s):
    for start in range(0, ROWS, 128):
        piece = scenes[start // 128 : start // 128 + 1, :].astype(F32)
        s.scene_col[start : start + 128, :] = jnp.transpose(jnp.broadcast_to(piece, (128, 128)))


def mlp_rows(rows, x, gain, s):
    attended = jnp.transpose(s.attended[:, rows])
    middle = (x[rows].astype(F32) + dot(attended, s.w_proj[...])).astype(BF16)
    normed = layer_norm(middle.astype(F32), gain)
    hidden = gelu(dot(normed, s.w_up[...])).astype(BF16)
    return middle.astype(F32) + dot(hidden, s.w_down[...])


def neighbours(me):
    return lax.rem(me + 1, 128), lax.rem(me + 127, 128)


def crossings(device, rank_ref):
    above, below = neighbours(device)
    flag = jnp.int32(0)
    for tile in range(TILES):
        owner = rank_ref[tile * TILE] >> 10
        crosses = ((owner ^ device) & 1) * ((owner != above) & (owner != below)).astype(jnp.int32)
        flag = flag | crosses
    return flag


def write_notes(scenes, flag, notes):
    lane = lax.broadcasted_iota(jnp.int32, (1, 128), 1)
    flags = jnp.where(lane == TILE + 1, flag, 0)
    notes.empty[...] = jnp.broadcast_to(flags, notes.empty.shape).astype(F32).astype(BF16)
    for tile in range(TILES):
        row = scenes[tile // 4 : tile // 4 + 1, (tile % 4) * TILE : (tile % 4 + 1) * TILE]
        row = jnp.concatenate([row] * 4, axis=1)
        row = jnp.where(lane < TILE, row, jnp.where(lane == TILE, tile + 1, flags))
        row = jnp.broadcast_to(row, (GROUP_ROWS, 128)).astype(F32).astype(BF16)
        notes.result[tile, :, NOTE:LANES] = row


def sort_tiles(entries, plan_out, scene_out):
    count = sum(notes.shape[0] for notes, _, _ in entries)
    total = -(-count // 128) * 128
    tables, sources = [], []
    for notes, first, step in entries:
        tables.append(notes[:, 0:1, NOTE:LANES].astype(F32).reshape(notes.shape[0], 128))
        index = lax.broadcasted_iota(jnp.int32, (notes.shape[0], 1), 0)
        sources.append(first + step * index)
    if total > count:
        tables.append(jnp.zeros((total - count, 128), F32))
        sources.append(jnp.zeros((total - count, 1), jnp.int32))
    table = jnp.concatenate(tables, axis=0)
    source = jnp.concatenate(sources, axis=0)
    place = table[:, TILE : TILE + 1]
    far = F32(1 << 20)
    key = jnp.where(place > 0, source.astype(F32) * TILE + place, far)
    wide = jnp.broadcast_to(key, (total, 128))
    row = jnp.concatenate(
        [jnp.transpose(wide[start : start + 128])[0:1] for start in range(0, total, 128)], axis=1
    )
    rank = jnp.sum((key < row).astype(F32), axis=0, keepdims=True)
    rank = jnp.where(row < far, rank, -1.0)
    target = lax.broadcasted_iota(jnp.int32, (TILES, total), 0).astype(F32)
    chosen = jnp.where(rank == target, 1.0, 0.0).astype(BF16)
    lane = lax.broadcasted_iota(jnp.int32, (total, 128), 1)
    entry = lax.broadcasted_iota(jnp.int32, (total, 128), 0)
    table = jnp.where(lane == TILE + 2, entry % 128, jnp.where(lane == TILE + 3, entry // 128, table.astype(jnp.int32)))
    ordered = dot(chosen, table.astype(F32).astype(BF16)).astype(jnp.int32)
    plan_out[0:TILES] = ordered
    group = lax.broadcasted_iota(jnp.int32, (1, 128), 1) // TILE
    lines = jnp.zeros((ROWS // 128, 128), jnp.int32)
    for part in range(4):
        piece = plan_out[pl.ds(part, ROWS // 128, stride=4), :]
        piece = pltpu.roll(piece, TILE * part, 1) if part else piece
        lines = jnp.where(group == part, piece, lines)
    scene_out[...] = lines


class Notes:
    def __init__(self, empty, result):
        self.empty, self.result = empty, result


def first_kernel(
    me_ref, rank_ref, x, scenes, gains, w_qkv, w_proj, w_up, w_down,
    send, send_other, up, down, local, empty, result, fill_sem, *scratch,
):
    s = Scratch(scratch)
    copies = start_weights(0, (w_proj, w_up, w_down), (s.w_proj, s.w_up, s.w_down), s)
    me = me_ref[0]
    write_notes(scenes, crossings(me, rank_ref), Notes(empty, result))
    fills = []
    for index, target in enumerate((send, send_other, up, down, local)):
        count = target.shape[0]
        fills.append(
            pltpu.make_async_copy(
                empty.at[0:count], target.at[:, :, NOTE:LANES], fill_sem.at[index]
            )
        )
        fills[-1].start()
    scene_columns(scenes, s)
    bound, largest = project(x, gains[0, 0:1], w_qkv.at[0], s)
    quick = (bound <= SCORE_LIMIT) & (largest <= VALUE_LIMIT)

    @pl.when(quick)
    def _():
        attend_bounded((ROWS,), lambda index: (0, 0), scenes, s)

    @pl.when(jnp.logical_not(quick))
    def _():
        attend_any(scenes, s)

    for copy in copies + fills:
        copy.wait()
    above, below = neighbours(me)
    slots = (jnp.int32(0), jnp.int32(0))
    for start in range(0, ROWS, MLP_BLOCK):
        rows = mlp_rows(slice(start, start + MLP_BLOCK), x, gains[0, 1:2], s)
        tiles = slice(start // TILE, (start + MLP_BLOCK) // TILE)
        rows = rows.reshape(MLP_BLOCK // TILE, GROUPS, GROUP_ROWS, C)
        for group in range(GROUPS):
            result[tiles, :, C * group : C * (group + 1)] = rows[:, group].astype(BF16)

        def one_tile(tile, slots):
            owner = rank_ref[tile * TILE] >> 10

            def put(target, index):
                pltpu.make_async_copy(result.at[tile], target.at[index], s.out_sem).start()

            is_up, is_down, stays = owner == above, owner == below, owner == me

            @pl.when(is_up)
            def _():
                put(up, jnp.minimum(slots[0], MOST_TILES - 1))

            @pl.when(is_down)
            def _():
                put(down, jnp.minimum(slots[1], MOST_TILES - 1))

            @pl.when(stays)
            def _():
                put(local, tile)

            far = jnp.logical_not(is_up | is_down | stays)
            crosses = (owner ^ me) & 1 == 1

            @pl.when(far & jnp.logical_not(crosses))
            def _():
                put(send, owner // 2)

            @pl.when(far & crosses)
            def _():
                put(send_other, owner // 2)

            return (slots[0] + is_up.astype(jnp.int32), slots[1] + is_down.astype(jnp.int32))

        slots = lax.fori_loop(start // TILE, (start + MLP_BLOCK) // TILE, one_tile, slots)
    pltpu.make_async_copy(result, local, s.out_sem).wait()


def second_kernel(
    me_ref, gains, *refs, sources,
):
    arrays, refs = refs[:sources], refs[sources:]
    w_qkv, w_proj, w_up, w_down, out, x, plan_vmem, scenes, result, plan, plan_sem = refs[:11]
    s = Scratch(refs[11:])
    me = me_ref[0]
    core = lax.rem(me, 2)
    above, below = neighbours(me)
    firsts = ((core, 2), (1 - core, 2))[: sources - 3] + ((below, 0), (above, 0), (me, 0))
    copies = start_weights(
        1, (w_qkv, w_proj, w_up, w_down), (s.w_qkv, s.w_proj, s.w_up, s.w_down), s
    )
    entries = [(array, *first) for array, first in zip(arrays, firsts, strict=True)]
    sort_tiles(entries, plan_vmem, scenes)
    to_scalars = pltpu.make_async_copy(plan_vmem.at[0:TILES], plan, plan_sem)
    to_scalars.start()
    scene_columns(scenes, s)
    to_scalars.wait()

    def fetch(index, carry):
        entry = plan[index, TILE + 2] + 128 * plan[index, TILE + 3]
        first = 0
        for array in arrays:
            end = first + array.shape[0]

            @pl.when((entry >= first) & (entry < end))
            def _(array=array, first=first):
                for group in range(GROUPS):
                    target = pl.ds(pl.multiple_of(index * TILE + group * GROUP_ROWS, GROUP_ROWS), GROUP_ROWS)
                    x[target, :] = array[entry - first, :, C * group : C * (group + 1)].astype(F32)

            first = end
        return carry

    lax.fori_loop(0, TILES, fetch, 0)
    copies[0].wait()
    bound, largest = project(x, gains[1, 0:1], s.w_qkv, s)
    quick = (bound <= SCORE_LIMIT) & (largest <= VALUE_LIMIT)

    def window(index, count):
        first = plan[index * (QUERY_BLOCK // TILE), 0]
        last = plan[(index + 1) * (QUERY_BLOCK // TILE) - 1, TILE - 1]
        start = jnp.int32(0)
        for piece in range(1, (ROWS - count) // 128 + 1):
            start = start + (plan[4 * piece - 1, TILE - 1] < first).astype(jnp.int32)
        end = start * 128 + count
        fits = (end >= ROWS) | (plan[jnp.minimum(end // TILE, TILES - 1), 0] > last)
        return pl.multiple_of(start * 128, 128), fits

    def choose(index):
        short, enough = window(index, WINDOWS[0])
        wide, _ = window(index, WINDOWS[1])
        return jnp.where(enough, 0, 1), pl.multiple_of(jnp.where(enough, short, wide), 128)

    fits = quick
    for index in range(ROWS // QUERY_BLOCK):
        fits = fits & window(index, WINDOWS[1])[1]

    @pl.when(fits)
    def _():
        attend_bounded(WINDOWS, choose, scenes, s)

    @pl.when(quick & jnp.logical_not(fits))
    def _():
        attend_bounded((ROWS,), lambda index: (0, 0), scenes, s)

    @pl.when(jnp.logical_not(quick))
    def _():
        attend_any(scenes, s)

    for copy in copies[1:]:
        copy.wait()
    for start in range(0, ROWS, MLP_BLOCK):
        rows = mlp_rows(slice(start, start + MLP_BLOCK), x, gains[1, 1:2], s)
        result[start : start + MLP_BLOCK] = rows.astype(BF16)

        def one_tile(index, carry):
            source = result.at[pl.ds(pl.multiple_of(index * TILE, TILE), TILE)]
            place = jnp.clip(plan[index, TILE] - 1, 0, TILES - 1)
            target = out.at[pl.ds(pl.multiple_of(place * TILE, TILE), TILE)]
            pltpu.make_async_copy(source, target, s.out_sem).start()
            return carry

        lax.fori_loop(start // TILE, (start + MLP_BLOCK) // TILE, one_tile, 0)
    pltpu.make_async_copy(result, out, s.out_sem).wait()


SMEM = pl.BlockSpec(memory_space=pltpu.SMEM)
VMEM = pl.BlockSpec(memory_space=pltpu.VMEM)
HBM = pl.BlockSpec(memory_space=pl.ANY)


def shards(point_feats, scene_id, hilbert_rank, norm_gains, w_qkv, w_proj, w_up, w_down):
    devices = lax.axis_size("seq")
    me = lax.axis_index("seq")
    me_array = me.reshape(1).astype(jnp.int32)
    weights = (w_qkv, w_proj, w_up, w_down)
    scenes = scene_id.reshape(ROWS // 128, 128)
    params = pltpu.CompilerParams(vmem_limit_bytes=VMEM_BYTES)
    rows = jax.ShapeDtypeStruct((ROWS, C), BF16)
    few = jax.ShapeDtypeStruct((MOST_TILES, GROUP_ROWS, LANES), BF16)
    bins = jax.ShapeDtypeStruct((CHIPS, GROUP_ROWS, LANES), BF16)
    own = jax.ShapeDtypeStruct((TILES, GROUP_ROWS, LANES), BF16)
    ring = range(devices)
    to_above = [(i, (i + 1) % devices) for i in ring]
    to_below = [(i, (i - 1) % devices) for i in ring]
    to_other = [(i, i ^ 1) for i in ring]
    cores = [list(range(core, devices, 2)) for core in range(2)]

    def among_chips(array):
        return lax.all_to_all(
            array, "seq", split_axis=0, concat_axis=0, tiled=True, axis_index_groups=cores
        )

    send, send_other, up, down, local = pl.pallas_call(
        first_kernel,
        in_specs=[SMEM, SMEM, VMEM, VMEM, VMEM, VMEM, HBM, HBM, HBM],
        out_specs=[HBM] * 5,
        out_shape=[bins, bins, few, few, own],
        scratch_shapes=[
            pltpu.VMEM((CHIPS, GROUP_ROWS, 128), BF16),
            pltpu.VMEM((TILES, GROUP_ROWS, LANES), BF16),
            pltpu.SemaphoreType.DMA((5,)),
        ]
        + scratch_shapes(),
        compiler_params=params,
        name="first_block",
    )(me_array, hilbert_rank, point_feats, scenes, norm_gains, *weights)

    received = among_chips(send)
    from_below = lax.ppermute(up, "seq", to_above)
    from_above = lax.ppermute(down, "seq", to_below)

    def second(*arrays):
        return pl.pallas_call(
            functools.partial(second_kernel, sources=len(arrays)),
            in_specs=[SMEM, VMEM] + [VMEM] * len(arrays) + [HBM] * 4,
            out_specs=HBM,
            out_shape=pltpu.HBM((ROWS, C), BF16),
            scratch_shapes=[
                pltpu.VMEM((ROWS, C), F32),
                pltpu.VMEM((TILES + 8, 128), jnp.int32),
                pltpu.VMEM((ROWS // 128, 128), jnp.int32),
                pltpu.VMEM((ROWS, C), BF16),
                pltpu.SMEM((TILES, 128), jnp.int32),
                pltpu.SemaphoreType.DMA,
            ]
            + scratch_shapes(),
            compiler_params=params,
            name="second_block",
        )(me_array, norm_gains, *arrays, *weights)

    crossing = jnp.max(received[:, 0, NOTE + TILE + 1].astype(jnp.int32)).reshape(1)
    crossing_other = lax.ppermute(crossing, "seq", to_other)
    out = second(received, from_below, from_above, local)

    def with_crossing(out, tiles, received, *rest):
        return second(received, among_chips(lax.ppermute(tiles, "seq", to_other)), *rest)

    def without_crossing(out, *rest):
        return out

    return lax.cond(
        jnp.maximum(crossing, crossing_other)[0] > 0, with_crossing, without_crossing,
        out, send_other, received, from_below, from_above, local,
    )


def solution(mesh):
    placed = (P("seq", None), P("seq"), P("seq"), P(), P(), P(), P(), P())
    return jax.shard_map(
        shards, mesh=mesh, in_specs=placed, out_specs=P("seq", None), check_vma=False
    )
```
